32 devices in a mesh: tok: 8 (over y, x, core), rep: 4 (over z).
Axes of the slice: x: 2, y: 2, z: 4, core: 2. Of those that a mesh axis runs over, the one named last changes fastest.
Arguments:
- tokens: bfloat16 [2, 4, 4096, 1024], P(None, 'rep', 'tok'), may hold values from -6 to 6
- cotangent: bfloat16 [2, 4, 4096, 1024], P(None, 'rep', 'tok'), may hold values from -6 to 6
- init_num: float32 [2, 4, 2, 1024], P(None, 'rep', None, 'tok'), may hold values from -34 to 34, as said below
- init_den: float32 [2, 4, 2, 1024], P(None, 'rep', None, 'tok'), may hold values from 0.5 to 20
- prev_att: bfloat16 [2, 4, 2, 1024], P(None, 'rep'), may hold values from -5 to 5
- seg_doc: int32 [2, 4, 2], P(None, 'rep'), may hold values from 0 to 1, as said below
- w_kvr: float32 [1024, 3072], P(('tok', 'rep')), may hold values from -0.1875 to 0.1875
- w_out: float32 [1024, 1024], P(('tok', 'rep')), may hold values from -0.75 to 0.75
- f_kr: float32 [1024, 5120], P(('tok', 'rep')), may hold values from -0.1875 to 0.1875
- f_value: float32 [4096, 1024], P(('tok', 'rep')), may hold values from -0.09375 to 0.09375
- vectors: float32 [11, 1024], replicated, may hold values from -16 to 2
- m_kvr: float32 [1024, 3072], P(('tok', 'rep')), may hold values from -36.20387 to 36.20387
- v_kvr: float32 [1024, 3072], P(('tok', 'rep')), may hold values from 211.02592 to 845.4144
- m_out: float32 [1024, 1024], P(('tok', 'rep')), may hold values from -16.29174 to 16.29174
- v_out: float32 [1024, 1024], P(('tok', 'rep')), may hold values from 38.66624 to 154.99265
- m_fkr: float32 [1024, 5120], P(('tok', 'rep')), may hold values from -36.20387 to 36.20387
- v_fkr: float32 [1024, 5120], P(('tok', 'rep')), may hold values from 187.76064 to 750.3872
- m_fvalue: float32 [4096, 1024], P(('tok', 'rep')), may hold values from -72.40774 to 72.40774
- v_fvalue: float32 [4096, 1024], P(('tok', 'rep')), may hold values from 773.3248 to 3093.2993
- vec_m: float32 [11, 1024], P(None, ('tok', 'rep')), may hold values from -54.3058 to 54.3058
- vec_v: float32 [11, 1024], P(None, ('tok', 'rep')), may hold values from 429.2608 to 1723.5968
Outputs:
- mixed: bfloat16 [2, 4, 4096, 1024], P(None, 'rep', 'tok')
- token_grad: bfloat16 [2, 4, 4096, 1024], P(None, 'rep', 'tok')
- new_kvr: float32 [1024, 3072], P(('tok', 'rep'))
- mom_kvr: float32 [1024, 3072], P(('tok', 'rep'))
- sq_kvr: float32 [1024, 3072], P(('tok', 'rep'))
- new_out: float32 [1024, 1024], P(('tok', 'rep'))
- mom_out: float32 [1024, 1024], P(('tok', 'rep'))
- sq_out: float32 [1024, 1024], P(('tok', 'rep'))
- new_fkr: float32 [1024, 5120], P(('tok', 'rep'))
- mom_fkr: float32 [1024, 5120], P(('tok', 'rep'))
- sq_fkr: float32 [1024, 5120], P(('tok', 'rep'))
- new_fvalue: float32 [4096, 1024], P(('tok', 'rep'))
- mom_fvalue: float32 [4096, 1024], P(('tok', 'rep'))
- sq_fvalue: float32 [4096, 1024], P(('tok', 'rep'))
- new_vectors: float32 [11, 1024], P(None, ('tok', 'rep'))
- mom_vectors: float32 [11, 1024], P(None, ('tok', 'rep'))
- sq_vectors: float32 [11, 1024], P(None, ('tok', 'rep'))
The draws below stay inside these ranges and needn't reach their ends.
Inputs may be any that keep to these rules, and one draw needn't show every extreme that they name: `seg_doc`: in each group, along the segments, document numbers start at 0, never fall and rise by one where a new document begins; a segment continues the document of the segment before it where its number is equal. init_num divided by init_den lies within -1.7 to 1.7.
All inputs are finite; a program needn't handle non-finite values.
Results may differ from the reference program's by a relative error of at most 0.023.
Values may be sent and summed in bfloat16 or wider, within the bound.
No kernel may reach another device: no remote copies, remote signals or barrier semaphores. Data moves between devices by JAX's collectives and lax.ppermute only.
A program may use at most 320 MiB of HBM per device.

```python
import math
import jax
import jax.numpy as jnp
from jax import lax

EMBED_SIZE = 1024
FF = 4096
MICRO = 2
SEG_LEN = 2048
WBLOCK = 128
STEP = 10
NVEC = 11
GROUPS = 4
GROUP_TOK = 4096
SEGS_REP = 2
ALLTOK = 32768
D3 = 3072
FFD = 5120


def state_pair(key, den_lower, den_upper, ratio_size):
    key_den, key_ratio = jax.random.split(key)
    shape = (MICRO, GROUPS, SEGS_REP, EMBED_SIZE)
    denom = jnp.exp(jax.random.uniform(key_den, shape, jnp.float32, math.log(den_lower), math.log(den_upper)))
    ratio = jax.random.uniform(key_ratio, shape, jnp.float32, -ratio_size, ratio_size)
    return (denom * ratio, denom)


def draw_init_num(key, part):
    paired = state_pair(key, 0.5, 20.0, 1.0)
    return paired[0]


def draw_init_den(key, part):
    paired = state_pair(key, 0.5, 20.0, 1.0)
    return paired[1]


def draw_seg_doc(key, part):
    key = jax.random.fold_in(key, 3)
    key_breaks, key_pick = jax.random.split(key)
    breaks = jax.random.randint(key_breaks, (MICRO, GROUPS, SEGS_REP), 0, 2)
    chosen = jax.random.randint(key_pick, (1, GROUPS, 1), 0, MICRO)
    micro_rows = jnp.arange(MICRO).reshape(MICRO, 1, 1)
    breaks = jnp.where(micro_rows == (chosen + 1) % MICRO, 1, breaks)
    breaks = jnp.where(micro_rows == chosen, 0, breaks)
    first_column = jnp.arange(SEGS_REP).reshape(1, 1, SEGS_REP) == 0
    breaks = jnp.where(first_column, 0, breaks)
    return jnp.cumsum(breaks, axis=-1).astype(jnp.int32)


def draw_vectors(key, part):
    key = jax.random.fold_in(key, 7)
    entire_lookup_matrix = jax.random.split(key, 5)
    slow_end = 1.0 / 30.0
    gain_size = 0.1
    layernorm_scales = 1.0 + jax.random.uniform(entire_lookup_matrix[0], (2, EMBED_SIZE), jnp.float32, -gain_size, gain_size)
    displacement_amounts = jax.random.uniform(entire_lookup_matrix[1], (2, EMBED_SIZE), jnp.float32, -0.5, 0.5)
    blend_fractions = jax.random.uniform(entire_lookup_matrix[2], (5, EMBED_SIZE), jnp.float32, 0.05, 0.95)
    fading_speeds = jax.random.uniform(entire_lookup_matrix[3], (1, EMBED_SIZE), jnp.float32, math.log(0.01 / GROUP_TOK), math.log(slow_end))
    ongoing_reward = jax.random.uniform(entire_lookup_matrix[4], (1, EMBED_SIZE), jnp.float32, -1.0, 2.0)
    return jnp.concatenate([layernorm_scales[0:1], displacement_amounts[0:1], layernorm_scales[1:2], displacement_amounts[1:2], blend_fractions, fading_speeds, ongoing_reward], axis=0)


def level_of(own_key, dims, cuts, least, top_value):
    factor_of = 1.0
    for axis_at, parts in cuts:
        heights = jax.random.uniform(jax.random.fold_in(jax.random.fold_in(own_key, 6), axis_at), (parts,), jnp.float32, least / len(cuts), top_value / len(cuts))
        factor_of = factor_of * jnp.repeat(jnp.exp(heights), dims[axis_at] // parts).reshape((-1,) + (1,) * (len(dims) - 1 - axis_at))
    return factor_of


def gaussian(rng, extent, width, most, shards=(), kind=jnp.bfloat16):
    factor_of = level_of(rng, extent, shards, -0.22, 0.18) if shards else 1.0
    entries = jax.random.normal(rng, extent, jnp.float32) * width * factor_of
    return jnp.minimum(jnp.maximum(entries, -most), most).astype(kind)


def setup_inputs(seed: int = 0) -> dict:
    key_list = jax.random.split(jax.random.key(seed), 22)
    tokens = gaussian(key_list[0], (MICRO, GROUPS, GROUP_TOK, EMBED_SIZE), 1.0, 6.0, ((1, 4), (2, 8)))
    cotangent = gaussian(key_list[1], (MICRO, GROUPS, GROUP_TOK, EMBED_SIZE), 1.0, 6.0, ((1, 4), (2, 8)))
    init_num = draw_init_num(jax.random.fold_in(key_list[21], 71), 0)
    init_den = draw_init_den(jax.random.fold_in(key_list[21], 71), 0)
    prev_att = gaussian(key_list[4], (MICRO, GROUPS, SEGS_REP, EMBED_SIZE), 1.0, 5.0, ((1, 4),))
    seg_doc = draw_seg_doc(jax.random.fold_in(key_list[21], 71), 0)
    w_kvr = gaussian(key_list[6], (EMBED_SIZE, D3), EMBED_SIZE ** -0.5, 0.1875, ((0, 32),), jnp.float32)
    w_out = gaussian(key_list[7], (EMBED_SIZE, EMBED_SIZE), (EMBED_SIZE // 16) ** -0.5, 0.75, ((0, 32),), jnp.float32)
    f_kr = gaussian(key_list[8], (EMBED_SIZE, FFD), EMBED_SIZE ** -0.5, 0.1875, ((0, 32),), jnp.float32)
    f_value = gaussian(key_list[9], (FF, EMBED_SIZE), FF ** -0.5, 0.09375, ((0, 32),), jnp.float32)
    vectors = draw_vectors(jax.random.fold_in(key_list[21], 71), 0)
    m_kvr = gaussian(key_list[11], (EMBED_SIZE, D3), (0.0389 * ALLTOK ** 0.5), 36.20387, ((0, 32),), jnp.float32)
    v_kvr = jnp.clip(jnp.exp(math.log(845.4144) - 1.387846 * jax.random.uniform(key_list[12], (EMBED_SIZE, D3), jnp.float32) ** level_of(key_list[12], (EMBED_SIZE, D3), ((0, 32),), -0.2, 0.2)), 211.02592, 845.4144)
    m_out = gaussian(key_list[13], (EMBED_SIZE, EMBED_SIZE), (0.0167 * ALLTOK ** 0.5), 16.29174, ((0, 32),), jnp.float32)
    v_out = jnp.clip(jnp.exp(math.log(154.99265) - 1.3884108 * jax.random.uniform(key_list[14], (EMBED_SIZE, EMBED_SIZE), jnp.float32) ** level_of(key_list[14], (EMBED_SIZE, EMBED_SIZE), ((0, 32),), -0.2, 0.2)), 38.66624, 154.99265)
    m_fkr = gaussian(key_list[15], (EMBED_SIZE, FFD), (0.0366 * ALLTOK ** 0.5), 36.20387, ((0, 32),), jnp.float32)
    v_fkr = jnp.clip(jnp.exp(math.log(750.3872) - 1.3854214 * jax.random.uniform(key_list[16], (EMBED_SIZE, FFD), jnp.float32) ** level_of(key_list[16], (EMBED_SIZE, FFD), ((0, 32),), -0.2, 0.2)), 187.76064, 750.3872)
    m_fvalue = gaussian(key_list[17], (FF, EMBED_SIZE), (0.0744 * ALLTOK ** 0.5), 72.40774, ((0, 32),), jnp.float32)
    v_fvalue = jnp.clip(jnp.exp(math.log(3093.2993) - 1.3862944 * jax.random.uniform(key_list[18], (FF, EMBED_SIZE), jnp.float32) ** level_of(key_list[18], (FF, EMBED_SIZE), ((0, 32),), -0.2, 0.2)), 773.3248, 3093.2993)
    vec_m = gaussian(key_list[19], (NVEC, EMBED_SIZE), (0.0555 * ALLTOK ** 0.5), 54.3058, ((1, 32),), jnp.float32)
    vec_v = jnp.clip(jnp.exp(math.log(1723.5968) - 1.3901039 * jax.random.uniform(key_list[20], (NVEC, EMBED_SIZE), jnp.float32) ** level_of(key_list[20], (NVEC, EMBED_SIZE), ((1, 32),), -0.2, 0.2)), 429.2608, 1723.5968)
    return dict(tokens=tokens, cotangent=cotangent, init_num=init_num, init_den=init_den, prev_att=prev_att, seg_doc=seg_doc, w_kvr=w_kvr, w_out=w_out, f_kr=f_kr, f_value=f_value, vectors=vectors, m_kvr=m_kvr, v_kvr=v_kvr, m_out=m_out, v_out=v_out, m_fkr=m_fkr, v_fkr=v_fkr, m_fvalue=m_fvalue, v_fvalue=v_fvalue, vec_m=vec_m, vec_v=vec_v)


@jax.custom_vjp
def low(v):
    return lax.optimization_barrier(v.astype(jnp.bfloat16)).astype(jnp.float32)

@jax.custom_vjp
def low_back(v):
    return v

def low_keep(v):
    return (low(v), None)

def low_pass(kept, grad):
    return (grad,)

def back_keep(v):
    return (v, None)

def back_low(kept, grad):
    return (low(grad),)
low.defvjp(low_keep, low_pass)
low_back.defvjp(back_keep, back_low)

def product(left, right):
    return jnp.dot(left, right, precision=lax.Precision.HIGHEST, preferred_element_type=jnp.float32)

def layer_norm(payload_entries, gain, offset):
    center = payload_entries - lax.optimization_barrier(jnp.mean(payload_entries, axis=-1, keepdims=True))
    spread = lax.optimization_barrier(jnp.mean(center * center, axis=-1, keepdims=True))
    return center * lax.rsqrt(spread + 1e-05) * gain + offset

def shifted(normed, previous, document_start_marker):
    before = jnp.concatenate([jnp.zeros_like(normed[:1]), normed[:-1]], axis=0)
    position = jnp.arange(GROUP_TOK)
    starts = jnp.logical_and(position % SEG_LEN == 0, jnp.repeat(document_start_marker, SEG_LEN))
    return jnp.where(starts[:, None], jnp.repeat(previous, SEG_LEN, axis=0), before)

def weighted_average_loop(lookup_entries, payload_entries, fading_speeds, ongoing_reward, starting_dividend, starting_divisor, document_start_marker):
    retain = jnp.exp(-jnp.exp(fading_speeds))

    def token_step(state, inputs):
        numer, denom = state
        ongoing_lookup, value_now = inputs
        diagonal_term = jnp.exp(ongoing_reward + ongoing_lookup)
        result = (numer + diagonal_term * value_now) / (denom + diagonal_term)
        weight_now = jnp.exp(ongoing_lookup)
        return ((retain * numer + weight_now * value_now, retain * denom + weight_now), result)

    def block_scan(state, inputs):
        return lax.scan(token_step, state, inputs)
    block_step = jax.checkpoint(block_scan)

    def segment_step(state, inputs):
        seg_keys, seg_values, supplied_numerator, supplied_denominator, is_new = inputs
        numer = jnp.where(is_new, supplied_numerator, state[0])
        denom = jnp.where(is_new, supplied_denominator, state[1])
        block_shape = (SEG_LEN // WBLOCK, WBLOCK, EMBED_SIZE)
        state, outputs = lax.scan(block_step, (numer, denom), (seg_keys.reshape(block_shape), seg_values.reshape(block_shape)))
        return (state, outputs.reshape(SEG_LEN, EMBED_SIZE))
    zero_state = jnp.zeros((EMBED_SIZE,), jnp.float32)
    seg_shape = (SEGS_REP, SEG_LEN, EMBED_SIZE)
    final_state, outputs = lax.scan(segment_step, (zero_state, zero_state), (lookup_entries.reshape(seg_shape), payload_entries.reshape(seg_shape), starting_dividend, starting_divisor, document_start_marker))
    return outputs.reshape(GROUP_TOK, EMBED_SIZE)

def block_forward(tokens_in, w_kvr, w_out, f_kr, f_value, vectors, starting_dividend, starting_divisor, att_prev, document_start_marker):
    normed = layer_norm(tokens_in, vectors[0], vectors[1])
    before = shifted(normed, att_prev, document_start_marker)
    mix_key = low(normed * vectors[4] + before * (1.0 - vectors[4]))
    mix_value = low(normed * vectors[5] + before * (1.0 - vectors[5]))
    mix_recept = low(normed * vectors[6] + before * (1.0 - vectors[6]))
    weights_kvr = low(w_kvr)
    lookup_entries = low(low_back(product(mix_key, weights_kvr[:, :EMBED_SIZE])))
    payload_entries = low(low_back(product(mix_value, weights_kvr[:, EMBED_SIZE:2 * EMBED_SIZE])))
    recept = low_back(product(mix_recept, weights_kvr[:, 2 * EMBED_SIZE:]))
    mixed_wkv = low(low_back(weighted_average_loop(lookup_entries, payload_entries, vectors[9], vectors[10], starting_dividend, starting_divisor, document_start_marker)))
    gated = low(jax.nn.sigmoid(recept) * mixed_wkv)
    attended = low_back(product(gated, low(w_out)))
    middle = tokens_in + attended
    normed_two = layer_norm(middle, vectors[2], vectors[3])
    before_two = shifted(normed_two, jnp.zeros((SEGS_REP, EMBED_SIZE), jnp.float32), document_start_marker)
    mix_key_two = low(normed_two * vectors[7] + before_two * (1.0 - vectors[7]))
    mix_recept_two = low(normed_two * vectors[8] + before_two * (1.0 - vectors[8]))
    weights_fkr = low(f_kr)
    hidden = low_back(product(mix_key_two, weights_fkr[:, :FF]))
    gate_pre = low_back(product(mix_recept_two, weights_fkr[:, FF:]))
    squared = low(jnp.square(jnp.maximum(hidden, 0.0)))
    channel = low_back(product(squared, low(f_value)))
    return middle + jax.nn.sigmoid(gate_pre) * channel

def adam_step(master, moment, second, gradient, rate, shrink):
    moment_new = 0.9 * moment + 0.1 * gradient
    second_new = 0.95 * second + 0.05 * gradient * gradient
    scaled = moment_new / (1.0 - 0.9 ** STEP) / (jnp.sqrt(second_new / (1.0 - 0.95 ** STEP)) + 1e-08)
    return (master - rate * (scaled + shrink * master), moment_new, second_new)

def reference(tokens, cotangent, init_num, init_den, prev_att, seg_doc, w_kvr, w_out, f_kr, f_value, vectors, m_kvr, v_kvr, m_out, v_out, m_fkr, v_fkr, m_fvalue, v_fvalue, vec_m, vec_v):
    unit_count = MICRO * GROUPS

    def flatten(array):
        return array.reshape((unit_count,) + array.shape[2:])
    params = (w_kvr, w_out, f_kr, f_value, vectors)

    def unit_step(totals, inputs):
        tokens_in, cot_in, starting_dividend, starting_divisor, att_prev, documents = inputs
        document_start_marker = jnp.concatenate([jnp.ones((1,), jnp.bool_), documents[1:] != documents[:-1]])

        def forward(tokens_float, weight_kvr, weight_out, weight_fkr, weight_fvalue, vector_rows):
            return block_forward(tokens_float, weight_kvr, weight_out, weight_fkr, weight_fvalue, vector_rows, starting_dividend, starting_divisor, att_prev.astype(jnp.float32), document_start_marker)
        result, pullback = jax.vjp(forward, tokens_in.astype(jnp.float32), params[0], params[1], params[2], params[3], params[4])
        gradients = pullback(cot_in.astype(jnp.float32))
        totals = tuple((total + grad_item for total, grad_item in zip(totals, gradients[1:])))
        return (totals, (result.astype(jnp.bfloat16), gradients[0].astype(jnp.bfloat16)))
    zero_grads = tuple((jnp.zeros_like(item) for item in params))
    totals, (results, input_grads) = lax.scan(unit_step, zero_grads, (flatten(tokens), flatten(cotangent), flatten(init_num), flatten(init_den), flatten(prev_att), flatten(seg_doc)))
    out_shape = (MICRO, GROUPS, GROUP_TOK, EMBED_SIZE)
    grad_kvr, grad_out, grad_fkr, grad_fvalue, grad_vec = totals
    base_rate = 2.5 / EMBED_SIZE ** 0.5
    new_kvr, mom_kvr, sq_kvr = adam_step(w_kvr, m_kvr, v_kvr, grad_kvr, base_rate, 0.01)
    new_out, mom_out, sq_out = adam_step(w_out, m_out, v_out, grad_out, 4.0 * base_rate, 0.01)
    new_fkr, mom_fkr, sq_fkr = adam_step(f_kr, m_fkr, v_fkr, grad_fkr, base_rate, 0.01)
    new_fvalue, mom_fvalue, sq_fvalue = adam_step(f_value, m_fvalue, v_fvalue, grad_fvalue, 2.5 / FF ** 0.5, 0.01)
    vec_rates = jnp.array([0.6, 0.3, 0.6, 0.3, 0.3, 0.3, 0.3, 0.3, 0.3, 3.0, 0.5], jnp.float32)[:, None]
    new_vectors, mom_vectors, sq_vectors = adam_step(vectors, vec_m, vec_v, grad_vec, vec_rates, 0.0)
    return (results.reshape(out_shape), input_grads.reshape(out_shape), new_kvr, mom_kvr, sq_kvr, new_out, mom_out, sq_out, new_fkr, mom_fkr, sq_fkr, new_fvalue, mom_fvalue, sq_fvalue, new_vectors, mom_vectors, sq_vectors)
```

```python
import functools
import math

import jax
import jax.numpy as jnp
from jax import lax
from jax.experimental import pallas as pl
from jax.experimental.pallas import tpu as pltpu
from jax.sharding import PartitionSpec as P

EMBED = 1024
FF = 4096
SEG_LEN = 2048
STEP = 10
CHUNKS = 8
GROUP = 16
STEPS = 16
ROWS = STEPS * GROUP
COLS = 512
EPS = 1e-05
F32 = jnp.float32
BF16 = jnp.bfloat16
VMEM_LIMIT = 60 * 1024 * 1024


def dot_nn(a, b):
    return jnp.dot(a, b, preferred_element_type=F32)


def dot_nt(a, b):
    return lax.dot_general(a, b, (((1,), (1,)), ((), ())), preferred_element_type=F32)


def dot_tn(a, b):
    return lax.dot_general(a, b, (((0,), (0,)), ((), ())), preferred_element_type=F32)


def sigmoid(v):
    return 1.0 / (1.0 + jnp.exp(-v))


def normalize(v):
    center = v - jnp.mean(v, axis=-1, keepdims=True)
    rstd = lax.rsqrt(jnp.mean(center * center, axis=-1, keepdims=True) + EPS)
    return center * rstd, rstd


def norm_back(e, n, rstd):
    return (e - jnp.mean(e, axis=-1, keepdims=True) - n * jnp.mean(e * n, axis=-1, keepdims=True)) * rstd


def swap_matrix():
    row = lax.broadcasted_iota(jnp.int32, (ROWS, ROWS), 0)
    col = lax.broadcasted_iota(jnp.int32, (ROWS, ROWS), 1)
    return jnp.where(col == (row % GROUP) * STEPS + row // GROUP, 1.0, 0.0).astype(BF16)


def swap_in(block):
    return dot_nn(swap_matrix(), block.reshape(ROWS, EMBED))


def swap_out(rows):
    moved = dot_nn(swap_matrix(), rows).astype(BF16)
    return moved.reshape(GROUP // CHUNKS, CHUNKS, STEPS, EMBED)


def col_chunks():
    return [slice(c * COLS, (c + 1) * COLS) for c in range(EMBED // COLS)]


def step_rows(j):
    return slice(j * GROUP, (j + 1) * GROUP)


def full(shape):
    return pl.BlockSpec(shape, lambda i: (0,) * len(shape), pipeline_mode=pl.Buffered(buffer_count=1))


def call(kernel, grid, in_specs, out_specs, out_shape, scratch, flops, name):
    return pl.pallas_call(
        kernel,
        grid=(grid,),
        in_specs=in_specs,
        out_specs=out_specs,
        out_shape=out_shape,
        scratch_shapes=scratch,
        compiler_params=pltpu.CompilerParams(
            dimension_semantics=("arbitrary",), vmem_limit_bytes=VMEM_LIMIT
        ),
        cost_estimate=pl.CostEstimate(flops=flops, bytes_accessed=flops // 400, transcendentals=0),
        name=name,
    )


def mix_one_kernel(
    tok_ref, edge_ref, vec_ref, w_ref,
    xp_ref, xk_ref, xv_ref, xr_ref, k_ref, v_ref, r_ref, end_ref, total_ref,
    carry, state_a, state_b,
):
    i = pl.program_id(0)

    @pl.when(i == 0)
    def _():
        carry[...] = edge_ref[...]
        state_a[...] = jnp.zeros_like(state_a)
        state_b[...] = jnp.zeros_like(state_b)

    x = swap_in(tok_ref[...])
    xp_ref[...] = x.astype(BF16)
    n, _ = normalize(x)
    h = n * vec_ref[0:1, :] + vec_ref[1:2, :]
    hp = jnp.concatenate([carry[...], h[:-GROUP]], axis=0)
    carry[...] = h[-GROUP:]
    diff = h - hp
    xk_ref[...] = (hp + diff * vec_ref[4:5, :]).astype(BF16)
    xv_ref[...] = (hp + diff * vec_ref[5:6, :]).astype(BF16)
    xr_ref[...] = (hp + diff * vec_ref[6:7, :]).astype(BF16)
    k_ref[...] = dot_nn(xk_ref[...], w_ref[:, :EMBED]).astype(BF16)
    v_ref[...] = dot_nn(xv_ref[...], w_ref[:, EMBED : 2 * EMBED]).astype(BF16)
    r_ref[...] = dot_nn(xr_ref[...], w_ref[:, 2 * EMBED :])
    for cols in col_chunks():
        retain = jnp.exp(-jnp.exp(vec_ref[9:10, cols]))
        a = state_a[:, cols]
        b = state_b[:, cols]
        for j in range(STEPS):
            weight = jnp.exp(k_ref[step_rows(j), cols].astype(F32))
            a = retain * a + weight * v_ref[step_rows(j), cols].astype(F32)
            b = retain * b + weight
        state_a[:, cols] = a
        state_b[:, cols] = b

    @pl.when(i == pl.num_programs(0) - 1)
    def _():
        end_ref[:GROUP, :] = state_a[...]
        end_ref[GROUP:, :] = state_b[...]
        rate = -jnp.exp(vec_ref[9:10, :])
        decay = jnp.exp(rate * float(STEPS * pl.num_programs(0)))
        for q in range(2 * GROUP // CHUNKS):
            total = end_ref[q * CHUNKS : q * CHUNKS + 1, :]
            for s in range(1, CHUNKS):
                total = decay * total + end_ref[q * CHUNKS + s : q * CHUNKS + s + 1, :]
            total_ref[q : q + 1, :] = total


def wkv_kernel(
    k_ref, v_ref, r_ref, xp_ref, vec_ref, start_ref, end_ref, w_ref,
    wkv_ref, y_ref, x1_ref, xk_ref, xr_ref, st_ref, first_ref, last_ref,
    carry, state_a, state_b,
):
    i = pl.program_id(0)

    @pl.when(i == 0)
    def _():
        rate = -jnp.exp(vec_ref[9:10, :])
        decay = jnp.exp(rate * float(STEPS * pl.num_programs(0)))
        for q in range(2 * GROUP // CHUNKS):
            state = start_ref[q : q + 1, :]
            target = state_a if q < GROUP // CHUNKS else state_b
            base = (q % (GROUP // CHUNKS)) * CHUNKS
            for s in range(CHUNKS):
                target[base + s : base + s + 1, :] = state
                state = decay * state + end_ref[q * CHUNKS + s : q * CHUNKS + s + 1, :]
        carry[...] = jnp.zeros_like(carry)

    st_ref[0, :GROUP, :] = state_a[...]
    st_ref[0, GROUP:, :] = state_b[...]
    for cols in col_chunks():
        retain = jnp.exp(-jnp.exp(vec_ref[9:10, cols]))
        bonus = vec_ref[10:11, cols]
        a = state_a[:, cols]
        b = state_b[:, cols]
        for j in range(STEPS):
            rows = step_rows(j)
            key = k_ref[rows, cols].astype(F32)
            value = v_ref[rows, cols].astype(F32)
            own = jnp.exp(bonus + key)
            weight = jnp.exp(key)
            wkv = ((a + own * value) / (b + own)).astype(BF16)
            wkv_ref[rows, cols] = wkv
            y_ref[rows, cols] = (sigmoid(r_ref[rows, cols]) * wkv.astype(F32)).astype(BF16)
            a = retain * a + weight * value
            b = retain * b + weight
        state_a[:, cols] = a
        state_b[:, cols] = b
    x1 = xp_ref[...].astype(F32) + dot_nn(y_ref[...], w_ref[...])
    x1_ref[...] = x1
    n, _ = normalize(x1)
    h = n * vec_ref[2:3, :] + vec_ref[3:4, :]
    hp = jnp.concatenate([carry[...], h[:-GROUP]], axis=0)
    carry[...] = h[-GROUP:]
    diff = h - hp
    xk_ref[...] = (hp + diff * vec_ref[7:8, :]).astype(BF16)
    xr_ref[...] = (hp + diff * vec_ref[8:9, :]).astype(BF16)

    @pl.when(i == 0)
    def _():
        first_ref[...] = h[:GROUP]

    last_ref[...] = h[-GROUP:]


def hidden_kernel(xk_ref, xr_ref, w_ref, kq_ref, gate_ref):
    for c in range(FF // EMBED):
        cols = slice(c * EMBED, (c + 1) * EMBED)
        active = jnp.maximum(dot_nn(xk_ref[...], w_ref[:, cols]), 0.0)
        kq_ref[:, cols] = (active * active).astype(BF16)
    gate_ref[...] = sigmoid(dot_nn(xr_ref[...], w_ref[:, FF:]))


def value_kernel(
    kq_ref, gate_ref, x1_ref, cot_ref, w_ref, mixed_ref, dvf_ref, drf_ref, dkf_ref, cp_ref
):
    vf = dot_nn(kq_ref[...], w_ref[...])
    gate = gate_ref[...]
    cot = swap_in(cot_ref[...])
    cp_ref[...] = cot.astype(BF16)
    mixed_ref[...] = swap_out((x1_ref[...] + gate * vf).astype(BF16))
    dvf_ref[...] = (cot * gate).astype(BF16)
    drf_ref[...] = (cot * vf * gate * (1.0 - gate)).astype(BF16)
    for c in range(FF // EMBED):
        cols = slice(c * EMBED, (c + 1) * EMBED)
        back = dot_nt(dvf_ref[...], w_ref[cols, :])
        dkf_ref[:, cols] = (back * 2.0 * jnp.sqrt(kq_ref[:, cols].astype(F32))).astype(BF16)


def middle_back_kernel(
    dkf_ref, drf_ref, w_ref, x1_ref, before_ref, edge_ref, later_ref, cp_ref, vec_ref, wo_ref,
    k_ref, v_ref, r_ref, wkv_ref, st_ref,
    dx1_ref, datt_ref, dwkv_ref, dr_ref, vsum_ref, first_ref, total_ref,
    carry, den, state_p, state_q,
):
    i = pl.program_id(0)
    count = pl.num_programs(0)

    @pl.when(i == 0)
    def _():
        carry[...] = later_ref[...]
        vsum_ref[...] = jnp.zeros_like(vsum_ref)
        state_p[...] = jnp.zeros_like(state_p)
        state_q[...] = jnp.zeros_like(state_q)

    gain = vec_ref[2:3, :]
    offset = vec_ref[3:4, :]
    share_k = vec_ref[7:8, :]
    share_r = vec_ref[8:9, :]
    dxk = dot_nt(dkf_ref[...], w_ref[:, :FF])
    dxr = dot_nt(drf_ref[...], w_ref[:, FF:])
    n, rstd = normalize(x1_ref[...])
    h = n * gain + offset
    n_before, _ = normalize(before_ref[...])
    h_before = jnp.where(i == count - 1, edge_ref[...], n_before * gain + offset)
    diff = h - jnp.concatenate([h_before, h[:-GROUP]], axis=0)
    shift = dxk * (1.0 - share_k) + dxr * (1.0 - share_r)
    dh = dxk * share_k + dxr * share_r + jnp.concatenate([shift[GROUP:], carry[...]], axis=0)
    carry[...] = shift[:GROUP]
    vsum_ref[0:1, :] += jnp.sum(dh * n, axis=0, keepdims=True)
    vsum_ref[1:2, :] += jnp.sum(dh, axis=0, keepdims=True)
    vsum_ref[2:3, :] += jnp.sum(dxk * diff, axis=0, keepdims=True)
    vsum_ref[3:4, :] += jnp.sum(dxr * diff, axis=0, keepdims=True)
    dx1 = cp_ref[...].astype(F32) + norm_back(dh * gain, n, rstd)
    dx1_ref[...] = dx1
    datt_ref[...] = dx1.astype(BF16)
    dy = dot_nt(datt_ref[...], wo_ref[...])
    gate = sigmoid(r_ref[...])
    dwkv_ref[...] = (dy * gate).astype(BF16)
    dr_ref[...] = (dy * wkv_ref[...].astype(F32) * gate * (1.0 - gate)).astype(BF16)
    for cols in col_chunks():
        retain = jnp.exp(-jnp.exp(vec_ref[9:10, cols]))
        bonus = vec_ref[10:11, cols]
        a = st_ref[0, :GROUP, cols]
        b = st_ref[0, GROUP:, cols]
        for j in range(STEPS):
            rows = step_rows(j)
            key = k_ref[rows, cols].astype(F32)
            value = v_ref[rows, cols].astype(F32)
            own = jnp.exp(bonus + key)
            weight = jnp.exp(key)
            scale = 1.0 / (b + own)
            den[0, rows, cols] = scale
            den[1, rows, cols] = (a + own * value) * scale
            a = retain * a + weight * value
            b = retain * b + weight
        p = state_p[:, cols]
        q = state_q[:, cols]
        for j in reversed(range(STEPS)):
            rows = step_rows(j)
            grad = dwkv_ref[rows, cols].astype(F32) * den[0, rows, cols]
            p = grad + retain * p
            q = retain * q - grad * den[1, rows, cols]
        state_p[:, cols] = p
        state_q[:, cols] = q

    @pl.when(i == count - 1)
    def _():
        first_ref[:GROUP, :] = state_p[...]
        first_ref[GROUP:, :] = state_q[...]
        rate = -jnp.exp(vec_ref[9:10, :])
        decay = jnp.exp(rate * float(STEPS * count))
        for q in range(2 * GROUP // CHUNKS):
            base = q * CHUNKS
            total = first_ref[base + CHUNKS - 1 : base + CHUNKS, :]
            for s in reversed(range(CHUNKS - 1)):
                total = decay * total + first_ref[base + s : base + s + 1, :]
            total_ref[q : q + 1, :] = total


def wkv_back_kernel(
    k_ref, v_ref, dwkv_ref, dr_ref, st_ref, vec_ref, later_ref, first_ref, w_ref,
    dk_ref, dv_ref, vsum_ref, edge_ref,
    past_a, past_b, state_p, state_q,
):
    i = pl.program_id(0)
    count = pl.num_programs(0)

    @pl.when(i == 0)
    def _():
        vsum_ref[...] = jnp.zeros_like(vsum_ref)
        rate = -jnp.exp(vec_ref[9:10, :])
        decay = jnp.exp(rate * float(STEPS * count))
        for q in range(2 * GROUP // CHUNKS):
            state = later_ref[q : q + 1, :]
            target = state_p if q < GROUP // CHUNKS else state_q
            base = (q % (GROUP // CHUNKS)) * CHUNKS
            for s in reversed(range(CHUNKS)):
                target[base + s : base + s + 1, :] = state
                state = decay * state + first_ref[q * CHUNKS + s : q * CHUNKS + s + 1, :]

    for cols in col_chunks():
        retain = jnp.exp(-jnp.exp(vec_ref[9:10, cols]))
        bonus = vec_ref[10:11, cols]
        a = st_ref[0, :GROUP, cols]
        b = st_ref[0, GROUP:, cols]
        for j in range(STEPS):
            rows = step_rows(j)
            weight = jnp.exp(k_ref[rows, cols].astype(F32))
            past_a[rows, cols] = a
            past_b[rows, cols] = b
            a = retain * a + weight * v_ref[rows, cols].astype(F32)
            b = retain * b + weight
        p = state_p[:, cols]
        q = state_q[:, cols]
        sum_decay = jnp.zeros((GROUP, COLS), F32)
        sum_bonus = jnp.zeros((GROUP, COLS), F32)
        for j in reversed(range(STEPS)):
            rows = step_rows(j)
            key = k_ref[rows, cols].astype(F32)
            value = v_ref[rows, cols].astype(F32)
            own = jnp.exp(bonus + key)
            weight = jnp.exp(key)
            a = past_a[rows, cols]
            b = past_b[rows, cols]
            scale = 1.0 / (b + own)
            wkv = (a + own * value) * scale
            grad = dwkv_ref[rows, cols].astype(F32) * scale
            own_grad = grad * own
            bonus_term = own_grad * (value - wkv)
            dv_ref[rows, cols] = (own_grad + weight * p).astype(BF16)
            dk_ref[rows, cols] = (bonus_term + weight * (value * p + q)).astype(BF16)
            sum_decay += a * p + b * q
            sum_bonus += bonus_term
            p = grad + retain * p
            q = retain * q - grad * wkv
        state_p[:, cols] = p
        state_q[:, cols] = q
        scaled = jnp.sum(sum_decay, axis=0, keepdims=True) * retain * -jnp.exp(vec_ref[9:10, cols])
        vsum_ref[0:1, cols] += scaled
        vsum_ref[1:2, cols] += jnp.sum(sum_bonus, axis=0, keepdims=True)

    @pl.when(i == count - 1)
    def _():
        rows = slice(0, GROUP)
        edge = dot_nt(dk_ref[rows, :], w_ref[:, :EMBED]) * (1.0 - vec_ref[4:5, :])
        edge += dot_nt(dv_ref[rows, :], w_ref[:, EMBED : 2 * EMBED]) * (1.0 - vec_ref[5:6, :])
        edge += dot_nt(dr_ref[rows, :], w_ref[:, 2 * EMBED :]) * (1.0 - vec_ref[6:7, :])
        edge_ref[...] = edge


def input_back_kernel(
    dk_ref, dv_ref, dr_ref, w_ref, xp_ref, before_ref, edge_ref, later_ref, dx1_ref, vec_ref,
    out_ref, vsum_ref, carry,
):
    i = pl.program_id(0)
    count = pl.num_programs(0)

    @pl.when(i == 0)
    def _():
        carry[...] = later_ref[...]
        vsum_ref[...] = jnp.zeros_like(vsum_ref)

    gain = vec_ref[0:1, :]
    offset = vec_ref[1:2, :]
    n, rstd = normalize(xp_ref[...].astype(F32))
    h = n * gain + offset
    n_before, _ = normalize(before_ref[...].astype(F32))
    h_before = jnp.where(i == count - 1, edge_ref[...], n_before * gain + offset)
    diff = h - jnp.concatenate([h_before, h[:-GROUP]], axis=0)
    dh = jnp.zeros((ROWS, EMBED), F32)
    shift = jnp.zeros((ROWS, EMBED), F32)
    for at, grad_ref in enumerate((dk_ref, dv_ref, dr_ref)):
        back = dot_nt(grad_ref[...], w_ref[:, at * EMBED : (at + 1) * EMBED])
        share = vec_ref[4 + at : 5 + at, :]
        vsum_ref[2 + at : 3 + at, :] += jnp.sum(back * diff, axis=0, keepdims=True)
        kept = back * share
        dh += kept
        shift += back - kept
    dh += jnp.concatenate([shift[GROUP:], carry[...]], axis=0)
    carry[...] = shift[:GROUP]
    vsum_ref[0:1, :] += jnp.sum(dh * n, axis=0, keepdims=True)
    vsum_ref[1:2, :] += jnp.sum(dh, axis=0, keepdims=True)
    out_ref[...] = swap_out((dx1_ref[...] + norm_back(dh * gain, n, rstd)).astype(BF16))


def adam_step(master, moment, second, gradient, rate, shrink):
    moment_new = 0.9 * moment + 0.1 * gradient
    second_new = 0.95 * second + 0.05 * gradient * gradient
    scaled = moment_new / (1.0 - 0.9**STEP) / (jnp.sqrt(second_new / (1.0 - 0.95**STEP)) + 1e-08)
    return (master - rate * (scaled + shrink * master), moment_new, second_new)


def neighbour(block, axis, distance):
    devices = range(lax.axis_size(axis))
    return lax.ppermute(block, axis, [(i, i + distance) for i in devices if i + distance in devices])


def everyone(block, axis):
    count = lax.axis_size(axis)
    return lax.all_to_all(
        jnp.broadcast_to(block[None], (count,) + block.shape), axis, 0, 0, tiled=True
    )


def gather_rows(weight):
    part = lax.all_gather(weight.astype(BF16), "rep", axis=0, tiled=True)
    return lax.all_gather(part, "tok", axis=0, tiled=True)


def scatter_rows(grad):
    part = lax.psum_scatter(grad.astype(BF16), "tok", scatter_dimension=0, tiled=True)
    return lax.psum_scatter(part, "rep", scatter_dimension=0, tiled=True).astype(F32)


def weight_grad(a, b):
    return lax.dot_general(a, b, (((0,), (0,)), ((), ())), preferred_element_type=F32).astype(BF16)


def on_device(
    tokens, cotangent, init_num, init_den, prev_att, seg_doc, w_kvr, w_out, f_kr, f_value, vectors,
    m_kvr, v_kvr, m_out, v_out, m_fkr, v_fkr, m_fvalue, v_fvalue, vec_m, vec_v,
):
    tok_count = lax.axis_size("tok")
    rep_count = lax.axis_size("rep")
    here = lax.axis_index("tok")
    flat_index = here * rep_count + lax.axis_index("rep")
    micro, _, local_len, _ = tokens.shape
    seg_count = seg_doc.shape[2]
    chunk = local_len // CHUNKS
    blocks = chunk // STEPS
    rows = micro * local_len

    kvr = gather_rows(w_kvr)
    out = gather_rows(w_out)
    fkr = gather_rows(f_kr)
    fvalue = gather_rows(f_value)

    documents = seg_doc[:, 0, :]
    marker = jnp.concatenate(
        [jnp.ones((micro, 1), jnp.bool_), documents[:, 1:] != documents[:, :-1]], axis=1
    )
    starts = jnp.arange(tok_count) * local_len
    fresh = jnp.logical_and(marker[:, starts // SEG_LEN], (starts % SEG_LEN == 0)[None, :])
    fresh_here = lax.dynamic_index_in_dim(fresh, here, 1, keepdims=True)
    seg_here = here * local_len // SEG_LEN
    prev_here = lax.dynamic_index_in_dim(prev_att[:, 0], seg_here, 1, keepdims=False).astype(F32)
    num_all = lax.all_gather(init_num[:, 0], "tok", axis=2, tiled=True)
    den_all = lax.all_gather(init_den[:, 0], "tok", axis=2, tiled=True)
    init_all = jnp.concatenate([num_all, den_all], axis=0)
    rate = -jnp.exp(vectors[9:10])
    fade = jnp.exp(rate * float(local_len))
    fresh_four = jnp.concatenate([fresh, fresh], axis=0)

    x4 = tokens.reshape(micro, CHUNKS, chunk, EMBED)
    c4 = cotangent.reshape(micro, CHUNKS, chunk, EMBED)

    def edge_back(last, incoming):
        moved = jnp.concatenate([incoming[:, None], last.reshape(micro, CHUNKS, EMBED)[:, :-1]], axis=1)
        return moved.reshape(GROUP, EMBED)

    def edge_forward(first, incoming):
        moved = jnp.concatenate([first.reshape(micro, CHUNKS, EMBED)[:, 1:], incoming[:, None]], axis=1)
        return moved.reshape(GROUP, EMBED)

    raw_in = neighbour(tokens[:, 0, -1, :], "tok", 1)
    raw_edge = edge_back(x4[:, :, -1, :], raw_in).astype(F32)
    edge_n, _ = normalize(raw_edge)
    edge_h = edge_n * vectors[0:1] + vectors[1:2]
    first_row = (jnp.arange(GROUP) % CHUNKS == 0)[:, None]
    fresh_rows = jnp.repeat(fresh_here[:, 0], CHUNKS)[:, None]
    replace = jnp.logical_and(first_row, fresh_rows)
    edge_one = jnp.where(replace, jnp.repeat(prev_here, CHUNKS, axis=0), edge_h)

    def up(width):
        return pl.BlockSpec((ROWS, width), lambda i: (i, 0))

    def down(width):
        return pl.BlockSpec((ROWS, width), lambda i: (blocks - 1 - i, 0))

    before_spec = pl.BlockSpec(
        (GROUP, EMBED), lambda i: (jnp.maximum((blocks - 1 - i) * STEPS - 1, 0), 0)
    )
    natural_up = pl.BlockSpec((micro, CHUNKS, STEPS, EMBED), lambda i: (0, 0, i, 0))
    natural_down = pl.BlockSpec((micro, CHUNKS, STEPS, EMBED), lambda i: (0, 0, blocks - 1 - i, 0))
    st_up = pl.BlockSpec((1, 2 * GROUP, EMBED), lambda i: (i, 0, 0))
    st_down = pl.BlockSpec((1, 2 * GROUP, EMBED), lambda i: (blocks - 1 - i, 0, 0))
    vec_spec = full(vectors.shape)
    edge_spec = full((GROUP, EMBED))
    state_spec = full((2 * GROUP, EMBED))
    total_spec = full((2 * micro, EMBED))
    sum_spec = full((8, EMBED))

    def like(width, dtype):
        return jax.ShapeDtypeStruct((rows, width), dtype)

    def small(count, dtype=F32):
        return jax.ShapeDtypeStruct((count, EMBED), dtype)

    state = pltpu.VMEM((GROUP, EMBED), F32)
    square = 2 * rows * EMBED * EMBED

    xp, xk, xv, xr, k, v, r, ends, totals = call(
        mix_one_kernel, blocks,
        [natural_up, edge_spec, vec_spec, full((EMBED, 3 * EMBED))],
        [up(EMBED)] * 7 + [state_spec, total_spec],
        [like(EMBED, BF16)] * 6 + [like(EMBED, F32), small(2 * GROUP), small(2 * micro)],
        [state] * 3, 4 * square, "mix_one",
    )(x4, edge_one, vectors, kvr)

    every = everyone(totals, "tok")
    carried = jnp.zeros((2 * micro, EMBED), F32)
    begin = jnp.zeros((2 * micro, EMBED), F32)
    for d in range(tok_count):
        seg = d * local_len // SEG_LEN
        carried = jnp.where(fresh_four[:, d : d + 1], init_all[:, seg], carried)
        begin = jnp.where(here == d, carried, begin)
        carried = fade * carried + every[d]

    wkv, y, x1, xk2, xr2, saved, first_two, last_two = call(
        wkv_kernel, blocks,
        [up(EMBED)] * 4 + [vec_spec, total_spec, state_spec, full((EMBED, EMBED))],
        [up(EMBED)] * 5 + [st_up, edge_spec, edge_spec],
        [like(EMBED, BF16), like(EMBED, BF16), like(EMBED, F32), like(EMBED, BF16), like(EMBED, BF16),
         jax.ShapeDtypeStruct((blocks, 2 * GROUP, EMBED), F32), small(GROUP), small(GROUP)],
        [state] * 3, 2 * square, "wkv",
    )(k, v, r, xp, vectors, begin, ends, out)

    row_in = neighbour(last_two.reshape(micro, CHUNKS, EMBED)[:, -1], "tok", 1)
    edge_two = jnp.where(replace, 0.0, edge_back(last_two, row_in))
    diff_two = first_two - edge_two
    xk2 = xk2.at[:GROUP].set((edge_two + diff_two * vectors[7:8]).astype(BF16))
    xr2 = xr2.at[:GROUP].set((edge_two + diff_two * vectors[8:9]).astype(BF16))

    kq, gate = call(
        hidden_kernel, blocks,
        [up(EMBED), up(EMBED), full((EMBED, FF + EMBED))],
        [up(FF), up(EMBED)],
        [like(FF, BF16), like(EMBED, F32)],
        [], 5 * square, "hidden",
    )(xk2, xr2, fkr)

    mixed, dvf, drf, dkf, cp = call(
        value_kernel, blocks,
        [up(FF), up(EMBED), up(EMBED), natural_up, full((FF, EMBED))],
        [natural_up, up(EMBED), up(EMBED), up(FF), up(EMBED)],
        [jax.ShapeDtypeStruct(x4.shape, BF16), like(EMBED, BF16), like(EMBED, BF16), like(FF, BF16),
         like(EMBED, BF16)],
        [], 9 * square, "value",
    )(kq, gate, x1, c4, fvalue)

    shift_two = dot_nt(dkf[:GROUP], fkr[:, :FF]) * (1.0 - vectors[7:8])
    shift_two += dot_nt(drf[:GROUP], fkr[:, FF:]) * (1.0 - vectors[8:9])

    def from_right(shift):
        incoming = neighbour(
            jnp.where(fresh_here, 0.0, shift.reshape(micro, CHUNKS, EMBED)[:, 0]), "tok", -1
        )
        return edge_forward(shift, incoming)

    later_two = from_right(shift_two)
    grad_fvalue = weight_grad(kq, dvf)
    grad_fkr = jnp.concatenate([weight_grad(xk2, dkf), weight_grad(xr2, drf)], axis=1)

    dx1, datt, dwkv, dr, vsum_two, firsts, back_totals = call(
        middle_back_kernel, blocks,
        [down(FF), down(EMBED), full((EMBED, FF + EMBED)), down(EMBED), before_spec, edge_spec,
         edge_spec, down(EMBED), vec_spec, full((EMBED, EMBED))] + [down(EMBED)] * 4 + [st_down],
        [down(EMBED)] * 4 + [sum_spec, state_spec, total_spec],
        [like(EMBED, F32), like(EMBED, BF16), like(EMBED, BF16), like(EMBED, BF16), small(8),
         small(2 * GROUP), small(2 * micro)],
        [state, pltpu.VMEM((2, ROWS, EMBED), F32), state, state], 6 * square, "middle_back",
    )(dkf, drf, fkr, x1, x1, edge_two, later_two, cp, vectors, out, k, v, r, wkv, saved)

    every_back = everyone(back_totals, "tok")
    grad_out = weight_grad(y, datt)
    grad_r = weight_grad(xr, dr)
    carried = jnp.zeros((2 * micro, EMBED), F32)
    later = jnp.zeros((2 * micro, EMBED), F32)
    for d in reversed(range(tok_count)):
        later = jnp.where(here == d, carried, later)
        carried = jnp.where(fresh_four[:, d : d + 1], 0.0, fade * carried + every_back[d])

    dk, dv, vsum_wkv, shift_one = call(
        wkv_back_kernel, blocks,
        [down(EMBED)] * 4 + [st_down, vec_spec, total_spec, state_spec, full((EMBED, 3 * EMBED))],
        [down(EMBED), down(EMBED), sum_spec, edge_spec],
        [like(EMBED, BF16), like(EMBED, BF16), small(8), small(GROUP)],
        [pltpu.VMEM((ROWS, EMBED), F32)] * 2 + [state] * 2, square, "wkv_back",
    )(k, v, dwkv, dr, saved, vectors, later, firsts, kvr)

    later_one = from_right(shift_one)
    grad_kvr = jnp.concatenate([weight_grad(xk, dk), weight_grad(xv, dv), grad_r], axis=1)

    token_grad, vsum_one = call(
        input_back_kernel, blocks,
        [down(EMBED)] * 3 + [full((EMBED, 3 * EMBED)), down(EMBED), before_spec, edge_spec, edge_spec,
         down(EMBED), vec_spec],
        [natural_down, sum_spec],
        [jax.ShapeDtypeStruct(x4.shape, BF16), small(8)],
        [state], 3 * square, "input_back",
    )(dk, dv, dr, kvr, xp, xp, edge_one, later_one, dx1, vectors)

    grad_vec = jnp.concatenate(
        [vsum_one[0:2], vsum_two[0:2], vsum_one[2:5], vsum_two[2:4], vsum_wkv[0:2]], axis=0
    )
    columns = vec_m.shape[1]
    pieces = jnp.moveaxis(grad_vec.reshape(vectors.shape[0], tok_count * rep_count, columns), 1, 0)
    sum_vec = jnp.sum(lax.all_to_all(pieces, ("tok", "rep"), 0, 0, tiled=True), axis=0)

    sum_kvr = scatter_rows(grad_kvr)
    sum_out = scatter_rows(grad_out)
    sum_fkr = scatter_rows(grad_fkr)
    sum_fvalue = scatter_rows(grad_fvalue)

    base_rate = 2.5 / math.sqrt(EMBED)
    new_kvr = adam_step(w_kvr, m_kvr, v_kvr, sum_kvr, base_rate, 0.01)
    new_out = adam_step(w_out, m_out, v_out, sum_out, 4.0 * base_rate, 0.01)
    new_fkr = adam_step(f_kr, m_fkr, v_fkr, sum_fkr, base_rate, 0.01)
    new_fvalue = adam_step(f_value, m_fvalue, v_fvalue, sum_fvalue, 2.5 / math.sqrt(FF), 0.01)
    vec_master = lax.dynamic_slice_in_dim(vectors, flat_index * columns, columns, 1)
    vec_rates = jnp.array([0.6, 0.3, 0.6, 0.3, 0.3, 0.3, 0.3, 0.3, 0.3, 3.0, 0.5], F32)[:, None]
    new_vectors = adam_step(vec_master, vec_m, vec_v, sum_vec, vec_rates, 0.0)
    shape = tokens.shape
    return (
        (mixed.reshape(shape), token_grad.reshape(shape))
        + new_kvr + new_out + new_fkr + new_fvalue + new_vectors
    )


def solution(mesh):
    rows = P(("tok", "rep"), None)
    columns = P(None, ("tok", "rep"))
    token_spec = P(None, "rep", "tok", None)
    channel_spec = P(None, "rep", None, "tok")
    placed = (
        (token_spec, token_spec, channel_spec, channel_spec, P(None, "rep", None, None), P(None, "rep", None))
        + (rows,) * 4 + (P(),) + (rows,) * 8 + (columns,) * 2
    )
    return jax.shard_map(
        on_device,
        mesh=mesh,
        in_specs=placed,
        out_specs=(token_spec, token_spec) + (rows,) * 12 + (columns,) * 3,
        check_vma=False,
    )
```

```python
import functools
import math

import jax
import jax.numpy as jnp
from jax import lax
from jax.experimental import pallas as pl
from jax.experimental.pallas import tpu as pltpu
from jax.sharding import PartitionSpec as P

EMBED = 1024
FF = 4096
SEG_LEN = 2048
STEP = 10
CHUNKS = 8
GROUP = 16
STEPS = 16
ROWS = STEPS * GROUP
COLS = 256
EPS = 1e-05
TINY = 1.2e-38
COSTS = dict(
    value=60, edge=14, grad_value=30, middle_back=60, grad_value_add_first=50, wkv_back=24, grad_value_merge=50,
    grad_hidden_add_first=50, grad_early_add_first=50, input_back_high=24,
)
F32 = jnp.float32
BF16 = jnp.bfloat16
MIB = 1024 * 1024
VMEM = dict(
    mix_one=30, wkv=28, hidden=36, value=60, edge=60, grad_value=60, middle_back=60, wkv_back=60, input_back_high=44,
    input_back_low=36,
)


def dot_nn(a, b):
    return jnp.dot(a, b, preferred_element_type=F32)


def dot_nt(a, b):
    return lax.dot_general(a, b, (((1,), (1,)), ((), ())), preferred_element_type=F32)


def dot_tn(a, b):
    return lax.dot_general(a, b, (((0,), (0,)), ((), ())), preferred_element_type=F32)


def sigmoid(v):
    return 0.5 * jnp.tanh(0.5 * v) + 0.5


def normalize(v):
    center = v - jnp.mean(v, axis=-1, keepdims=True)
    rstd = lax.rsqrt(jnp.mean(center * center, axis=-1, keepdims=True) + EPS)
    return center * rstd, rstd


def norm_back(e, n, rstd):
    return (e - jnp.mean(e, axis=-1, keepdims=True) - n * jnp.mean(e * n, axis=-1, keepdims=True)) * rstd


def swap_matrix():
    row = lax.broadcasted_iota(jnp.int32, (ROWS, ROWS), 0)
    col = lax.broadcasted_iota(jnp.int32, (ROWS, ROWS), 1)
    return jnp.where(col == (row % GROUP) * STEPS + row // GROUP, 1.0, 0.0).astype(BF16)


def swap_in(block):
    return dot_nn(swap_matrix(), block.reshape(ROWS, EMBED))


def swap_out(rows):
    moved = dot_nn(swap_matrix(), rows).astype(BF16)
    return moved.reshape(GROUP // CHUNKS, CHUNKS, STEPS, EMBED)


def part(at, count=1):
    return slice(at * EMBED, (at + count) * EMBED)


def col_chunks():
    return [slice(c * COLS, (c + 1) * COLS) for c in range(EMBED // COLS)]


def step_rows(j):
    return slice(j * GROUP, (j + 1) * GROUP)


def full(shape):
    return pl.BlockSpec(shape, lambda i: (0,) * len(shape), pipeline_mode=pl.Buffered(buffer_count=1))


def ordered(kernel, skip, count):
    return lambda *refs: kernel(*refs[:skip], *refs[skip + count :])


def cost(name):
    return pl.CostEstimate(flops=int(COSTS.get(name, 2) * 1e9), bytes_accessed=0, transcendentals=0)


def call(kernel, grid, in_specs, out_specs, out_shape, scratch, name, after=(), bits=None, weights=(), aliases=None):
    if weights:
        kernel = grouped(kernel, [len(pieces) for pieces in weights])
        in_specs = [SMEM_SPEC] + [ANY_SPEC] * sum(len(pieces) for pieces in weights) + in_specs
    made = pl.pallas_call(
        ordered(kernel, 0, len(after)),
        grid=(grid,),
        in_specs=[ANY_SPEC] * len(after) + in_specs,
        out_specs=out_specs,
        out_shape=out_shape,
        scratch_shapes=scratch,
        compiler_params=pltpu.CompilerParams(
            dimension_semantics=("arbitrary",), vmem_limit_bytes=VMEM.get(name, 16) * MIB
        ),
        cost_estimate=cost(name),
        input_output_aliases=aliases or {},
        name=name,
    )
    head = (bits,) + tuple(piece for pieces in weights for piece in pieces) if weights else ()
    return lambda *args: made(*after, *head, *args)


def grouped(kernel, counts):
    def run(bits_ref, *refs):
        groups = []
        for count in counts:
            groups.append(refs[:count])
            refs = refs[count:]
        return kernel(bits_ref, *groups, *refs)

    return run


SMEM_SPEC = pl.BlockSpec(memory_space=pltpu.SMEM)
ANY_SPEC = pl.BlockSpec(memory_space=pl.ANY)


def column_loads(pieces, target, sems, first, low, high, base=0, bits_ref=None):
    cols, place = slice(low, high), slice(low - base, high - base)
    if len(pieces) == 1:
        return [pltpu.make_async_copy(pieces[0].at[:, cols], target.at[:, place], sems.at[first])]
    copies = []
    height = target.shape[0] // 8
    for piece, core in zip(pieces, (bits_ref[0], 1 - bits_ref[0])):
        for q in range(4):
            rows = pl.ds(pl.multiple_of((2 * q + core) * height, height), height)
            copies.append(
                pltpu.make_async_copy(
                    piece.at[q * height : (q + 1) * height, cols], target.at[rows, place],
                    sems.at[first + len(copies)],
                )
            )
    return copies


def start_loads(*loads):
    @pl.when(pl.program_id(0) == 0)
    def _():
        for copies in loads:
            for copy in copies:
                copy.start()


def wait_all(copies):
    for copy in copies:
        copy.wait()


def wait_load(copies):
    pl.when(pl.program_id(0) == 0)(lambda: wait_all(copies))


def first_and_rest(body):
    pl.when(pl.program_id(0) == 0)(lambda: body(True))
    pl.when(pl.program_id(0) > 0)(lambda: body(False))


def mix_one_kernel(
    bits_ref, pieces, tok_ref, edge_ref, vec_ref,
    xp_ref, mix_ref, k_ref, v_ref, r_ref, end_ref, total_ref,
    carry, state_a, state_b, w_ref, sems,
):
    i = pl.program_id(0)
    loads = [
        column_loads(pieces, w_ref, sems, 16 * at, at * EMBED, (at + 1) * EMBED) for at in range(3)
    ]
    start_loads(*loads)

    @pl.when(i == 0)
    def _():
        carry[...] = edge_ref[...]
        state_a[...] = jnp.zeros_like(state_a)
        state_b[...] = jnp.zeros_like(state_b)

    xp_ref[...] = swap_in(tok_ref[...]).astype(BF16)
    hp = carry[...]
    for j in range(STEPS):
        rows = step_rows(j)
        n, _ = normalize(xp_ref[rows, :].astype(F32))
        h = n * vec_ref[0:1, :] + vec_ref[1:2, :]
        diff = h - hp
        for at in range(3):
            mix_ref[rows, part(at)] = (hp + diff * vec_ref[4 + at : 5 + at, :]).astype(BF16)
        hp = h
    carry[...] = hp

    def project(first):
        for at, out_ref in enumerate((k_ref, v_ref, r_ref)):
            if first:
                wait_all(loads[at])
            out_ref[...] = dot_nn(mix_ref[:, part(at)], w_ref[:, part(at)]).astype(out_ref.dtype)

    first_and_rest(project)
    for cols in col_chunks():
        retain = jnp.exp(-jnp.exp(vec_ref[9:10, cols]))
        a = state_a[:, cols]
        b = state_b[:, cols]
        for j in range(STEPS):
            weight = jnp.exp(k_ref[step_rows(j), cols].astype(F32))
            a = retain * a + weight * v_ref[step_rows(j), cols].astype(F32)
            b = retain * b + weight
        state_a[:, cols] = a
        state_b[:, cols] = b

    @pl.when(i == pl.num_programs(0) - 1)
    def _():
        end_ref[:GROUP, :] = state_a[...]
        end_ref[GROUP:, :] = state_b[...]
        rate = -jnp.exp(vec_ref[9:10, :])
        decay = jnp.exp(rate * float(STEPS * pl.num_programs(0)))
        for q in range(2 * GROUP // CHUNKS):
            total = end_ref[q * CHUNKS : q * CHUNKS + 1, :]
            for s in range(1, CHUNKS):
                total = decay * total + end_ref[q * CHUNKS + s : q * CHUNKS + s + 1, :]
            total_ref[q : q + 1, :] = total


def wkv_kernel(
    bits_ref, pieces, k_ref, v_ref, r_ref, xp_ref, vec_ref, start_ref, end_ref,
    wkv_ref, y_ref, x1_ref, mix_ref, st_ref, first_ref, last_ref,
    carry, state_a, state_b, w_ref, sems,
):
    i = pl.program_id(0)
    loads = column_loads(pieces, w_ref, sems, 0, 3 * EMBED, 4 * EMBED, 3 * EMBED)
    start_loads(loads)

    @pl.when(i == 0)
    def _():
        rate = -jnp.exp(vec_ref[9:10, :])
        decay = jnp.exp(rate * float(STEPS * pl.num_programs(0)))
        for q in range(2 * GROUP // CHUNKS):
            state = start_ref[q : q + 1, :]
            target = state_a if q < GROUP // CHUNKS else state_b
            base = (q % (GROUP // CHUNKS)) * CHUNKS
            for s in range(CHUNKS):
                target[base + s : base + s + 1, :] = state
                state = decay * state + end_ref[q * CHUNKS + s : q * CHUNKS + s + 1, :]
        carry[...] = jnp.zeros_like(carry)

    st_ref[0, :GROUP, :] = state_a[...]
    st_ref[0, GROUP:, :] = state_b[...]
    for cols in col_chunks():
        retain = jnp.exp(-jnp.exp(vec_ref[9:10, cols]))
        bonus = vec_ref[10:11, cols]
        a = state_a[:, cols]
        b = state_b[:, cols]
        for j in range(STEPS):
            rows = step_rows(j)
            key = k_ref[rows, cols].astype(F32)
            value = v_ref[rows, cols].astype(F32)
            own = jnp.exp(bonus + key)
            weight = jnp.exp(key)
            wkv = ((a + own * value) * pl.reciprocal(b + own)).astype(BF16)
            wkv_ref[rows, cols] = wkv
            y_ref[rows, cols] = (sigmoid(r_ref[rows, cols].astype(F32)) * wkv.astype(F32)).astype(BF16)
            a = retain * a + weight * value
            b = retain * b + weight
        state_a[:, cols] = a
        state_b[:, cols] = b
    wait_load(loads)
    x1_ref[...] = xp_ref[...].astype(F32) + dot_nn(y_ref[...], w_ref[...])
    hp = carry[...]
    for j in range(STEPS):
        rows = step_rows(j)
        n, _ = normalize(x1_ref[rows, :])
        h = n * vec_ref[2:3, :] + vec_ref[3:4, :]
        diff = h - hp
        for at in range(2):
            mix_ref[rows, part(at)] = (hp + diff * vec_ref[7 + at : 8 + at, :]).astype(BF16)
        if j == 0:

            @pl.when(i == 0)
            def _(h=h):
                first_ref[...] = h

        hp = h
    carry[...] = hp
    last_ref[...] = hp


def hidden_kernel(bits_ref, pieces, mix_ref, kq_ref, gate_ref, w_ref, sems):
    loads = [
        column_loads(pieces, w_ref, sems, 16 * at, at * EMBED, (at + 1) * EMBED) for at in range(5)
    ]
    start_loads(*loads)

    def project(first):
        for c in range(FF // EMBED):
            if first:
                wait_all(loads[c])
            active = jnp.maximum(dot_nn(mix_ref[:, part(0)], w_ref[:, part(c)]), 0.0)
            kq_ref[:, part(c)] = (active * active).astype(BF16)
        if first:
            wait_all(loads[4])
        gate_ref[...] = dot_nn(mix_ref[:, part(1)], w_ref[:, FF:]).astype(BF16)

    first_and_rest(project)


def rep_loads(bits_ref, pieces, target, sems, first, low):
    copies = []
    for at, piece in enumerate(pieces):
        high = bits_ref[4] if at % 2 == 0 else 1 - bits_ref[4]
        bit = bits_ref[3] if at < 2 else 1 - bits_ref[3]
        height = target.shape[0] // 32
        for block in range(8):
            rows = pl.ds(pl.multiple_of((4 * block + 2 * high + bit) * height, height), height)
            copies.append(
                pltpu.make_async_copy(
                    piece.at[block * height : (block + 1) * height, :], target.at[rows, low:],
                    sems.at[first + len(copies)],
                )
            )
    return copies


def value_kernel(
    bits_ref, pieces, others, kq_ref, gate_ref, x1_ref, cot_ref,
    mixed_ref, dvf_ref, grad_ref, cp_ref, w_ref, vf_ref, out_ref, sems,
):
    half = EMBED // 2
    if others:
        loads = [
            column_loads(pieces, w_ref, sems, 0, 0, half),
            rep_loads(bits_ref, others, w_ref, sems, 1, half),
        ]
    else:
        loads = [column_loads(pieces, w_ref, sems, at, at * half, (at + 1) * half) for at in range(2)]
    start_loads(*loads)
    cp_ref[...] = swap_in(cot_ref[...]).astype(BF16)

    def project(first):
        if not first:
            vf_ref[...] = dot_nn(kq_ref[...], w_ref[...])
            return
        for at in range(2):
            wait_all(loads[at])
            cols = slice(at * half, (at + 1) * half)
            vf_ref[:, cols] = dot_nn(kq_ref[...], w_ref[:, cols])

    first_and_rest(project)
    for j in range(STEPS):
        rows = step_rows(j)
        gate = sigmoid(gate_ref[rows, :].astype(F32))
        vf = vf_ref[rows, :]
        out_ref[rows, :] = (x1_ref[rows, :] + gate * vf).astype(BF16)
        scaled = cp_ref[rows, :].astype(F32) * gate
        dvf_ref[rows, :] = scaled.astype(BF16)
        grad_ref[rows, FF:] = (scaled * vf * (1.0 - gate)).astype(BF16)
    for c in range(FF // EMBED):
        back = dot_nt(dvf_ref[...], w_ref[part(c), :])
        square = kq_ref[:, part(c)].astype(F32)
        root = square * lax.rsqrt(jnp.maximum(square, TINY))
        grad_ref[:, part(c)] = (back * (2.0 * root)).astype(BF16)
    mixed_ref[...] = swap_out(out_ref[...])


def send_rows(flag_ref, shift, send_ref):
    for m in range(send_ref.shape[0]):
        row = shift[m * CHUNKS : m * CHUNKS + 1]
        send_ref[m : m + 1, :] = jnp.where(flag_ref[m] > 0, 0.0, row)


def take_rows(carry, shift_ref, got_ref):
    for m in range(got_ref.shape[0]):
        base = m * CHUNKS
        carry[base : base + CHUNKS - 1, :] = shift_ref[base + 1 : base + CHUNKS, :]
        carry[base + CHUNKS - 1 : base + CHUNKS, :] = got_ref[m : m + 1, :]


def edge_kernel(bits_ref, pieces, flag_ref, grad_ref, vec_ref, shift_ref, send_ref, w_ref, sems):
    loads = column_loads(pieces, w_ref, sems, 0, 0, FF + EMBED)
    start_loads(loads)
    wait_all(loads)
    shift = dot_nt(grad_ref[:, :FF], w_ref[:, :FF]) * (1.0 - vec_ref[7:8, :])
    shift += dot_nt(grad_ref[:, FF:], w_ref[:, FF:]) * (1.0 - vec_ref[8:9, :])
    shift_ref[...] = shift
    send_rows(flag_ref, shift, send_ref)


def add_sums(sums, values):
    for at, value in enumerate(values):
        sums[at] += value


def middle_back_kernel(weights, ins, outs, scratch, copies, grad):
    pieces, out_pieces = weights
    (
        grad_ref, x1_ref, before_ref, edge_ref, later_ref, got_ref, cp_ref, vec_ref, k_ref, v_ref, r_ref, wkv_ref,
        st_ref,
    ) = ins
    dx1_ref, out_ref, dwkv_ref, vsum_ref, first_ref, total_ref = outs
    carry, den, state_p, state_q, w_ref, wo_ref, dxk_ref, dxr_ref, sums, sems = scratch
    i = pl.program_id(0)
    count = pl.num_programs(0)
    loads = [
        column_loads((pieces,), w_ref, sems, 0, 0, FF + EMBED),
        column_loads((out_pieces,), wo_ref, sems, 16, 3 * EMBED, 4 * EMBED, 3 * EMBED),
    ]
    start_loads(*loads)

    @pl.when(i == 0)
    def _():
        take_rows(carry, later_ref, got_ref)
        sums[...] = jnp.zeros_like(sums)
        state_p[...] = jnp.zeros_like(state_p)
        state_q[...] = jnp.zeros_like(state_q)

    for cols in col_chunks():
        retain = jnp.exp(-jnp.exp(vec_ref[9:10, cols]))
        bonus = vec_ref[10:11, cols]
        a = st_ref[0, :GROUP, cols]
        b = st_ref[0, GROUP:, cols]
        for j in range(STEPS):
            rows = step_rows(j)
            key = k_ref[rows, cols].astype(F32)
            value = v_ref[rows, cols].astype(F32)
            own = jnp.exp(bonus + key)
            weight = jnp.exp(key)
            scale = pl.reciprocal(b + own)
            den[0, rows, cols] = scale
            den[1, rows, cols] = (a + own * value) * scale
            a = retain * a + weight * value
            b = retain * b + weight
    wait_load(loads[0] + loads[1] + copies)
    dxk_ref[...] = dot_nt(grad_ref[:, :FF], w_ref[:, :FF])
    dxr_ref[...] = dot_nt(grad_ref[:, FF:], w_ref[:, FF:])
    grad()
    gain = vec_ref[2:3, :]
    offset = vec_ref[3:4, :]
    share_k = vec_ref[7:8, :]
    share_r = vec_ref[8:9, :]
    n, rstd = normalize(x1_ref[step_rows(STEPS - 1), :])
    later = carry[...]
    for j in reversed(range(STEPS)):
        rows = step_rows(j)
        if j > 0:
            n_next, rstd_next = normalize(x1_ref[step_rows(j - 1), :])
            h_before = n_next * gain + offset
        else:
            n_before, _ = normalize(before_ref[...])
            h_before = jnp.where(i == count - 1, edge_ref[...], n_before * gain + offset)
        diff = n * gain + offset - h_before
        dxk = dxk_ref[rows, :]
        dxr = dxr_ref[rows, :]
        kept_k = dxk * share_k
        kept_r = dxr * share_r
        dh = kept_k + kept_r + later
        later = (dxk - kept_k) + (dxr - kept_r)
        add_sums(sums, (dh * n, dh, dxk * diff, dxr * diff))
        dx1 = cp_ref[rows, :].astype(F32) + norm_back(dh * gain, n, rstd)
        dx1_ref[rows, :] = dx1
        out_ref[rows, part(0)] = dx1.astype(BF16)
        if j > 0:
            n, rstd = n_next, rstd_next
    carry[...] = later
    dxk_ref[...] = dot_nt(out_ref[:, part(0)], wo_ref[...])
    for cols in col_chunks():
        retain = jnp.exp(-jnp.exp(vec_ref[9:10, cols]))
        right = slice(EMBED + cols.start, EMBED + cols.stop)
        p = state_p[:, cols]
        q = state_q[:, cols]
        for j in reversed(range(STEPS)):
            rows = step_rows(j)
            gate = sigmoid(r_ref[rows, cols].astype(F32))
            scaled = dxk_ref[rows, cols] * gate
            dwkv = scaled.astype(BF16)
            dwkv_ref[rows, cols] = dwkv
            out_ref[rows, right] = (scaled * wkv_ref[rows, cols].astype(F32) * (1.0 - gate)).astype(BF16)
            grad = dwkv.astype(F32) * den[0, rows, cols]
            p = grad + retain * p
            q = retain * q - grad * den[1, rows, cols]
        state_p[:, cols] = p
        state_q[:, cols] = q

    @pl.when(i == count - 1)
    def _():
        vsum_ref[...] = jnp.zeros_like(vsum_ref)
        for at in range(4):
            vsum_ref[at : at + 1, :] = jnp.sum(sums[at], axis=0, keepdims=True)
        first_ref[:GROUP, :] = state_p[...]
        first_ref[GROUP:, :] = state_q[...]
        rate = -jnp.exp(vec_ref[9:10, :])
        decay = jnp.exp(rate * float(STEPS * count))
        for q in range(2 * GROUP // CHUNKS):
            base = q * CHUNKS
            total = first_ref[base + CHUNKS - 1 : base + CHUNKS, :]
            for s in reversed(range(CHUNKS - 1)):
                total = decay * total + first_ref[base + s : base + s + 1, :]
            for d in range(total_ref.shape[0]):
                total_ref[d, q : q + 1, :] = total


def wkv_back_kernel(weights, ins, outs, scratch, copies, grad):
    (pieces,) = weights
    flag_ref, k_ref, v_ref, dwkv_ref, dr_ref, st_ref, vec_ref, every_ref, first_ref = ins
    out_ref, vsum_ref, edge_ref, send_ref = outs
    past_a, past_b, state_p, state_q, sums, w_ref, sems = scratch
    i = pl.program_id(0)
    count = pl.num_programs(0)
    loads = column_loads((pieces,), w_ref, sems, 0, 0, 3 * EMBED)
    start_loads(loads)

    @pl.when(i == 0)
    def _():
        sums[...] = jnp.zeros_like(sums)
        rate = -jnp.exp(vec_ref[9:10, :])
        decay = jnp.exp(rate * float(STEPS * count))
        devices, four, _ = every_ref.shape
        micro = four // 2
        whole = jnp.exp(rate * float(STEPS * count * CHUNKS))
        for q in range(2 * GROUP // CHUNKS):
            state = jnp.zeros((1, EMBED), F32)
            passed = state
            for d in reversed(range(devices)):
                state = jnp.where(flag_ref[micro] == d, passed, state)
                begins = flag_ref[micro + 1 + d * micro + q % micro]
                passed = jnp.where(begins > 0, 0.0, whole * passed + every_ref[d, q : q + 1, :])
            target = state_p if q < GROUP // CHUNKS else state_q
            base = (q % (GROUP // CHUNKS)) * CHUNKS
            for s in reversed(range(CHUNKS)):
                target[base + s : base + s + 1, :] = state
                state = decay * state + first_ref[q * CHUNKS + s : q * CHUNKS + s + 1, :]

    wait_load(copies)
    grad()
    for cols in col_chunks():
        right = slice(EMBED + cols.start, EMBED + cols.stop)
        retain = jnp.exp(-jnp.exp(vec_ref[9:10, cols]))
        bonus = vec_ref[10:11, cols]
        a = st_ref[0, :GROUP, cols]
        b = st_ref[0, GROUP:, cols]
        for j in range(STEPS):
            rows = step_rows(j)
            weight = jnp.exp(k_ref[rows, cols].astype(F32))
            past_a[rows, cols] = a
            past_b[rows, cols] = b
            a = retain * a + weight * v_ref[rows, cols].astype(F32)
            b = retain * b + weight
        p = state_p[:, cols]
        q = state_q[:, cols]
        sum_decay = sums[0, :, cols]
        sum_bonus = sums[1, :, cols]
        for j in reversed(range(STEPS)):
            rows = step_rows(j)
            key = k_ref[rows, cols].astype(F32)
            value = v_ref[rows, cols].astype(F32)
            own = jnp.exp(bonus + key)
            weight = jnp.exp(key)
            a = past_a[rows, cols]
            b = past_b[rows, cols]
            scale = pl.reciprocal(b + own)
            wkv = (a + own * value) * scale
            grad = dwkv_ref[rows, cols].astype(F32) * scale
            own_grad = grad * own
            bonus_term = own_grad * (value - wkv)
            out_ref[rows, cols] = (bonus_term + weight * (value * p + q)).astype(BF16)
            out_ref[rows, right] = (own_grad + weight * p).astype(BF16)
            sum_decay += a * p + b * q
            sum_bonus += bonus_term
            p = grad + retain * p
            q = retain * q - grad * wkv
        state_p[:, cols] = p
        state_q[:, cols] = q
        sums[0, :, cols] = sum_decay
        sums[1, :, cols] = sum_bonus

    @pl.when(i == count - 1)
    def _():
        rate = -jnp.exp(vec_ref[9:10, :])
        vsum_ref[...] = jnp.zeros_like(vsum_ref)
        vsum_ref[0:1, :] = jnp.sum(sums[0], axis=0, keepdims=True) * jnp.exp(rate) * rate
        vsum_ref[1:2, :] = jnp.sum(sums[1], axis=0, keepdims=True)
        wait_all(loads)
        rows = slice(0, GROUP)
        edge = dot_nt(out_ref[rows, part(0)], w_ref[:, part(0)]) * (1.0 - vec_ref[4:5, :])
        edge += dot_nt(out_ref[rows, part(1)], w_ref[:, part(1)]) * (1.0 - vec_ref[5:6, :])
        edge += dot_nt(dr_ref[rows, :], w_ref[:, part(2)]) * (1.0 - vec_ref[6:7, :])
        edge_ref[...] = edge
        send_rows(flag_ref, edge, send_ref)


def input_back_kernel(lowest, weights, ins, outs, scratch, copies=(), grad=None):
    (pieces,) = weights
    grad_ref, dr_ref, xp_ref, before_ref, edge_ref, later_ref, got_ref, dx1_ref, vec_ref = ins[:9]
    out_ref, vsum_ref, later_out = outs
    carry, w_ref, back, rows_ref, sums, sems = scratch
    i = pl.program_id(0)
    count = pl.num_programs(0)
    loads = column_loads((pieces,), w_ref, sems, 0, 0, 3 * EMBED)
    start_loads(loads)

    @pl.when(i == 0)
    def _():
        if lowest:
            carry[...] = later_ref[...]
        else:
            take_rows(carry, later_ref, got_ref)
        sums[...] = jnp.zeros_like(sums)

    wait_load(loads + list(copies))
    if grad is not None:
        grad()
    for at, grads in enumerate((grad_ref[:, part(0)], grad_ref[:, part(1)], dr_ref[...])):
        back[at] = dot_nt(grads, w_ref[:, part(at)])
    gain = vec_ref[0:1, :]
    offset = vec_ref[1:2, :]
    n, rstd = normalize(xp_ref[step_rows(STEPS - 1), :].astype(F32))
    later = carry[...]
    for j in reversed(range(STEPS)):
        rows = step_rows(j)
        if j > 0:
            n_next, rstd_next = normalize(xp_ref[step_rows(j - 1), :].astype(F32))
            h_before = n_next * gain + offset
        else:
            n_before, _ = normalize(before_ref[...].astype(F32))
            h_before = n_before * gain + offset
            if lowest:
                h_before = jnp.where(i == count - 1, edge_ref[...], h_before)
        diff = n * gain + offset - h_before
        dh = later
        later = None
        for at in range(3):
            grad = back[at, rows, :]
            kept = grad * vec_ref[4 + at : 5 + at, :]
            sums[2 + at] += grad * diff
            dh = dh + kept
            passed = grad - kept
            later = passed if later is None else later + passed
        sums[0] += dh * n
        sums[1] += dh
        rows_ref[rows, :] = (dx1_ref[rows, :] + norm_back(dh * gain, n, rstd)).astype(BF16)
        if j > 0:
            n, rstd = n_next, rstd_next
    carry[...] = later
    later_out[...] = later
    out_ref[...] = swap_out(rows_ref[...])

    @pl.when(i == count - 1)
    def _():
        vsum_ref[...] = jnp.zeros_like(vsum_ref)
        for at in range(5):
            vsum_ref[at : at + 1, :] = jnp.sum(sums[at], axis=0, keepdims=True)
        if lowest:
            vsum_ref[...] += ins[10][...]


def adam_step(master, moment, second, gradient, rate, shrink):
    moment_new = 0.9 * moment + 0.1 * gradient
    second_new = 0.95 * second + 0.05 * gradient * gradient
    scaled = moment_new / (1.0 - 0.9**STEP) / (jnp.sqrt(second_new / (1.0 - 0.95**STEP)) + 1e-08)
    return (master - rate * (scaled + shrink * master), moment_new, second_new)


def neighbour(block, axis, distance):
    devices = range(lax.axis_size(axis))
    return lax.ppermute(block, axis, [(i, i + distance) for i in devices if i + distance in devices])


def everyone(block, axis):
    count = lax.axis_size(axis)
    return lax.all_to_all(
        jnp.broadcast_to(block[None], (count,) + block.shape), axis, 0, 0, tiled=True
    )


def scatter_rows(grad):
    part = lax.psum_scatter(grad.astype(BF16), "tok", scatter_dimension=0, tiled=True)
    return lax.psum_scatter(part, "rep", scatter_dimension=0, tiled=True).astype(F32)


def weight_grad(a, b):
    return dot_tn(a, b).astype(BF16)


def flip(block, axis, bit):
    return lax.ppermute(block, axis, [(i, i ^ bit) for i in range(lax.axis_size(axis))])


def place_all_kernel(bits_ref, own, far, near, both, out):
    height = own.shape[0]
    for source, high, low in (
        (own, bits_ref[4], bits_ref[3]), (far, 1 - bits_ref[4], bits_ref[3]),
        (near, bits_ref[4], 1 - bits_ref[3]), (both, 1 - bits_ref[4], 1 - bits_ref[3]),
    ):
        out[pl.ds(pl.multiple_of((2 * high + low) * height, height), height), :] = source[...]


def place(kernel, bits, inputs, shapes, name, after=()):
    vmem = pl.BlockSpec(memory_space=pltpu.VMEM)
    return pl.pallas_call(
        ordered(kernel, 0, len(after)),
        in_specs=[ANY_SPEC] * len(after) + [SMEM_SPEC] + [vmem] * len(inputs),
        out_specs=[vmem] * len(shapes),
        out_shape=[jax.ShapeDtypeStruct(shape, BF16) for shape in shapes],
        compiler_params=pltpu.CompilerParams(vmem_limit_bytes=VMEM.get(name, 16) * MIB),
        cost_estimate=cost(name),
        name=name,
    )(*after, bits, *inputs)


def cast_kernel(source, target):
    target[...] = source[...].astype(BF16)


def cast(shard, after, name):
    block = pl.BlockSpec(shard.shape, lambda i: (0, 0))
    return call(
        cast_kernel, 1, [block], block, jax.ShapeDtypeStruct(shard.shape, BF16), [], name, after
    )(shard)


def gather_plain(shard):
    return [lax.all_gather(lax.all_gather(shard, "rep", axis=0, tiled=True), "tok", axis=0, tiled=True)]


def rep_rows(shard):
    far = flip(shard, "rep", 2)
    return shard, far, flip(shard, "rep", 1), flip(far, "rep", 1)


def gather_rep(shard, bits, name, after=()):
    height, width = shard.shape
    return place(place_all_kernel, bits, rep_rows(shard), [(4 * height, width)], name + "_rep", after)[0]


def held(array, after, name):
    return pl.pallas_call(
        lambda *refs: None,
        in_specs=[ANY_SPEC] * (1 + len(after)),
        out_specs=ANY_SPEC,
        out_shape=jax.ShapeDtypeStruct(array.shape, array.dtype),
        input_output_aliases={0: 0},
        cost_estimate=cost(name),
        name=name,
    )(array, *after)


SLOTS = ((0, 0), (0, 1), (1, 0), (1, 1))


def store_slot(outs, slot, value, left):
    dy, dx = SLOTS[slot]
    if left:
        outs[dx][dy] = value
    else:
        outs[2 + dy][dx] = value


def beside(main, counts, pairs, takes, bits_ref, *refs):
    lists, lhs_count = [], 2 * len(pairs)
    for count in (counts[0], counts[1], lhs_count, 2 * len(takes), counts[2], 4, counts[3], 3):
        lists.append(refs[:count])
        refs = refs[count:]
    weights, ins, lhs_refs, rhs_refs, outs, grads, scratch, (lhs, made, sems) = lists
    i = pl.program_id(0)
    steps = pl.num_programs(0)
    height = EMBED // 8
    copies = []
    for at, base in enumerate(pairs):
        for which in range(2):
            for slot, (dy, dx) in enumerate(SLOTS):
                block = base + 4 * (bits_ref[2] ^ dy) + 2 * (bits_ref[1] ^ dx) + bits_ref[0]
                cols = pl.ds(pl.multiple_of(block * height, height), height)
                copies.append(
                    pltpu.make_async_copy(
                        lhs_refs[2 * at + which].at[:, cols],
                        lhs.at[2 * at + which, :, slot * height : (slot + 1) * height],
                        sems.at[len(copies)],
                    )
                )
    start_loads(copies)

    def grad():
        column = 0
        for at, (width, of_step) in enumerate(takes):
            pair = of_step[0] if len(set(of_step)) == 1 else i * len(pairs) // steps
            total = dot_tn(lhs[2 * pair], rhs_refs[2 * at][...]) + dot_tn(lhs[2 * pair + 1], rhs_refs[2 * at + 1][...])
            made[:, column : column + width] = total.astype(BF16)
            column += width

    main(weights, ins, outs, scratch, copies, grad)
    for left in (True, False):

        @pl.when((i < steps // 2) == left)
        def _(left=left):
            for slot in range(4):
                store_slot(grads, slot, made[slot * height : (slot + 1) * height, :], left)


def alone(main, counts, bits_ref, *refs):
    lists = []
    for count in counts:
        lists.append(refs[:count])
        refs = refs[count:]
    main(*lists, [], lambda: None)


def call_main(
    kernel, grid, ins, in_specs, out_specs, out_shape, scratch, name, after, bits, weights, lhs=(), takes=(),
    rhs=(), aliases=None,
):
    counts = (len(weights), len(in_specs), len(out_specs), len(scratch))
    if lhs:
        rows = rhs[0].shape[0]
        height = EMBED // 8
        lhs_args = [array for own, other, _ in lhs for array in (own, other)]
        rhs_specs, rhs_args = [], []
        for width, base, _ in takes:
            rhs_specs += [pl.BlockSpec((rows, width), lambda i, base=base: (0, base + i))] * 2
            rhs_args += rhs
        total = sum(width for width, _, _ in takes)
        left = pl.BlockSpec((2, height, total), lambda i: (0, 0, jnp.minimum(i, grid // 2 - 1)))
        right = pl.BlockSpec((2, height, total), lambda i: (0, 0, jnp.maximum(i - grid // 2, 0)))
        body = functools.partial(
            beside, kernel, counts, [base for _, _, base in lhs], [(width, pair) for width, _, pair in takes]
        )
        in_specs = in_specs + [ANY_SPEC] * len(lhs_args) + rhs_specs
        out_specs = out_specs + [left, left, right, right]
        out_shape = out_shape + [jax.ShapeDtypeStruct((2, height, total * grid // 2), BF16)] * 4
        scratch = scratch + [
            pltpu.VMEM((2 * len(lhs), rows, 4 * height), BF16), pltpu.VMEM((4 * height, total), BF16),
            pltpu.SemaphoreType.DMA((8 * len(lhs),)),
        ]
        ins = (*ins, *lhs_args, *rhs_args)
    else:
        body = functools.partial(alone, kernel, counts)
    heads = len(weights)

    def run(bits_ref, *refs):
        body(bits_ref, *[group[0] for group in refs[:heads]], *refs[heads:])

    results = call(
        run, grid, in_specs, out_specs, out_shape, scratch, name, after, bits, weights, aliases
    )(*ins)
    return results[: counts[2]], results[counts[2] :]


def tall_kernel(bits_ref, lhs_own, lhs_other, rhs_own, rhs_other, *outs):
    i = pl.program_id(0)
    total = dot_tn(lhs_own[...], rhs_own[...]) + dot_tn(lhs_other[...], rhs_other[...])
    total = total.astype(BF16)
    half = total.shape[1] // 2
    for at, (left, right) in enumerate(((0, 2), (0, 3), (1, 2), (1, 3))):

        @pl.when(i == at)
        def _(left=left, right=right):
            outs[left][0] = total[:, :half]
            outs[right][0] = total[:, half:]


def core_grad(bits, lhs, rhs, name, after=()):
    rows, height, width = rhs[0].shape[0], lhs[0].shape[1] // 8, rhs[0].shape[1] // 2

    def column(i, b):
        return (0, 4 * (b[2] ^ (i % 2)) + 2 * (b[1] ^ (i // 2)) + b[0])

    spec = pl.BlockSpec((rows, height), column)
    whole = pl.BlockSpec((rows, 2 * width), lambda i, b: (0, 0))
    return pl.pallas_call(
        ordered(tall_kernel, 1, len(after)),
        grid_spec=pltpu.PrefetchScalarGridSpec(
            num_scalar_prefetch=1,
            grid=(4,),
            in_specs=[ANY_SPEC] * len(after) + [spec, spec, whole, whole],
            out_specs=[
                pl.BlockSpec((1, height, width), lambda i, b: (jnp.minimum(i, 1), 0, 0)),
                pl.BlockSpec((1, height, width), lambda i, b: (jnp.maximum(i - 2, 0), 0, 0)),
                pl.BlockSpec((1, height, width), lambda i, b: (i // 2, 0, 0)),
                pl.BlockSpec((1, height, width), lambda i, b: (i // 2, 0, 0)),
            ],
        ),
        out_shape=[jax.ShapeDtypeStruct((2, height, width), BF16)] * 4,
        compiler_params=pltpu.CompilerParams(
            dimension_semantics=("arbitrary",), vmem_limit_bytes=VMEM.get(name, 16) * MIB
        ),
        cost_estimate=cost(name),
        name=name,
    )(bits, *after, *lhs, *rhs)


def add_kernel(count, bits_ref, *refs):
    for at in range(count):
        total = refs[2 * at][...].astype(F32) + refs[2 * at + 1][...].astype(F32)
        refs[2 * count + at][...] = total.astype(BF16)


def add_split(bits, grid, sums, name, after=()):
    in_specs, out_specs, shapes, args = [], [], [], []
    for a, b, block, source, shape, target in sums:
        in_specs += [pl.BlockSpec(block, source)] * 2
        args += [a, b]
        out_specs.append(pl.BlockSpec(block, target))
        shapes.append(jax.ShapeDtypeStruct(shape, BF16))
    return pl.pallas_call(
        ordered(functools.partial(add_kernel, len(sums)), 1, len(after)),
        grid_spec=pltpu.PrefetchScalarGridSpec(
            num_scalar_prefetch=1, grid=grid, in_specs=[ANY_SPEC] * len(after) + in_specs, out_specs=out_specs
        ),
        out_shape=shapes,
        compiler_params=pltpu.CompilerParams(vmem_limit_bytes=VMEM.get(name, 16) * MIB),
        cost_estimate=cost(name),
        name=name,
    )(bits, *after, *args)


def merge_kernel(moves, bits_ref, p_keep, p_got, q_keep, q_got, *outs):
    p = (p_keep[...].astype(F32) + p_got[...].astype(F32)).astype(BF16)
    q = (q_keep[...].astype(F32) + q_got[...].astype(F32)).astype(BF16)
    half = p.shape[-1]
    if len(outs) == 1:
        for side, start, width, column in moves or ((0, 0, half, 0), (1, 0, q.shape[-1], half)):
            outs[0][:, column : column + width] = (p, q)[side][0, :, start : start + width]
        return
    height = p.shape[1] // 2
    moves = moves or ((0, 0, half, 0), (1, 0, q.shape[-1], half))
    for out, low in ((outs[0], 1 - bits_ref[3]), (outs[1], bits_ref[3])):
        for at in range(2):

            @pl.when(low == at)
            def _(out=out, at=at):
                rows = slice(at * height, (at + 1) * height)
                for side, start, width, column in moves:
                    out[0, :, column : column + width] = (p, q)[side][0, rows, start : start + width]


def merge(bits, p_keep, p_got, q_keep, q_got, shapes, name, after, moves=()):
    _, block, p_width = p_keep.shape
    q_width = q_keep.shape[2]
    in_specs = [
        pl.BlockSpec((1, block // 2, width), lambda h, b: (0, h, 0))
        for width in (p_width, p_width, q_width, q_width)
    ]
    if len(shapes) == 1:
        out_specs = [pl.BlockSpec((block // 2, p_width + q_width), lambda h, b: (h, 0))]
    else:
        out_specs = [pl.BlockSpec((1,) + shapes[0][1:], lambda h, b: (h, 0, 0))] * 2
    return pl.pallas_call(
        ordered(functools.partial(merge_kernel, moves), 1, len(after)),
        grid_spec=pltpu.PrefetchScalarGridSpec(
            num_scalar_prefetch=1, grid=(2,), in_specs=[ANY_SPEC] * len(after) + in_specs, out_specs=out_specs
        ),
        out_shape=[jax.ShapeDtypeStruct(shape, BF16) for shape in shapes],
        compiler_params=pltpu.CompilerParams(vmem_limit_bytes=VMEM.get(name, 16) * MIB),
        cost_estimate=cost(name),
        name=name,
    )(bits, *after, p_keep, p_got, q_keep, q_got)


def reduce_grad(bits, made, offload, name, moves=()):
    p_keep, p_send, q_keep, q_send = made
    p_got, q_got = flip(p_send, "tok", 2), flip(q_send, "tok", 4)
    after = yield p_keep
    _, block, p_width = p_keep.shape
    q_width = q_keep.shape[2]
    half = block // 2
    sums = []
    for which in (1, 0):
        for keep, got, width in ((p_keep, p_got, p_width), (q_keep, q_got, q_width)):
            sums.append((
                keep, got, (1, half, width), lambda r, b, which=which: (which, r, 0),
                (1, block, width), lambda r, b: (0, r, 0),
            ))
    p_send, q_send, p_keep, q_keep = add_split(bits, (2,), sums, name + "_add_first", after)
    p_got, q_got = flip(p_send, "tok", 4), flip(q_send, "tok", 2)
    after = yield p_keep
    width = p_width + q_width
    if offload:
        (total,) = merge(bits, p_keep, p_got, q_keep, q_got, [(block, width)], name + "_merge", after, moves)
        yield total
        part = lax.psum_scatter(total, "rep", scatter_dimension=0, tiled=True)
        yield part
        yield part.astype(F32)
        return
    shape = (2, block // 4, width)
    send, keep = merge(bits, p_keep, p_got, q_keep, q_got, [shape] * 2, name + "_merge", after, moves)
    got = flip(send, "rep", 1)
    after = yield keep
    sums = [
        (keep, got, (1,) + shape[1:], lambda i, b, f=f: (b[4] ^ f, 0, 0), (1,) + shape[1:], lambda i, b: (0, 0, 0))
        for f in (1, 0)
    ]
    send, keep = add_split(bits, (1,), sums, name + "_add_low", after)
    got = flip(send, "rep", 2)
    yield keep
    yield got
    yield (keep.astype(F32) + got.astype(F32))[0]


def reduce_plain(lhs, rhs):
    sums, column = [], 0
    for array, _, base, tiles in lhs:
        if array.shape[1] > EMBED and array.shape[1] != FF:
            array = array[:, base * EMBED // 8 : base * EMBED // 8 + EMBED]
        sums.append(scatter_rows(weight_grad(array, rhs[0][:, part(column, tiles)])))
        column += tiles
    total = jnp.concatenate(sums, axis=1)
    for _ in range(5):
        yield total[:8]
    yield total


def advance(work, *after):
    return work.send(tuple(after))


def on_device(
    tokens, cotangent, init_num, init_den, prev_att, seg_doc, w_kvr, w_out, f_kr, f_value, vectors,
    m_kvr, v_kvr, m_out, v_out, m_fkr, v_fkr, m_fvalue, v_fvalue, vec_m, vec_v,
):
    tok_count = lax.axis_size("tok")
    rep_count = lax.axis_size("rep")
    here = lax.axis_index("tok")
    flat_index = here * rep_count + lax.axis_index("rep")
    micro, _, local_len, _ = tokens.shape
    seg_count = seg_doc.shape[2]
    chunk = local_len // CHUNKS
    blocks = chunk // STEPS
    rows = micro * local_len

    rep_index = lax.axis_index("rep")
    bits = jnp.stack([here & 1, (here >> 1) & 1, (here >> 2) & 1, rep_index & 1, (rep_index >> 1) & 1])
    bits = bits.astype(jnp.int32)
    paired = tok_count == 8 and rep_count == 4
    att_shard = jnp.concatenate([w_kvr, w_out], axis=1).astype(BF16)
    before_mix = before_wkv = before_hidden = ()
    if paired:
        half_cols = EMBED // 2
        value_left, value_raw = f_value[:, :half_cols].astype(BF16), f_value[:, half_cols:].astype(BF16)
        att_part = gather_rep(att_shard, bits, "place_att")
        att_w = [lax.all_gather(att_part, "tok", axis=0, tiled=True)]
        hidden_part = gather_rep(cast(f_kr, (att_part,), "cast_hidden"), bits, "place_hidden")
        fkr = [lax.all_gather(hidden_part, "tok", axis=0, tiled=True)]
        value_rows = lax.all_gather(value_raw, "tok", axis=0, tiled=True)
        value_part = gather_rep(value_left, bits, "place_value", (hidden_part,))
        fvalue = [lax.all_gather(value_part, "tok", axis=0, tiled=True)]
        value_rows = held(value_rows, (value_part,), "hold_value")
        value_far = flip(value_rows, "rep", 2)
        value_near = flip(value_rows, "rep", 1)
        value_others = [value_rows, value_far, value_near, flip(value_far, "rep", 1)]
        before_mix = (value_rows,)
        before_wkv = (value_far, value_near)
    else:
        value_others = []
        att_w, fkr, fvalue = gather_plain(att_shard), gather_plain(f_kr.astype(BF16)), gather_plain(f_value.astype(BF16))

    def other_core(array):
        return flip(array, "tok", 1) if paired else None

    documents = seg_doc[:, 0, :]
    marker = jnp.concatenate(
        [jnp.ones((micro, 1), jnp.bool_), documents[:, 1:] != documents[:, :-1]], axis=1
    )
    starts = jnp.arange(tok_count) * local_len
    fresh = jnp.logical_and(marker[:, starts // SEG_LEN], (starts % SEG_LEN == 0)[None, :])
    fresh_here = lax.dynamic_index_in_dim(fresh, here, 1, keepdims=True)
    seg_here = here * local_len // SEG_LEN
    prev_here = lax.dynamic_index_in_dim(prev_att[:, 0], seg_here, 1, keepdims=False).astype(F32)
    init_all = everyone(jnp.concatenate([init_num[:, 0], init_den[:, 0]], axis=0), "tok")
    init_all = jnp.moveaxis(init_all, 0, 2).reshape(2 * micro, seg_count, EMBED)
    rate = -jnp.exp(vectors[9:10])
    fade = jnp.exp(rate * float(local_len))
    fresh_four = jnp.concatenate([fresh, fresh], axis=0)
    flags = jnp.concatenate(
        [fresh_here[:, 0].astype(jnp.int32), jnp.reshape(here, (1,)).astype(jnp.int32),
         jnp.moveaxis(fresh, 1, 0).reshape(-1).astype(jnp.int32)]
    )

    x4 = tokens.reshape(micro, CHUNKS, chunk, EMBED)
    c4 = cotangent.reshape(micro, CHUNKS, chunk, EMBED)

    def edge_back(last, incoming):
        moved = jnp.concatenate([incoming[:, None], last.reshape(micro, CHUNKS, EMBED)[:, :-1]], axis=1)
        return moved.reshape(GROUP, EMBED)

    raw_in = neighbour(tokens[:, 0, -1, :], "tok", 1)
    raw_edge = edge_back(x4[:, :, -1, :], raw_in).astype(F32)
    edge_n, _ = normalize(raw_edge)
    edge_h = edge_n * vectors[0:1] + vectors[1:2]
    first_row = (jnp.arange(GROUP) % CHUNKS == 0)[:, None]
    fresh_rows = jnp.repeat(fresh_here[:, 0], CHUNKS)[:, None]
    replace = jnp.logical_and(first_row, fresh_rows)
    edge_one = jnp.where(replace, jnp.repeat(prev_here, CHUNKS, axis=0), edge_h)

    def up(width):
        return pl.BlockSpec((ROWS, width), lambda i: (i, 0))

    def down(width):
        return pl.BlockSpec((ROWS, width), lambda i: (blocks - 1 - i, 0))

    before_spec = pl.BlockSpec(
        (GROUP, EMBED), lambda i: (jnp.maximum((blocks - 1 - i) * STEPS - 1, 0), 0)
    )
    natural_up = pl.BlockSpec((micro, CHUNKS, STEPS, EMBED), lambda i: (0, 0, i, 0))
    natural_down = pl.BlockSpec((micro, CHUNKS, STEPS, EMBED), lambda i: (0, 0, blocks - 1 - i, 0))
    st_up = pl.BlockSpec((1, 2 * GROUP, EMBED), lambda i: (i, 0, 0))
    st_down = pl.BlockSpec((1, 2 * GROUP, EMBED), lambda i: (blocks - 1 - i, 0, 0))
    vec_spec = full(vectors.shape)
    edge_spec = full((GROUP, EMBED))
    state_spec = full((2 * GROUP, EMBED))
    total_spec = full((2 * micro, EMBED))
    sum_spec = full((8, EMBED))

    def like(width, dtype):
        return jax.ShapeDtypeStruct((rows, width), dtype)

    def small(count, dtype=F32):
        return jax.ShapeDtypeStruct((count, EMBED), dtype)

    def weight(height, width):
        return pltpu.VMEM((height, width), BF16)

    sems = pltpu.SemaphoreType.DMA((80,))
    state = pltpu.VMEM((GROUP, EMBED), F32)
    square = 2 * rows * EMBED * EMBED

    xp, mix, k, v, r, ends, totals = call(
        mix_one_kernel, blocks,
        [natural_up, edge_spec, vec_spec],
        [up(EMBED), up(3 * EMBED)] + [up(EMBED)] * 3 + [state_spec, total_spec],
        [like(EMBED, BF16), like(3 * EMBED, BF16), like(EMBED, BF16), like(EMBED, BF16), like(EMBED, BF16),
         small(2 * GROUP), small(2 * micro)],
        [state] * 3 + [weight(EMBED, 3 * EMBED), sems], "mix_one", before_mix, bits, (att_w,),
    )(x4, edge_one, vectors)

    every = everyone(totals, "tok")
    carried = jnp.zeros((2 * micro, EMBED), F32)
    begin = jnp.zeros((2 * micro, EMBED), F32)
    for d in range(tok_count):
        seg = d * local_len // SEG_LEN
        carried = jnp.where(fresh_four[:, d : d + 1], init_all[:, seg], carried)
        begin = jnp.where(here == d, carried, begin)
        carried = fade * carried + every[d]

    wkv, y, x1, mix_two, saved, first_two, last_two = call(
        wkv_kernel, blocks,
        [up(EMBED)] * 4 + [vec_spec, total_spec, state_spec],
        [up(EMBED)] * 3 + [up(2 * EMBED), st_up, edge_spec, edge_spec],
        [like(EMBED, BF16), like(EMBED, BF16), like(EMBED, F32), like(2 * EMBED, BF16),
         jax.ShapeDtypeStruct((blocks, 2 * GROUP, EMBED), F32), small(GROUP), small(GROUP)],
        [state] * 3 + [weight(EMBED, EMBED), sems], "wkv", before_wkv, bits, (att_w,),
    )(k, v, r, xp, vectors, begin, ends)

    if paired:
        mix = held(mix, (last_two,), "hold_mix")
    row_in = neighbour(last_two.reshape(micro, CHUNKS, EMBED)[:, -1], "tok", 1)
    edge_two = jnp.where(replace, 0.0, edge_back(last_two, row_in))
    diff_two = first_two - edge_two
    fixed = jnp.concatenate([edge_two + diff_two * vectors[7:8], edge_two + diff_two * vectors[8:9]], axis=1)
    mix_two = lax.dynamic_update_slice(mix_two, fixed.astype(BF16), (0, 0))

    kq, gate = call(
        hidden_kernel, blocks,
        [up(2 * EMBED)],
        [up(FF), up(EMBED)],
        [like(FF, BF16), like(EMBED, BF16)],
        [weight(EMBED, FF + EMBED), sems], "hidden", before_hidden, bits, (fkr,),
    )(mix_two)
    kq_other, mix_two_other, y_other, mix_other = [other_core(array) for array in (kq, mix_two, y, mix)]

    known = (mix_two_other, y_other, mix_other) if paired else ()
    mixed, dvf, dkf, cp = call(
        value_kernel, blocks,
        [up(FF), up(EMBED), up(EMBED), natural_up],
        [natural_up, up(EMBED), up(FF + EMBED), up(EMBED)],
        [jax.ShapeDtypeStruct(x4.shape, BF16), like(EMBED, BF16), like(FF + EMBED, BF16),
         like(EMBED, BF16)],
        [weight(FF, EMBED), pltpu.VMEM((ROWS, EMBED), F32), weight(ROWS, EMBED), sems],
        "value", known, bits, (fvalue, value_others),
    )(kq, gate, x1, c4)
    row_spec = full((micro, EMBED))
    shift_two, send_two = call(
        edge_kernel, 1,
        [SMEM_SPEC, pl.BlockSpec((GROUP, FF + EMBED), lambda i: (0, 0)), vec_spec], [edge_spec, row_spec],
        [small(GROUP), small(micro)],
        [weight(EMBED, FF + EMBED), sems], "edge", (), bits, (fkr,),
    )(flags, dkf, vectors)

    got_two = neighbour(send_two, "tok", -1)

    def reduced(made, plain, offload, name, moves=()):
        work = reduce_grad(bits, made, offload, name, moves) if paired else reduce_plain(*plain)
        next(work)
        return work

    def fused(kernel, grid, ins, in_specs, out_specs, out_shape, scratch, name, after, weights, lhs, takes, rhs,
              aliases=None):
        if not paired:
            lhs = takes = rhs = ()
        return call_main(
            kernel, grid, ins, in_specs, out_specs, out_shape, scratch, name, after, bits, weights, lhs, takes,
            rhs, aliases,
        )

    wide, narrow = FF // blocks, EMBED // blocks
    dvf_other = other_core(dvf)
    if paired:
        dkf = held(dkf, (dvf_other, shift_two), "hold_dkf")
    dkf_other = other_core(dkf)
    made = core_grad(bits, (kq, kq_other), (dvf, dvf_other), "grad_value", (shift_two,)) if paired else (shift_two,)
    value_sum = reduced(made, ([(kq, None, 0, 1)], (dvf, None)), True, "grad_value")

    got_two = held(got_two, (made[0],), "hold_row")
    every_spec = full((tok_count, 2 * micro, EMBED))
    (dx1, datt, dwkv, vsum_two, firsts, back_totals), grads = fused(
        middle_back_kernel, blocks,
        (dkf, x1, x1, edge_two, shift_two, got_two, cp, vectors, k, v, r, wkv, saved),
        [down(FF + EMBED), down(EMBED), before_spec, edge_spec,
         edge_spec, row_spec, down(EMBED), vec_spec] + [down(EMBED)] * 4 + [st_down],
        [down(EMBED), down(2 * EMBED), down(EMBED)] + [sum_spec, state_spec, every_spec],
        [like(EMBED, F32), like(2 * EMBED, BF16), like(EMBED, BF16), small(8),
         small(2 * GROUP), jax.ShapeDtypeStruct((tok_count, 2 * micro, EMBED), F32)],
        [state, pltpu.VMEM((2, ROWS, EMBED), F32), state, state, weight(EMBED, FF + EMBED),
         weight(EMBED, EMBED), pltpu.VMEM((ROWS, EMBED), F32), pltpu.VMEM((ROWS, EMBED), F32),
         pltpu.VMEM((4, GROUP, EMBED), F32), sems],
        "middle_back", (made[0],), (fkr, att_w),
        [(mix_two, mix_two_other, 0), (mix_two, mix_two_other, 8)],
        [(FF // blocks, 0, (0,) * blocks), (EMBED // blocks, FF * blocks // EMBED, (1,) * blocks)], (dkf, dkf_other),
    )
    hidden_sum = reduced(
        grads, ([(mix_two, None, 0, 4), (mix_two, None, 8, 1)], (dkf, None)), False, "grad_hidden",
        [(at // (blocks // 2), at % (blocks // 2) * (wide + narrow), wide, at * wide) for at in range(blocks)]
        + [(at // (blocks // 2), at % (blocks // 2) * (wide + narrow) + wide, narrow, FF + at * narrow)
           for at in range(blocks)],
    )

    every_back = lax.all_to_all(back_totals, "tok", 0, 0, tiled=True)
    made = advance(value_sum, firsts)
    datt_other = other_core(datt)
    right_down = pl.BlockSpec((ROWS, EMBED), lambda i: (blocks - 1 - i, 1))
    (dkv, vsum_wkv, shift_one, send_one), grads = fused(
        wkv_back_kernel, blocks,
        (flags, k, v, dwkv, datt, saved, vectors, every_back, firsts),
        [SMEM_SPEC] + [down(EMBED)] * 3 + [right_down, st_down, vec_spec, every_spec, state_spec],
        [down(2 * EMBED), sum_spec, edge_spec, row_spec],
        [like(2 * EMBED, BF16), small(8), small(GROUP), small(micro)],
        [pltpu.VMEM((ROWS, EMBED), F32)] * 2 + [state] * 2
        + [pltpu.VMEM((2, GROUP, EMBED), F32), weight(EMBED, 3 * EMBED), sems],
        "wkv_back", (made,), (att_w,),
        [(y, y_other, 0), (mix, mix_other, 16)], [(2 * EMBED // blocks, 0, (0, 0, 1, 1))], (datt, datt_other),
    )
    early_sum = reduced(grads, ([(y, None, 0, 1), (mix, None, 16, 1)], (datt, None)), False, "grad_early")
    dkv_other = other_core(dkv)

    got_one = neighbour(send_one, "tok", -1)
    made = advance(value_sum, dkv)
    value_part = advance(value_sum)
    made = advance(hidden_sum, made)
    made = advance(early_sum, made)

    half = blocks // 2

    def input_back(high, before, later_rows, started):
        def at(width, column=0):
            return pl.BlockSpec((ROWS, width), lambda i: (high - i, column))

        before_block = pl.BlockSpec((GROUP, EMBED), lambda i: (jnp.maximum((high - i) * STEPS - 1, 0), 0))
        natural = pl.BlockSpec((micro, CHUNKS, STEPS, EMBED), lambda i: (0, 0, high - i, 0))
        return fused(
            functools.partial(input_back_kernel, bool(started)), half,
            (dkv, datt, xp, xp, edge_one, later_rows, got_one, dx1, vectors, *started),
            [at(2 * EMBED), at(EMBED, 1), at(EMBED), before_block, edge_spec, edge_spec, row_spec, at(EMBED), vec_spec]
            + [ANY_SPEC, sum_spec][: len(started)],
            [natural, sum_spec, edge_spec],
            [jax.ShapeDtypeStruct(x4.shape, BF16), small(8), small(GROUP)],
            [state, weight(EMBED, 3 * EMBED), pltpu.VMEM((3, ROWS, EMBED), F32), weight(ROWS, EMBED),
             pltpu.VMEM((5, GROUP, EMBED), F32), sems],
            "input_back_low" if started else "input_back_high", before, (att_w,),
            () if started else [(mix, mix_other, 0), (mix, mix_other, 8)], [(EMBED, 0, (0, 1))], (dkv, dkv_other),
            {len(before) + 1 + len(att_w) + 9: 0} if started else None,
        )

    (token_high, vsum_high, later_half), grads = input_back(blocks - 1, (made,), shift_one, ())
    late_sum = reduced(grads, ([(mix, None, 0, 1), (mix, None, 8, 1)], (dkv, None)), False, "grad_late")
    made = advance(hidden_sum, vsum_high)
    made = advance(early_sum, made)
    (token_grad, vsum_one, _), _ = input_back(half - 1, (made, value_part), later_half, (token_high, vsum_high))

    made = advance(late_sum, vsum_one)
    made = advance(hidden_sum, made)
    hidden_got = advance(hidden_sum)
    made = advance(late_sum, made)
    made = advance(early_sum, made)
    early_got = advance(early_sum)
    columns = vec_m.shape[1]
    grad_vec = held(jnp.concatenate([vsum_one, vsum_two, vsum_wkv], axis=0), (made,), "hold_vec")
    pieces = jnp.moveaxis(grad_vec.reshape(grad_vec.shape[0], tok_count * rep_count, columns), 1, 0)
    vec_terms = lax.all_to_all(pieces, ("tok", "rep"), 0, 0, tiled=True)
    made = advance(late_sum, made, hidden_got, early_got)
    advance(late_sum)
    sum_fvalue = advance(value_sum)
    if not paired:
        sum_fvalue = advance(value_sum)
    sum_fkr = advance(hidden_sum)
    sum_early = advance(early_sum)
    sum_late = advance(late_sum)
    sums = jnp.sum(held(vec_terms, (made,), "hold_terms"), axis=0)
    sum_vec = jnp.concatenate([sums[0:2], sums[8:10], sums[2:5], sums[10:12], sums[16:18]], axis=0)
    sum_out = sum_early[:, :EMBED]
    sum_kvr = jnp.concatenate([sum_late, sum_early[:, EMBED:]], axis=1)

    base_rate = 2.5 / math.sqrt(EMBED)
    new_kvr = adam_step(w_kvr, m_kvr, v_kvr, sum_kvr, base_rate, 0.01)
    new_out = adam_step(w_out, m_out, v_out, sum_out, 4.0 * base_rate, 0.01)
    new_fkr = adam_step(f_kr, m_fkr, v_fkr, sum_fkr, base_rate, 0.01)
    new_fvalue = adam_step(f_value, m_fvalue, v_fvalue, sum_fvalue, 2.5 / math.sqrt(FF), 0.01)
    vec_master = lax.dynamic_slice_in_dim(vectors, flat_index * columns, columns, 1)
    vec_rates = jnp.array([0.6, 0.3, 0.6, 0.3, 0.3, 0.3, 0.3, 0.3, 0.3, 3.0, 0.5], F32)[:, None]
    new_vectors = adam_step(vec_master, vec_m, vec_v, sum_vec, vec_rates, 0.0)
    shape = tokens.shape
    return (
        (mixed.reshape(shape), token_grad.reshape(shape))
        + new_kvr + new_out + new_fkr + new_fvalue + new_vectors
    )


def solution(mesh):
    rows = P(("tok", "rep"), None)
    columns = P(None, ("tok", "rep"))
    token_spec = P(None, "rep", "tok", None)
    channel_spec = P(None, "rep", None, "tok")
    placed = (
        (token_spec, token_spec, channel_spec, channel_spec, P(None, "rep", None, None), P(None, "rep", None))
        + (rows,) * 4 + (P(),) + (rows,) * 8 + (columns,) * 2
    )
    return jax.shard_map(
        on_device,
        mesh=mesh,
        in_specs=placed,
        out_specs=(token_spec, token_spec) + (rows,) * 12 + (columns,) * 3,
        check_vma=False,
    )
```

```python
import functools
import math

import jax
import jax.numpy as jnp
from jax import lax
from jax.experimental import pallas as pl
from jax.experimental.pallas import tpu as pltpu
from jax.sharding import PartitionSpec as P

EMBED = 1024
FF = 4096
SEG_LEN = 2048
STEP = 10
CHUNKS = 8
GROUP = 16
STEPS = 16
ROWS = STEPS * GROUP
COLS = 256
EPS = 1e-05
TINY = 1.2e-38
COSTS = dict(
    value=60, edge=14, grad_value=30, grad_hidden=40, grad_value_add_first=8, grad_hidden_add_first=100, wkv_back=24,
    grad_value_merge=50, grad_hidden_merge=50, input_back_high=24,
)
F32 = jnp.float32
BF16 = jnp.bfloat16
MIB = 1024 * 1024
VMEM = dict(
    mix_one=30, wkv=28, hidden=36, value=60, edge=60, grad_value=60, middle_back=60, wkv_back=60, input_back_high=44,
    input_back_low=60, grad_hidden_merge=60, grad_value_add_first=60, grad_hidden_add_first=60, grad_value_merge=60, grad_hidden=60,
)


def dot_nn(a, b):
    return jnp.dot(a, b, preferred_element_type=F32)


def dot_nt(a, b):
    return lax.dot_general(a, b, (((1,), (1,)), ((), ())), preferred_element_type=F32)


def dot_tn(a, b):
    return lax.dot_general(a, b, (((0,), (0,)), ((), ())), preferred_element_type=F32)


def sigmoid(v):
    return 0.5 * jnp.tanh(0.5 * v) + 0.5


def normalize(v):
    center = v - jnp.mean(v, axis=-1, keepdims=True)
    rstd = lax.rsqrt(jnp.mean(center * center, axis=-1, keepdims=True) + EPS)
    return center * rstd, rstd


def norm_back(e, n, rstd):
    return (e - jnp.mean(e, axis=-1, keepdims=True) - n * jnp.mean(e * n, axis=-1, keepdims=True)) * rstd


def swap_matrix():
    row = lax.broadcasted_iota(jnp.int32, (ROWS, ROWS), 0)
    col = lax.broadcasted_iota(jnp.int32, (ROWS, ROWS), 1)
    return jnp.where(col == (row % GROUP) * STEPS + row // GROUP, 1.0, 0.0).astype(BF16)


def swap_in(block):
    return dot_nn(swap_matrix(), block.reshape(ROWS, EMBED))


def swap_out(rows):
    moved = dot_nn(swap_matrix(), rows).astype(BF16)
    return moved.reshape(GROUP // CHUNKS, CHUNKS, STEPS, EMBED)


def part(at, count=1):
    return slice(at * EMBED, (at + count) * EMBED)


def col_chunks():
    return [slice(c * COLS, (c + 1) * COLS) for c in range(EMBED // COLS)]


def step_rows(j):
    return slice(j * GROUP, (j + 1) * GROUP)


def full(shape):
    return pl.BlockSpec(shape, lambda i: (0,) * len(shape), pipeline_mode=pl.Buffered(buffer_count=1))


def ordered(kernel, skip, count):
    return lambda *refs: kernel(*refs[:skip], *refs[skip + count :])


def cost(name):
    return pl.CostEstimate(flops=int(COSTS.get(name, 2) * 1e9), bytes_accessed=0, transcendentals=0)


def call(kernel, grid, in_specs, out_specs, out_shape, scratch, name, after=(), bits=None, weights=(), aliases=None):
    if bits is not None:
        kernel = grouped(kernel, [len(pieces) for pieces in weights])
        in_specs = [SMEM_SPEC] + [ANY_SPEC] * sum(len(pieces) for pieces in weights) + in_specs
    made = pl.pallas_call(
        ordered(kernel, 0, len(after)),
        grid=(grid,),
        in_specs=[ANY_SPEC] * len(after) + in_specs,
        out_specs=out_specs,
        out_shape=out_shape,
        scratch_shapes=scratch,
        compiler_params=pltpu.CompilerParams(
            dimension_semantics=("arbitrary",), vmem_limit_bytes=VMEM.get(name, 16) * MIB
        ),
        cost_estimate=cost(name),
        input_output_aliases=aliases or {},
        name=name,
    )
    head = (bits,) + tuple(piece for pieces in weights for piece in pieces) if bits is not None else ()
    return lambda *args: made(*after, *head, *args)


def grouped(kernel, counts):
    def run(bits_ref, *refs):
        groups = []
        for count in counts:
            groups.append(refs[:count])
            refs = refs[count:]
        return kernel(bits_ref, *groups, *refs)

    return run


SMEM_SPEC = pl.BlockSpec(memory_space=pltpu.SMEM)
ANY_SPEC = pl.BlockSpec(memory_space=pl.ANY)


def column_loads(pieces, target, sems, first, low, high, base=0, bits_ref=None):
    cols, place = slice(low, high), slice(low - base, high - base)
    if len(pieces) == 1:
        return [pltpu.make_async_copy(pieces[0].at[:, cols], target.at[:, place], sems.at[first])]
    copies = []
    height = target.shape[0] // 8
    for piece, core in zip(pieces, (bits_ref[0], 1 - bits_ref[0])):
        for q in range(4):
            rows = pl.ds(pl.multiple_of((2 * q + core) * height, height), height)
            copies.append(
                pltpu.make_async_copy(
                    piece.at[q * height : (q + 1) * height, cols], target.at[rows, place],
                    sems.at[first + len(copies)],
                )
            )
    return copies


def start_loads(*loads):
    @pl.when(pl.program_id(0) == 0)
    def _():
        for copies in loads:
            for copy in copies:
                copy.start()


def wait_all(copies):
    for copy in copies:
        copy.wait()


def wait_load(copies):
    pl.when(pl.program_id(0) == 0)(lambda: wait_all(copies))


def first_and_rest(body):
    pl.when(pl.program_id(0) == 0)(lambda: body(True))
    pl.when(pl.program_id(0) > 0)(lambda: body(False))


def mix_one_kernel(
    bits_ref, pieces, tok_ref, edge_ref, vec_ref,
    xp_ref, mix_ref, k_ref, v_ref, r_ref, end_ref, total_ref,
    carry, state_a, state_b, w_ref, sems,
):
    i = pl.program_id(0)
    loads = [
        column_loads(pieces, w_ref, sems, 16 * at, at * EMBED, (at + 1) * EMBED) for at in range(3)
    ]
    start_loads(*loads)

    @pl.when(i == 0)
    def _():
        carry[...] = edge_ref[...]
        state_a[...] = jnp.zeros_like(state_a)
        state_b[...] = jnp.zeros_like(state_b)

    xp_ref[...] = swap_in(tok_ref[...]).astype(BF16)
    hp = carry[...]
    for j in range(STEPS):
        rows = step_rows(j)
        n, _ = normalize(xp_ref[rows, :].astype(F32))
        h = n * vec_ref[0:1, :] + vec_ref[1:2, :]
        diff = h - hp
        for at in range(3):
            mix_ref[rows, part(at)] = (hp + diff * vec_ref[4 + at : 5 + at, :]).astype(BF16)
        hp = h
    carry[...] = hp

    def project(first):
        for at, out_ref in enumerate((k_ref, v_ref, r_ref)):
            if first:
                wait_all(loads[at])
            out_ref[...] = dot_nn(mix_ref[:, part(at)], w_ref[:, part(at)]).astype(out_ref.dtype)

    first_and_rest(project)
    for cols in col_chunks():
        retain = jnp.exp(-jnp.exp(vec_ref[9:10, cols]))
        a = state_a[:, cols]
        b = state_b[:, cols]
        for j in range(STEPS):
            weight = jnp.exp(k_ref[step_rows(j), cols].astype(F32))
            a = retain * a + weight * v_ref[step_rows(j), cols].astype(F32)
            b = retain * b + weight
        state_a[:, cols] = a
        state_b[:, cols] = b

    @pl.when(i == pl.num_programs(0) - 1)
    def _():
        end_ref[:GROUP, :] = state_a[...]
        end_ref[GROUP:, :] = state_b[...]
        rate = -jnp.exp(vec_ref[9:10, :])
        decay = jnp.exp(rate * float(STEPS * pl.num_programs(0)))
        for q in range(2 * GROUP // CHUNKS):
            total = end_ref[q * CHUNKS : q * CHUNKS + 1, :]
            for s in range(1, CHUNKS):
                total = decay * total + end_ref[q * CHUNKS + s : q * CHUNKS + s + 1, :]
            total_ref[q : q + 1, :] = total


def wkv_kernel(
    bits_ref, pieces, k_ref, v_ref, r_ref, xp_ref, vec_ref, start_ref, end_ref,
    wkv_ref, y_ref, x1_ref, mix_ref, st_ref, first_ref, last_ref,
    carry, state_a, state_b, w_ref, sems,
):
    i = pl.program_id(0)
    loads = column_loads(pieces, w_ref, sems, 0, 3 * EMBED, 4 * EMBED, 3 * EMBED)
    start_loads(loads)

    @pl.when(i == 0)
    def _():
        rate = -jnp.exp(vec_ref[9:10, :])
        decay = jnp.exp(rate * float(STEPS * pl.num_programs(0)))
        for q in range(2 * GROUP // CHUNKS):
            state = start_ref[q : q + 1, :]
            target = state_a if q < GROUP // CHUNKS else state_b
            base = (q % (GROUP // CHUNKS)) * CHUNKS
            for s in range(CHUNKS):
                target[base + s : base + s + 1, :] = state
                state = decay * state + end_ref[q * CHUNKS + s : q * CHUNKS + s + 1, :]
        carry[...] = jnp.zeros_like(carry)

    st_ref[0, :GROUP, :] = state_a[...]
    st_ref[0, GROUP:, :] = state_b[...]
    for cols in col_chunks():
        retain = jnp.exp(-jnp.exp(vec_ref[9:10, cols]))
        bonus = vec_ref[10:11, cols]
        a = state_a[:, cols]
        b = state_b[:, cols]
        for j in range(STEPS):
            rows = step_rows(j)
            key = k_ref[rows, cols].astype(F32)
            value = v_ref[rows, cols].astype(F32)
            own = jnp.exp(bonus + key)
            weight = jnp.exp(key)
            wkv = ((a + own * value) * pl.reciprocal(b + own)).astype(BF16)
            wkv_ref[rows, cols] = wkv
            y_ref[rows, cols] = (sigmoid(r_ref[rows, cols].astype(F32)) * wkv.astype(F32)).astype(BF16)
            a = retain * a + weight * value
            b = retain * b + weight
        state_a[:, cols] = a
        state_b[:, cols] = b
    wait_load(loads)
    x1_ref[...] = xp_ref[...].astype(F32) + dot_nn(y_ref[...], w_ref[...])
    hp = carry[...]
    for j in range(STEPS):
        rows = step_rows(j)
        n, _ = normalize(x1_ref[rows, :])
        h = n * vec_ref[2:3, :] + vec_ref[3:4, :]
        diff = h - hp
        for at in range(2):
            mix_ref[rows, part(at)] = (hp + diff * vec_ref[7 + at : 8 + at, :]).astype(BF16)
        if j == 0:

            @pl.when(i == 0)
            def _(h=h):
                first_ref[...] = h

        hp = h
    carry[...] = hp
    last_ref[...] = hp


def hidden_kernel(bits_ref, pieces, mix_ref, kq_ref, gate_ref, w_ref, sems):
    loads = [
        column_loads(pieces, w_ref, sems, 16 * at, at * EMBED, (at + 1) * EMBED) for at in range(5)
    ]
    start_loads(*loads)

    def project(first):
        for c in range(FF // EMBED):
            if first:
                wait_all(loads[c])
            active = jnp.maximum(dot_nn(mix_ref[:, part(0)], w_ref[:, part(c)]), 0.0)
            kq_ref[:, part(c)] = (active * active).astype(BF16)
        if first:
            wait_all(loads[4])
        gate_ref[...] = dot_nn(mix_ref[:, part(1)], w_ref[:, FF:]).astype(BF16)

    first_and_rest(project)


def rep_loads(bits_ref, pieces, target, sems, first, low):
    copies = []
    for at, piece in enumerate(pieces):
        high = bits_ref[4] if at % 2 == 0 else 1 - bits_ref[4]
        bit = bits_ref[3] if at < 2 else 1 - bits_ref[3]
        height = target.shape[0] // 32
        for block in range(8):
            rows = pl.ds(pl.multiple_of((4 * block + 2 * high + bit) * height, height), height)
            copies.append(
                pltpu.make_async_copy(
                    piece.at[block * height : (block + 1) * height, :], target.at[rows, low:],
                    sems.at[first + len(copies)],
                )
            )
    return copies


def value_kernel(
    bits_ref, pieces, others, kq_ref, gate_ref, x1_ref, cot_ref,
    mixed_ref, dvf_ref, grad_ref, cp_ref, w_ref, vf_ref, out_ref, sems,
):
    half = EMBED // 2
    if others:
        loads = [
            column_loads(pieces, w_ref, sems, 0, 0, half),
            rep_loads(bits_ref, others, w_ref, sems, 1, half),
        ]
    else:
        loads = [column_loads(pieces, w_ref, sems, at, at * half, (at + 1) * half) for at in range(2)]
    start_loads(*loads)
    cp_ref[...] = swap_in(cot_ref[...]).astype(BF16)

    def project(first):
        if not first:
            vf_ref[...] = dot_nn(kq_ref[...], w_ref[...])
            return
        for at in range(2):
            wait_all(loads[at])
            cols = slice(at * half, (at + 1) * half)
            vf_ref[:, cols] = dot_nn(kq_ref[...], w_ref[:, cols])

    first_and_rest(project)
    for j in range(STEPS):
        rows = step_rows(j)
        gate = sigmoid(gate_ref[rows, :].astype(F32))
        vf = vf_ref[rows, :]
        out_ref[rows, :] = (x1_ref[rows, :] + gate * vf).astype(BF16)
        scaled = cp_ref[rows, :].astype(F32) * gate
        dvf_ref[rows, :] = scaled.astype(BF16)
        grad_ref[rows, FF:] = (scaled * vf * (1.0 - gate)).astype(BF16)
    for c in range(FF // EMBED):
        back = dot_nt(dvf_ref[...], w_ref[part(c), :])
        square = kq_ref[:, part(c)].astype(F32)
        root = square * lax.rsqrt(jnp.maximum(square, TINY))
        grad_ref[:, part(c)] = (back * (2.0 * root)).astype(BF16)
    mixed_ref[...] = swap_out(out_ref[...])


def send_rows(flag_ref, shift, send_ref):
    for m in range(send_ref.shape[0]):
        row = shift[m * CHUNKS : m * CHUNKS + 1]
        send_ref[m : m + 1, :] = jnp.where(flag_ref[m] > 0, 0.0, row)


def take_rows(carry, shift_ref, got_ref):
    for m in range(got_ref.shape[0]):
        base = m * CHUNKS
        carry[base : base + CHUNKS - 1, :] = shift_ref[base + 1 : base + CHUNKS, :]
        carry[base + CHUNKS - 1 : base + CHUNKS, :] = got_ref[m : m + 1, :]


def edge_kernel(bits_ref, pieces, flag_ref, grad_ref, vec_ref, shift_ref, send_ref, w_ref, sems):
    loads = column_loads(pieces, w_ref, sems, 0, 0, FF + EMBED)
    start_loads(loads)
    wait_all(loads)
    shift = dot_nt(grad_ref[:, :FF], w_ref[:, :FF]) * (1.0 - vec_ref[7:8, :])
    shift += dot_nt(grad_ref[:, FF:], w_ref[:, FF:]) * (1.0 - vec_ref[8:9, :])
    shift_ref[...] = shift
    send_rows(flag_ref, shift, send_ref)


def add_sums(sums, values):
    for at, value in enumerate(values):
        sums[at] += value


def middle_back_kernel(weights, ins, outs, scratch, copies, grad):
    pieces, out_pieces = weights
    (
        grad_ref, x1_ref, before_ref, edge_ref, later_ref, got_ref, cp_ref, vec_ref, k_ref, v_ref, r_ref, wkv_ref,
        st_ref,
    ) = ins
    dx1_ref, out_ref, dwkv_ref, vsum_ref, first_ref, total_ref = outs
    carry, den, state_p, state_q, w_ref, wo_ref, dxk_ref, dxr_ref, sums, sems = scratch
    i = pl.program_id(0)
    count = pl.num_programs(0)
    loads = [
        column_loads((pieces,), w_ref, sems, 0, 0, FF + EMBED),
        column_loads((out_pieces,), wo_ref, sems, 16, 3 * EMBED, 4 * EMBED, 3 * EMBED),
    ]
    start_loads(*loads)

    @pl.when(i == 0)
    def _():
        take_rows(carry, later_ref, got_ref)
        sums[...] = jnp.zeros_like(sums)
        state_p[...] = jnp.zeros_like(state_p)
        state_q[...] = jnp.zeros_like(state_q)

    for cols in col_chunks():
        retain = jnp.exp(-jnp.exp(vec_ref[9:10, cols]))
        bonus = vec_ref[10:11, cols]
        a = st_ref[0, :GROUP, cols]
        b = st_ref[0, GROUP:, cols]
        for j in range(STEPS):
            rows = step_rows(j)
            key = k_ref[rows, cols].astype(F32)
            value = v_ref[rows, cols].astype(F32)
            own = jnp.exp(bonus + key)
            weight = jnp.exp(key)
            scale = pl.reciprocal(b + own)
            den[0, rows, cols] = scale
            den[1, rows, cols] = (a + own * value) * scale
            a = retain * a + weight * value
            b = retain * b + weight
    wait_load(loads[0] + loads[1] + copies)
    dxk_ref[...] = dot_nt(grad_ref[:, :FF], w_ref[:, :FF])
    dxr_ref[...] = dot_nt(grad_ref[:, FF:], w_ref[:, FF:])
    grad()
    gain = vec_ref[2:3, :]
    offset = vec_ref[3:4, :]
    share_k = vec_ref[7:8, :]
    share_r = vec_ref[8:9, :]
    n, rstd = normalize(x1_ref[step_rows(STEPS - 1), :])
    later = carry[...]
    for j in reversed(range(STEPS)):
        rows = step_rows(j)
        if j > 0:
            n_next, rstd_next = normalize(x1_ref[step_rows(j - 1), :])
            h_before = n_next * gain + offset
        else:
            n_before, _ = normalize(before_ref[...])
            h_before = jnp.where(i == count - 1, edge_ref[...], n_before * gain + offset)
        diff = n * gain + offset - h_before
        dxk = dxk_ref[rows, :]
        dxr = dxr_ref[rows, :]
        kept_k = dxk * share_k
        kept_r = dxr * share_r
        dh = kept_k + kept_r + later
        later = (dxk - kept_k) + (dxr - kept_r)
        add_sums(sums, (dh * n, dh, dxk * diff, dxr * diff))
        dx1 = cp_ref[rows, :].astype(F32) + norm_back(dh * gain, n, rstd)
        dx1_ref[rows, :] = dx1
        out_ref[rows, part(0)] = dx1.astype(BF16)
        if j > 0:
            n, rstd = n_next, rstd_next
    carry[...] = later
    dxk_ref[...] = dot_nt(out_ref[:, part(0)], wo_ref[...])
    for cols in col_chunks():
        retain = jnp.exp(-jnp.exp(vec_ref[9:10, cols]))
        right = slice(EMBED + cols.start, EMBED + cols.stop)
        p = state_p[:, cols]
        q = state_q[:, cols]
        for j in reversed(range(STEPS)):
            rows = step_rows(j)
            gate = sigmoid(r_ref[rows, cols].astype(F32))
            scaled = dxk_ref[rows, cols] * gate
            dwkv = scaled.astype(BF16)
            dwkv_ref[rows, cols] = dwkv
            out_ref[rows, right] = (scaled * wkv_ref[rows, cols].astype(F32) * (1.0 - gate)).astype(BF16)
            grad = dwkv.astype(F32) * den[0, rows, cols]
            p = grad + retain * p
            q = retain * q - grad * den[1, rows, cols]
        state_p[:, cols] = p
        state_q[:, cols] = q

    @pl.when(i == count - 1)
    def _():
        vsum_ref[...] = jnp.zeros_like(vsum_ref)
        for at in range(4):
            vsum_ref[at : at + 1, :] = jnp.sum(sums[at], axis=0, keepdims=True)
        first_ref[:GROUP, :] = state_p[...]
        first_ref[GROUP:, :] = state_q[...]
        rate = -jnp.exp(vec_ref[9:10, :])
        decay = jnp.exp(rate * float(STEPS * count))
        for q in range(2 * GROUP // CHUNKS):
            base = q * CHUNKS
            total = first_ref[base + CHUNKS - 1 : base + CHUNKS, :]
            for s in reversed(range(CHUNKS - 1)):
                total = decay * total + first_ref[base + s : base + s + 1, :]
            for d in range(total_ref.shape[0]):
                total_ref[d, q : q + 1, :] = total


def wkv_back_kernel(weights, ins, outs, scratch, copies, grad):
    (pieces,) = weights
    flag_ref, k_ref, v_ref, dwkv_ref, dr_ref, st_ref, vec_ref, every_ref, first_ref = ins
    out_ref, vsum_ref, edge_ref, send_ref = outs
    past_a, past_b, state_p, state_q, sums, w_ref, sems = scratch
    i = pl.program_id(0)
    count = pl.num_programs(0)
    loads = column_loads((pieces,), w_ref, sems, 0, 0, 3 * EMBED)
    start_loads(loads)

    @pl.when(i == 0)
    def _():
        sums[...] = jnp.zeros_like(sums)
        rate = -jnp.exp(vec_ref[9:10, :])
        decay = jnp.exp(rate * float(STEPS * count))
        devices, four, _ = every_ref.shape
        micro = four // 2
        whole = jnp.exp(rate * float(STEPS * count * CHUNKS))
        for q in range(2 * GROUP // CHUNKS):
            state = jnp.zeros((1, EMBED), F32)
            passed = state
            for d in reversed(range(devices)):
                state = jnp.where(flag_ref[micro] == d, passed, state)
                begins = flag_ref[micro + 1 + d * micro + q % micro]
                passed = jnp.where(begins > 0, 0.0, whole * passed + every_ref[d, q : q + 1, :])
            target = state_p if q < GROUP // CHUNKS else state_q
            base = (q % (GROUP // CHUNKS)) * CHUNKS
            for s in reversed(range(CHUNKS)):
                target[base + s : base + s + 1, :] = state
                state = decay * state + first_ref[q * CHUNKS + s : q * CHUNKS + s + 1, :]

    wait_load(copies)
    grad()
    for cols in col_chunks():
        right = slice(EMBED + cols.start, EMBED + cols.stop)
        retain = jnp.exp(-jnp.exp(vec_ref[9:10, cols]))
        bonus = vec_ref[10:11, cols]
        a = st_ref[0, :GROUP, cols]
        b = st_ref[0, GROUP:, cols]
        for j in range(STEPS):
            rows = step_rows(j)
            weight = jnp.exp(k_ref[rows, cols].astype(F32))
            past_a[rows, cols] = a
            past_b[rows, cols] = b
            a = retain * a + weight * v_ref[rows, cols].astype(F32)
            b = retain * b + weight
        p = state_p[:, cols]
        q = state_q[:, cols]
        sum_decay = sums[0, :, cols]
        sum_bonus = sums[1, :, cols]
        for j in reversed(range(STEPS)):
            rows = step_rows(j)
            key = k_ref[rows, cols].astype(F32)
            value = v_ref[rows, cols].astype(F32)
            own = jnp.exp(bonus + key)
            weight = jnp.exp(key)
            a = past_a[rows, cols]
            b = past_b[rows, cols]
            scale = pl.reciprocal(b + own)
            wkv = (a + own * value) * scale
            grad = dwkv_ref[rows, cols].astype(F32) * scale
            own_grad = grad * own
            bonus_term = own_grad * (value - wkv)
            out_ref[rows, cols] = (bonus_term + weight * (value * p + q)).astype(BF16)
            out_ref[rows, right] = (own_grad + weight * p).astype(BF16)
            sum_decay += a * p + b * q
            sum_bonus += bonus_term
            p = grad + retain * p
            q = retain * q - grad * wkv
        state_p[:, cols] = p
        state_q[:, cols] = q
        sums[0, :, cols] = sum_decay
        sums[1, :, cols] = sum_bonus

    @pl.when(i == count - 1)
    def _():
        rate = -jnp.exp(vec_ref[9:10, :])
        vsum_ref[...] = jnp.zeros_like(vsum_ref)
        vsum_ref[0:1, :] = jnp.sum(sums[0], axis=0, keepdims=True) * jnp.exp(rate) * rate
        vsum_ref[1:2, :] = jnp.sum(sums[1], axis=0, keepdims=True)
        wait_all(loads)
        rows = slice(0, GROUP)
        edge = dot_nt(out_ref[rows, part(0)], w_ref[:, part(0)]) * (1.0 - vec_ref[4:5, :])
        edge += dot_nt(out_ref[rows, part(1)], w_ref[:, part(1)]) * (1.0 - vec_ref[5:6, :])
        edge += dot_nt(dr_ref[rows, :], w_ref[:, part(2)]) * (1.0 - vec_ref[6:7, :])
        edge_ref[...] = edge
        send_rows(flag_ref, edge, send_ref)


def input_back_kernel(lowest, weights, ins, outs, scratch, copies=(), grad=None):
    (pieces,) = weights
    grad_ref, dr_ref, xp_ref, before_ref, edge_ref, later_ref, got_ref, dx1_ref, vec_ref = ins[:9]
    out_ref, vsum_ref, later_out = outs
    carry, w_ref, back, rows_ref, sums, sems = scratch
    i = pl.program_id(0)
    count = pl.num_programs(0)
    loads = column_loads((pieces,), w_ref, sems, 0, 0, 3 * EMBED)
    start_loads(loads)

    @pl.when(i == 0)
    def _():
        if lowest:
            carry[...] = later_ref[...]
        else:
            take_rows(carry, later_ref, got_ref)
        sums[...] = jnp.zeros_like(sums)

    wait_load(loads + list(copies))
    if grad is not None:
        grad()
    for at, grads in enumerate((grad_ref[:, part(0)], grad_ref[:, part(1)], dr_ref[...])):
        back[at] = dot_nt(grads, w_ref[:, part(at)])
    gain = vec_ref[0:1, :]
    offset = vec_ref[1:2, :]
    n, rstd = normalize(xp_ref[step_rows(STEPS - 1), :].astype(F32))
    later = carry[...]
    for j in reversed(range(STEPS)):
        rows = step_rows(j)
        if j > 0:
            n_next, rstd_next = normalize(xp_ref[step_rows(j - 1), :].astype(F32))
            h_before = n_next * gain + offset
        else:
            n_before, _ = normalize(before_ref[...].astype(F32))
            h_before = n_before * gain + offset
            if lowest:
                h_before = jnp.where(i == count - 1, edge_ref[...], h_before)
        diff = n * gain + offset - h_before
        dh = later
        later = None
        for at in range(3):
            grad = back[at, rows, :]
            kept = grad * vec_ref[4 + at : 5 + at, :]
            sums[2 + at] += grad * diff
            dh = dh + kept
            passed = grad - kept
            later = passed if later is None else later + passed
        sums[0] += dh * n
        sums[1] += dh
        rows_ref[rows, :] = (dx1_ref[rows, :] + norm_back(dh * gain, n, rstd)).astype(BF16)
        if j > 0:
            n, rstd = n_next, rstd_next
    carry[...] = later
    later_out[...] = later
    out_ref[...] = swap_out(rows_ref[...])

    @pl.when(i == count - 1)
    def _():
        vsum_ref[...] = jnp.zeros_like(vsum_ref)
        for at in range(5):
            vsum_ref[at : at + 1, :] = jnp.sum(sums[at], axis=0, keepdims=True)
        if lowest:
            vsum_ref[...] += ins[10][...]


def adam_step(master, moment, second, gradient, rate, shrink):
    moment_new = 0.9 * moment + 0.1 * gradient
    second_new = 0.95 * second + 0.05 * gradient * gradient
    scaled = moment_new / (1.0 - 0.9**STEP) / (jnp.sqrt(second_new / (1.0 - 0.95**STEP)) + 1e-08)
    return (master - rate * (scaled + shrink * master), moment_new, second_new)


def neighbour(block, axis, distance):
    devices = range(lax.axis_size(axis))
    return lax.ppermute(block, axis, [(i, i + distance) for i in devices if i + distance in devices])


def everyone(block, axis):
    count = lax.axis_size(axis)
    return lax.all_to_all(
        jnp.broadcast_to(block[None], (count,) + block.shape), axis, 0, 0, tiled=True
    )


def scatter_rows(grad):
    part = lax.psum_scatter(grad.astype(BF16), "tok", scatter_dimension=0, tiled=True)
    return lax.psum_scatter(part, "rep", scatter_dimension=0, tiled=True).astype(F32)


def weight_grad(a, b):
    return dot_tn(a, b).astype(BF16)


def flip(block, axis, bit):
    return lax.ppermute(block, axis, [(i, i ^ bit) for i in range(lax.axis_size(axis))])


def place_all_kernel(bits_ref, own, far, near, both, out):
    height = own.shape[0]
    for source, high, low in (
        (own, bits_ref[4], bits_ref[3]), (far, 1 - bits_ref[4], bits_ref[3]),
        (near, bits_ref[4], 1 - bits_ref[3]), (both, 1 - bits_ref[4], 1 - bits_ref[3]),
    ):
        out[pl.ds(pl.multiple_of((2 * high + low) * height, height), height), :] = source[...]


def place(kernel, bits, inputs, shapes, name, after=()):
    vmem = pl.BlockSpec(memory_space=pltpu.VMEM)
    return pl.pallas_call(
        ordered(kernel, 0, len(after)),
        in_specs=[ANY_SPEC] * len(after) + [SMEM_SPEC] + [vmem] * len(inputs),
        out_specs=[vmem] * len(shapes),
        out_shape=[jax.ShapeDtypeStruct(shape, BF16) for shape in shapes],
        compiler_params=pltpu.CompilerParams(vmem_limit_bytes=VMEM.get(name, 16) * MIB),
        cost_estimate=cost(name),
        name=name,
    )(*after, bits, *inputs)


def cast_kernel(source, target):
    target[...] = source[...].astype(BF16)


def cast(shard, after, name):
    block = pl.BlockSpec(shard.shape, lambda i: (0, 0))
    return call(
        cast_kernel, 1, [block], block, jax.ShapeDtypeStruct(shard.shape, BF16), [], name, after
    )(shard)


def gather_plain(shard):
    return [lax.all_gather(lax.all_gather(shard, "rep", axis=0, tiled=True), "tok", axis=0, tiled=True)]


def rep_rows(shard):
    far = flip(shard, "rep", 2)
    return shard, far, flip(shard, "rep", 1), flip(far, "rep", 1)


def gather_rep(shard, bits, name, after=()):
    height, width = shard.shape
    return place(place_all_kernel, bits, rep_rows(shard), [(4 * height, width)], name + "_rep", after)[0]


def held(array, after, name):
    return pl.pallas_call(
        lambda *refs: None,
        in_specs=[ANY_SPEC] * (1 + len(after)),
        out_specs=ANY_SPEC,
        out_shape=jax.ShapeDtypeStruct(array.shape, array.dtype),
        input_output_aliases={0: 0},
        cost_estimate=cost(name),
        name=name,
    )(array, *after)


SLOTS = ((0, 0), (0, 1), (1, 0), (1, 1))


def store_slot(outs, slot, value, left):
    dy, dx = SLOTS[slot]
    if left:
        outs[dx][dy] = value
    else:
        outs[2 + dy][dx] = value


def beside(main, counts, pairs, takes, bits_ref, *refs):
    lists, lhs_count = [], 2 * len(pairs)
    for count in (counts[0], counts[1], lhs_count, 2 * len(takes), counts[2], 4, counts[3], 3):
        lists.append(refs[:count])
        refs = refs[count:]
    weights, ins, lhs_refs, rhs_refs, outs, grads, scratch, (lhs, made, sems) = lists
    i = pl.program_id(0)
    steps = pl.num_programs(0)
    height = EMBED // 8
    copies = []
    for at, base in enumerate(pairs):
        for which in range(2):
            for slot, (dy, dx) in enumerate(SLOTS):
                block = base + 4 * (bits_ref[2] ^ dy) + 2 * (bits_ref[1] ^ dx) + bits_ref[0]
                cols = pl.ds(pl.multiple_of(block * height, height), height)
                copies.append(
                    pltpu.make_async_copy(
                        lhs_refs[2 * at + which].at[:, cols],
                        lhs.at[2 * at + which, :, slot * height : (slot + 1) * height],
                        sems.at[len(copies)],
                    )
                )
    start_loads(copies)

    def grad():
        column = 0
        for at, (width, of_step) in enumerate(takes):
            pair = of_step[0] if len(set(of_step)) == 1 else i * len(pairs) // steps
            total = dot_tn(lhs[2 * pair], rhs_refs[2 * at][...]) + dot_tn(lhs[2 * pair + 1], rhs_refs[2 * at + 1][...])
            made[:, column : column + width] = total.astype(BF16)
            column += width

    main(weights, ins, outs, scratch, copies, grad)
    for left in (True, False):

        @pl.when((i < steps // 2) == left)
        def _(left=left):
            for slot in range(4):
                store_slot(grads, slot, made[slot * height : (slot + 1) * height, :], left)


def alone(main, counts, bits_ref, *refs):
    lists = []
    for count in counts:
        lists.append(refs[:count])
        refs = refs[count:]
    main(*lists, [], lambda: None)


def call_main(
    kernel, grid, ins, in_specs, out_specs, out_shape, scratch, name, after, bits, weights, lhs=(), takes=(),
    rhs=(), aliases=None,
):
    counts = (len(weights), len(in_specs), len(out_specs), len(scratch))
    if lhs:
        rows = rhs[0].shape[0]
        height = EMBED // 8
        lhs_args = [array for own, other, _ in lhs for array in (own, other)]
        rhs_specs, rhs_args = [], []
        for width, base, _ in takes:
            rhs_specs += [pl.BlockSpec((rows, width), lambda i, base=base: (0, base + i))] * 2
            rhs_args += rhs
        total = sum(width for width, _, _ in takes)
        left = pl.BlockSpec((2, height, total), lambda i: (0, 0, jnp.minimum(i, grid // 2 - 1)))
        right = pl.BlockSpec((2, height, total), lambda i: (0, 0, jnp.maximum(i - grid // 2, 0)))
        body = functools.partial(
            beside, kernel, counts, [base for _, _, base in lhs], [(width, pair) for width, _, pair in takes]
        )
        in_specs = in_specs + [ANY_SPEC] * len(lhs_args) + rhs_specs
        out_specs = out_specs + [left, left, right, right]
        out_shape = out_shape + [jax.ShapeDtypeStruct((2, height, total * grid // 2), BF16)] * 4
        scratch = scratch + [
            pltpu.VMEM((2 * len(lhs), rows, 4 * height), BF16), pltpu.VMEM((4 * height, total), BF16),
            pltpu.SemaphoreType.DMA((8 * len(lhs),)),
        ]
        ins = (*ins, *lhs_args, *rhs_args)
    else:
        body = functools.partial(alone, kernel, counts)
    heads = len(weights)

    def run(bits_ref, *refs):
        body(bits_ref, *[group[0] for group in refs[:heads]], *refs[heads:])

    results = call(
        run, grid, in_specs, out_specs, out_shape, scratch, name, after, bits, weights, aliases
    )(*ins)
    return results[: counts[2]], results[counts[2] :]


def grad_only(weights, ins, outs, scratch, copies, grad):
    wait_load(copies)
    grad()


def tall_kernel(bits_ref, lhs_own, lhs_other, rhs_own, rhs_other, *outs):
    i = pl.program_id(0)
    total = dot_tn(lhs_own[...], rhs_own[...]) + dot_tn(lhs_other[...], rhs_other[...])
    total = total.astype(BF16)
    half = total.shape[1] // 2
    for at, (left, right) in enumerate(((0, 2), (0, 3), (1, 2), (1, 3))):

        @pl.when(i == at)
        def _(left=left, right=right):
            outs[left][0] = total[:, :half]
            outs[right][0] = total[:, half:]


def core_grad(bits, lhs, rhs, name, after=()):
    rows, height, width = rhs[0].shape[0], lhs[0].shape[1] // 8, rhs[0].shape[1] // 2

    def column(i, b):
        return (0, 4 * (b[2] ^ (i % 2)) + 2 * (b[1] ^ (i // 2)) + b[0])

    spec = pl.BlockSpec((rows, height), column)
    whole = pl.BlockSpec((rows, 2 * width), lambda i, b: (0, 0))
    return pl.pallas_call(
        ordered(tall_kernel, 1, len(after)),
        grid_spec=pltpu.PrefetchScalarGridSpec(
            num_scalar_prefetch=1,
            grid=(4,),
            in_specs=[ANY_SPEC] * len(after) + [spec, spec, whole, whole],
            out_specs=[
                pl.BlockSpec((1, height, width), lambda i, b: (jnp.minimum(i, 1), 0, 0)),
                pl.BlockSpec((1, height, width), lambda i, b: (jnp.maximum(i - 2, 0), 0, 0)),
                pl.BlockSpec((1, height, width), lambda i, b: (i // 2, 0, 0)),
                pl.BlockSpec((1, height, width), lambda i, b: (i // 2, 0, 0)),
            ],
        ),
        out_shape=[jax.ShapeDtypeStruct((2, height, width), BF16)] * 4,
        compiler_params=pltpu.CompilerParams(
            dimension_semantics=("arbitrary",), vmem_limit_bytes=VMEM.get(name, 16) * MIB
        ),
        cost_estimate=cost(name),
        name=name,
    )(bits, *after, *lhs, *rhs)


def add_kernel(count, bits_ref, *refs):
    for at in range(count):
        total = refs[2 * at][...].astype(F32) + refs[2 * at + 1][...].astype(F32)
        refs[2 * count + at][...] = total.astype(BF16)


def add_split(bits, grid, sums, name, after=()):
    in_specs, out_specs, shapes, args = [], [], [], []
    for a, b, block, source, shape, target in sums:
        in_specs += [pl.BlockSpec(block, source)] * 2
        args += [a, b]
        out_specs.append(pl.BlockSpec(block, target))
        shapes.append(jax.ShapeDtypeStruct(shape, BF16))
    return pl.pallas_call(
        ordered(functools.partial(add_kernel, len(sums)), 1, len(after)),
        grid_spec=pltpu.PrefetchScalarGridSpec(
            num_scalar_prefetch=1, grid=grid, in_specs=[ANY_SPEC] * len(after) + in_specs, out_specs=out_specs
        ),
        out_shape=shapes,
        compiler_params=pltpu.CompilerParams(vmem_limit_bytes=VMEM.get(name, 16) * MIB),
        cost_estimate=cost(name),
        name=name,
    )(bits, *after, *args)


def merge_kernel(moves, bits_ref, p_keep, p_got, q_keep, q_got, *outs):
    p = (p_keep[...].astype(F32) + p_got[...].astype(F32)).astype(BF16)
    q = (q_keep[...].astype(F32) + q_got[...].astype(F32)).astype(BF16)
    half = p.shape[-1]
    if len(outs) == 1:
        for side, start, width, column in moves or ((0, 0, half, 0), (1, 0, q.shape[-1], half)):
            outs[0][:, column : column + width] = (p, q)[side][0, :, start : start + width]
        return
    height = p.shape[1] // 2
    moves = moves or ((0, 0, half, 0), (1, 0, q.shape[-1], half))
    for out, low in ((outs[0], 1 - bits_ref[3]), (outs[1], bits_ref[3])):
        for at in range(2):

            @pl.when(low == at)
            def _(out=out, at=at):
                rows = slice(at * height, (at + 1) * height)
                for side, start, width, column in moves:
                    out[0, :, column : column + width] = (p, q)[side][0, rows, start : start + width]


def merge(bits, p_keep, p_got, q_keep, q_got, shapes, name, after, moves=()):
    _, block, p_width = p_keep.shape
    q_width = q_keep.shape[2]
    in_specs = [
        pl.BlockSpec((1, block // 2, width), lambda h, b: (0, h, 0))
        for width in (p_width, p_width, q_width, q_width)
    ]
    if len(shapes) == 1:
        out_specs = [pl.BlockSpec((block // 2, p_width + q_width), lambda h, b: (h, 0))]
    else:
        out_specs = [pl.BlockSpec((1,) + shapes[0][1:], lambda h, b: (h, 0, 0))] * 2
    return pl.pallas_call(
        ordered(functools.partial(merge_kernel, moves), 1, len(after)),
        grid_spec=pltpu.PrefetchScalarGridSpec(
            num_scalar_prefetch=1, grid=(2,), in_specs=[ANY_SPEC] * len(after) + in_specs, out_specs=out_specs
        ),
        out_shape=[jax.ShapeDtypeStruct(shape, BF16) for shape in shapes],
        compiler_params=pltpu.CompilerParams(vmem_limit_bytes=VMEM.get(name, 16) * MIB),
        cost_estimate=cost(name),
        name=name,
    )(bits, *after, p_keep, p_got, q_keep, q_got)


def reduce_grad(bits, made, offload, name, moves=()):
    p_keep, p_send, q_keep, q_send = made
    p_got, q_got = flip(p_send, "tok", 2), flip(q_send, "tok", 4)
    after = yield p_keep
    _, block, p_width = p_keep.shape
    q_width = q_keep.shape[2]
    half = block // 2
    sums = []
    for which in (1, 0):
        for keep, got, width in ((p_keep, p_got, p_width), (q_keep, q_got, q_width)):
            sums.append((
                keep, got, (1, half, width), lambda r, b, which=which: (which, r, 0),
                (1, block, width), lambda r, b: (0, r, 0),
            ))
    p_send, q_send, p_keep, q_keep = add_split(bits, (2,), sums, name + "_add_first", after)
    p_got, q_got = flip(p_send, "tok", 4), flip(q_send, "tok", 2)
    after = yield p_keep
    width = p_width + q_width
    if offload:
        (total,) = merge(bits, p_keep, p_got, q_keep, q_got, [(block, width)], name + "_merge", after, moves)
        yield total
        part = lax.psum_scatter(total, "rep", scatter_dimension=0, tiled=True)
        after = yield part
        yield held(part, after, name + "_hold").astype(F32)
        return
    shape = (2, block // 4, width)
    send, keep = merge(bits, p_keep, p_got, q_keep, q_got, [shape] * 2, name + "_merge", after, moves)
    got = flip(send, "rep", 1)
    after = yield keep
    sums = [
        (keep, got, (1,) + shape[1:], lambda i, b, f=f: (b[4] ^ f, 0, 0), (1,) + shape[1:], lambda i, b: (0, 0, 0))
        for f in (1, 0)
    ]
    send, keep = add_split(bits, (1,), sums, name + "_add_low", after)
    got = flip(send, "rep", 2)
    yield keep
    after = yield got
    if after:
        got = held(got, after, name + "_hold")
    yield (keep.astype(F32) + got.astype(F32))[0]


def reduce_plain(lhs, rhs):
    sums, column = [], 0
    for array, _, base, tiles in lhs:
        if array.shape[1] > EMBED and array.shape[1] != FF:
            array = array[:, base * EMBED // 8 : base * EMBED // 8 + EMBED]
        sums.append(scatter_rows(weight_grad(array, rhs[0][:, part(column, tiles)])))
        column += tiles
    total = jnp.concatenate(sums, axis=1)
    for _ in range(5):
        yield total[:8]
    yield total


def advance(work, *after):
    return work.send(tuple(after))


def on_device(
    tokens, cotangent, init_num, init_den, prev_att, seg_doc, w_kvr, w_out, f_kr, f_value, vectors,
    m_kvr, v_kvr, m_out, v_out, m_fkr, v_fkr, m_fvalue, v_fvalue, vec_m, vec_v,
):
    tok_count = lax.axis_size("tok")
    rep_count = lax.axis_size("rep")
    here = lax.axis_index("tok")
    flat_index = here * rep_count + lax.axis_index("rep")
    micro, _, local_len, _ = tokens.shape
    seg_count = seg_doc.shape[2]
    chunk = local_len // CHUNKS
    blocks = chunk // STEPS
    rows = micro * local_len

    rep_index = lax.axis_index("rep")
    bits = jnp.stack([here & 1, (here >> 1) & 1, (here >> 2) & 1, rep_index & 1, (rep_index >> 1) & 1])
    bits = bits.astype(jnp.int32)
    paired = tok_count == 8 and rep_count == 4
    att_shard = jnp.concatenate([w_kvr, w_out], axis=1).astype(BF16)
    before_mix = before_wkv = before_hidden = ()
    if paired:
        half_cols = EMBED // 2
        value_left, value_raw = f_value[:, :half_cols].astype(BF16), f_value[:, half_cols:].astype(BF16)
        att_part = gather_rep(att_shard, bits, "place_att")
        att_w = [lax.all_gather(att_part, "tok", axis=0, tiled=True)]
        hidden_part = gather_rep(cast(f_kr, (att_part,), "cast_hidden"), bits, "place_hidden")
        fkr = [lax.all_gather(hidden_part, "tok", axis=0, tiled=True)]
        value_rows = lax.all_gather(value_raw, "tok", axis=0, tiled=True)
        value_part = gather_rep(value_left, bits, "place_value", (hidden_part,))
        fvalue = [lax.all_gather(value_part, "tok", axis=0, tiled=True)]
        value_rows = held(value_rows, (value_part,), "hold_value")
        value_far = flip(value_rows, "rep", 2)
        value_near = flip(value_rows, "rep", 1)
        value_others = [value_rows, value_far, value_near, flip(value_far, "rep", 1)]
        before_mix = (value_rows,)
        before_wkv = (value_far, value_near)
    else:
        value_others = []
        att_w, fkr, fvalue = gather_plain(att_shard), gather_plain(f_kr.astype(BF16)), gather_plain(f_value.astype(BF16))

    def other_core(array):
        return flip(array, "tok", 1) if paired else None

    documents = seg_doc[:, 0, :]
    marker = jnp.concatenate(
        [jnp.ones((micro, 1), jnp.bool_), documents[:, 1:] != documents[:, :-1]], axis=1
    )
    starts = jnp.arange(tok_count) * local_len
    fresh = jnp.logical_and(marker[:, starts // SEG_LEN], (starts % SEG_LEN == 0)[None, :])
    fresh_here = lax.dynamic_index_in_dim(fresh, here, 1, keepdims=True)
    seg_here = here * local_len // SEG_LEN
    prev_here = lax.dynamic_index_in_dim(prev_att[:, 0], seg_here, 1, keepdims=False).astype(F32)
    init_all = everyone(jnp.concatenate([init_num[:, 0], init_den[:, 0]], axis=0), "tok")
    init_all = jnp.moveaxis(init_all, 0, 2).reshape(2 * micro, seg_count, EMBED)
    rate = -jnp.exp(vectors[9:10])
    fade = jnp.exp(rate * float(local_len))
    fresh_four = jnp.concatenate([fresh, fresh], axis=0)
    flags = jnp.concatenate(
        [fresh_here[:, 0].astype(jnp.int32), jnp.reshape(here, (1,)).astype(jnp.int32),
         jnp.moveaxis(fresh, 1, 0).reshape(-1).astype(jnp.int32)]
    )

    x4 = tokens.reshape(micro, CHUNKS, chunk, EMBED)
    c4 = cotangent.reshape(micro, CHUNKS, chunk, EMBED)

    def edge_back(last, incoming):
        moved = jnp.concatenate([incoming[:, None], last.reshape(micro, CHUNKS, EMBED)[:, :-1]], axis=1)
        return moved.reshape(GROUP, EMBED)

    raw_in = neighbour(tokens[:, 0, -1, :], "tok", 1)
    raw_edge = edge_back(x4[:, :, -1, :], raw_in).astype(F32)
    edge_n, _ = normalize(raw_edge)
    edge_h = edge_n * vectors[0:1] + vectors[1:2]
    first_row = (jnp.arange(GROUP) % CHUNKS == 0)[:, None]
    fresh_rows = jnp.repeat(fresh_here[:, 0], CHUNKS)[:, None]
    replace = jnp.logical_and(first_row, fresh_rows)
    edge_one = jnp.where(replace, jnp.repeat(prev_here, CHUNKS, axis=0), edge_h)

    def up(width):
        return pl.BlockSpec((ROWS, width), lambda i: (i, 0))

    def down(width):
        return pl.BlockSpec((ROWS, width), lambda i: (blocks - 1 - i, 0))

    before_spec = pl.BlockSpec(
        (GROUP, EMBED), lambda i: (jnp.maximum((blocks - 1 - i) * STEPS - 1, 0), 0)
    )
    natural_up = pl.BlockSpec((micro, CHUNKS, STEPS, EMBED), lambda i: (0, 0, i, 0))
    natural_down = pl.BlockSpec((micro, CHUNKS, STEPS, EMBED), lambda i: (0, 0, blocks - 1 - i, 0))
    st_up = pl.BlockSpec((1, 2 * GROUP, EMBED), lambda i: (i, 0, 0))
    st_down = pl.BlockSpec((1, 2 * GROUP, EMBED), lambda i: (blocks - 1 - i, 0, 0))
    vec_spec = full(vectors.shape)
    edge_spec = full((GROUP, EMBED))
    state_spec = full((2 * GROUP, EMBED))
    total_spec = full((2 * micro, EMBED))
    sum_spec = full((8, EMBED))

    def like(width, dtype):
        return jax.ShapeDtypeStruct((rows, width), dtype)

    def small(count, dtype=F32):
        return jax.ShapeDtypeStruct((count, EMBED), dtype)

    def weight(height, width):
        return pltpu.VMEM((height, width), BF16)

    sems = pltpu.SemaphoreType.DMA((80,))
    state = pltpu.VMEM((GROUP, EMBED), F32)
    square = 2 * rows * EMBED * EMBED

    xp, mix, k, v, r, ends, totals = call(
        mix_one_kernel, blocks,
        [natural_up, edge_spec, vec_spec],
        [up(EMBED), up(3 * EMBED)] + [up(EMBED)] * 3 + [state_spec, total_spec],
        [like(EMBED, BF16), like(3 * EMBED, BF16), like(EMBED, BF16), like(EMBED, BF16), like(EMBED, BF16),
         small(2 * GROUP), small(2 * micro)],
        [state] * 3 + [weight(EMBED, 3 * EMBED), sems], "mix_one", before_mix, bits, (att_w,),
    )(x4, edge_one, vectors)

    every = everyone(totals, "tok")
    carried = jnp.zeros((2 * micro, EMBED), F32)
    begin = jnp.zeros((2 * micro, EMBED), F32)
    for d in range(tok_count):
        seg = d * local_len // SEG_LEN
        carried = jnp.where(fresh_four[:, d : d + 1], init_all[:, seg], carried)
        begin = jnp.where(here == d, carried, begin)
        carried = fade * carried + every[d]

    wkv, y, x1, mix_two, saved, first_two, last_two = call(
        wkv_kernel, blocks,
        [up(EMBED)] * 4 + [vec_spec, total_spec, state_spec],
        [up(EMBED)] * 3 + [up(2 * EMBED), st_up, edge_spec, edge_spec],
        [like(EMBED, BF16), like(EMBED, BF16), like(EMBED, F32), like(2 * EMBED, BF16),
         jax.ShapeDtypeStruct((blocks, 2 * GROUP, EMBED), F32), small(GROUP), small(GROUP)],
        [state] * 3 + [weight(EMBED, EMBED), sems], "wkv", before_wkv, bits, (att_w,),
    )(k, v, r, xp, vectors, begin, ends)

    if paired:
        mix = held(mix, (last_two,), "hold_mix")
    row_in = neighbour(last_two.reshape(micro, CHUNKS, EMBED)[:, -1], "tok", 1)
    edge_two = jnp.where(replace, 0.0, edge_back(last_two, row_in))
    diff_two = first_two - edge_two
    fixed = jnp.concatenate([edge_two + diff_two * vectors[7:8], edge_two + diff_two * vectors[8:9]], axis=1)
    mix_two = lax.dynamic_update_slice(mix_two, fixed.astype(BF16), (0, 0))

    kq, gate = call(
        hidden_kernel, blocks,
        [up(2 * EMBED)],
        [up(FF), up(EMBED)],
        [like(FF, BF16), like(EMBED, BF16)],
        [weight(EMBED, FF + EMBED), sems], "hidden", before_hidden, bits, (fkr,),
    )(mix_two)
    kq_other, mix_two_other, y_other, mix_other = [other_core(array) for array in (kq, mix_two, y, mix)]

    known = (mix_two_other, y_other, mix_other) if paired else ()
    mixed, dvf, dkf, cp = call(
        value_kernel, blocks,
        [up(FF), up(EMBED), up(EMBED), natural_up],
        [natural_up, up(EMBED), up(FF + EMBED), up(EMBED)],
        [jax.ShapeDtypeStruct(x4.shape, BF16), like(EMBED, BF16), like(FF + EMBED, BF16),
         like(EMBED, BF16)],
        [weight(FF, EMBED), pltpu.VMEM((ROWS, EMBED), F32), weight(ROWS, EMBED), sems],
        "value", known, bits, (fvalue, value_others),
    )(kq, gate, x1, c4)
    row_spec = full((micro, EMBED))
    shift_two, send_two = call(
        edge_kernel, 1,
        [SMEM_SPEC, pl.BlockSpec((GROUP, FF + EMBED), lambda i: (0, 0)), vec_spec], [edge_spec, row_spec],
        [small(GROUP), small(micro)],
        [weight(EMBED, FF + EMBED), sems], "edge", (), bits, (fkr,),
    )(flags, dkf, vectors)

    got_two = neighbour(send_two, "tok", -1)

    def reduced(made, plain, offload, name, moves=()):
        work = reduce_grad(bits, made, offload, name, moves) if paired else reduce_plain(*plain)
        next(work)
        return work

    def fused(kernel, grid, ins, in_specs, out_specs, out_shape, scratch, name, after, weights, lhs, takes, rhs,
              aliases=None):
        if not paired:
            lhs = takes = rhs = ()
        return call_main(
            kernel, grid, ins, in_specs, out_specs, out_shape, scratch, name, after, bits, weights, lhs, takes,
            rhs, aliases,
        )

    wide, narrow = FF // blocks, EMBED // blocks
    dvf_other = other_core(dvf)
    if paired:
        dkf = held(dkf, (dvf_other, shift_two), "hold_dkf")
    dkf_other = other_core(dkf)
    made = core_grad(bits, (kq, kq_other), (dvf, dvf_other), "grad_value", (shift_two, got_two)) if paired else (shift_two,)
    value_sum = reduced(made, ([(kq, None, 0, 1)], (dvf, None)), True, "grad_value")

    every_spec = full((tok_count, 2 * micro, EMBED))
    _, grads = fused(
        grad_only, blocks, (vectors,), [vec_spec], [], [], [], "grad_hidden", (made[0],), (),
        [(mix_two, mix_two_other, 0), (mix_two, mix_two_other, 8)],
        [(wide, 0, (0,) * blocks), (narrow, FF // narrow, (1,) * blocks)], (dkf, dkf_other),
    ) if paired else (None, made)
    hidden_sum = reduced(
        grads, ([(mix_two, None, 0, 4), (mix_two, None, 8, 1)], (dkf, None)), False, "grad_hidden",
        [(at // (blocks // 2), at % (blocks // 2) * (wide + narrow), wide, at * wide) for at in range(blocks)]
        + [(at // (blocks // 2), at % (blocks // 2) * (wide + narrow) + wide, narrow, FF + at * narrow)
           for at in range(blocks)],
    )
    made = grads
    (dx1, datt, dwkv, vsum_two, firsts, back_totals), grads = fused(
        middle_back_kernel, blocks,
        (dkf, x1, x1, edge_two, shift_two, got_two, cp, vectors, k, v, r, wkv, saved),
        [down(FF + EMBED), down(EMBED), before_spec, edge_spec,
         edge_spec, row_spec, down(EMBED), vec_spec] + [down(EMBED)] * 4 + [st_down],
        [down(EMBED), down(2 * EMBED), down(EMBED)] + [sum_spec, state_spec, every_spec],
        [like(EMBED, F32), like(2 * EMBED, BF16), like(EMBED, BF16), small(8),
         small(2 * GROUP), jax.ShapeDtypeStruct((tok_count, 2 * micro, EMBED), F32)],
        [state, pltpu.VMEM((2, ROWS, EMBED), F32), state, state, weight(EMBED, FF + EMBED),
         weight(EMBED, EMBED), pltpu.VMEM((ROWS, EMBED), F32), pltpu.VMEM((ROWS, EMBED), F32),
         pltpu.VMEM((4, GROUP, EMBED), F32), sems],
        "middle_back", (made[0],), (fkr, att_w), (), (), (),
    )
    every_back = lax.all_to_all(back_totals, "tok", 0, 0, tiled=True)
    made = advance(value_sum, firsts)
    made = advance(hidden_sum, made)
    datt_other = other_core(datt)
    right_down = pl.BlockSpec((ROWS, EMBED), lambda i: (blocks - 1 - i, 1))
    (dkv, vsum_wkv, shift_one, send_one), grads = fused(
        wkv_back_kernel, blocks,
        (flags, k, v, dwkv, datt, saved, vectors, every_back, firsts),
        [SMEM_SPEC] + [down(EMBED)] * 3 + [right_down, st_down, vec_spec, every_spec, state_spec],
        [down(2 * EMBED), sum_spec, edge_spec, row_spec],
        [like(2 * EMBED, BF16), small(8), small(GROUP), small(micro)],
        [pltpu.VMEM((ROWS, EMBED), F32)] * 2 + [state] * 2
        + [pltpu.VMEM((2, GROUP, EMBED), F32), weight(EMBED, 3 * EMBED), sems],
        "wkv_back", (made,), (att_w,),
        [(y, y_other, 0), (mix, mix_other, 16)], [(2 * EMBED // blocks, 0, (0, 0, 1, 1))], (datt, datt_other),
    )
    early_sum = reduced(grads, ([(y, None, 0, 1), (mix, None, 16, 1)], (datt, None)), False, "grad_early")
    dkv_other = other_core(dkv)

    got_one = neighbour(send_one, "tok", -1)
    made = advance(value_sum, dkv)
    value_part = advance(value_sum)
    made = advance(hidden_sum, made)

    half = blocks // 2

    def input_back(high, before, later_rows, started):
        def at(width, column=0):
            return pl.BlockSpec((ROWS, width), lambda i: (high - i, column))

        before_block = pl.BlockSpec((GROUP, EMBED), lambda i: (jnp.maximum((high - i) * STEPS - 1, 0), 0))
        natural = pl.BlockSpec((micro, CHUNKS, STEPS, EMBED), lambda i: (0, 0, high - i, 0))
        return fused(
            functools.partial(input_back_kernel, bool(started)), half,
            (dkv, datt, xp, xp, edge_one, later_rows, got_one, dx1, vectors, *started),
            [at(2 * EMBED), at(EMBED, 1), at(EMBED), before_block, edge_spec, edge_spec, row_spec, at(EMBED), vec_spec]
            + [ANY_SPEC, sum_spec][: len(started)],
            [natural, sum_spec, edge_spec],
            [jax.ShapeDtypeStruct(x4.shape, BF16), small(8), small(GROUP)],
            [state, weight(EMBED, 3 * EMBED), pltpu.VMEM((3, ROWS, EMBED), F32), weight(ROWS, EMBED),
             pltpu.VMEM((5, GROUP, EMBED), F32), sems],
            "input_back_low" if started else "input_back_high", before, (att_w,),
            () if started else [(mix, mix_other, 0), (mix, mix_other, 8)], [(EMBED, 0, (0, 1))], (dkv, dkv_other),
            {len(before) + 1 + len(att_w) + 9: 0} if started else None,
        )

    (token_high, vsum_high, later_half), grads = input_back(blocks - 1, (made,), shift_one, ())
    late_sum = reduced(grads, ([(mix, None, 0, 1), (mix, None, 8, 1)], (dkv, None)), False, "grad_late")
    made = advance(early_sum, vsum_high)
    made = advance(hidden_sum, made)
    hidden_got = advance(hidden_sum)
    (token_grad, vsum_one, _), _ = input_back(half - 1, (made, value_part), later_half, (token_high, vsum_high))

    made = advance(late_sum, vsum_one)
    made = advance(early_sum, made)
    made = advance(late_sum, made, hidden_got)
    columns = vec_m.shape[1]
    grad_vec = held(jnp.concatenate([vsum_one, vsum_two, vsum_wkv], axis=0), (made,), "hold_vec")
    pieces = jnp.moveaxis(grad_vec.reshape(grad_vec.shape[0], tok_count * rep_count, columns), 1, 0)
    vec_terms = lax.all_to_all(pieces, ("tok", "rep"), 0, 0, tiled=True)
    made = advance(early_sum, made)
    advance(early_sum)
    made = advance(late_sum, made)
    advance(late_sum)
    if not paired:
        advance(value_sum)
    sum_fvalue = advance(value_sum, made)
    sum_fkr = advance(hidden_sum, made)
    sum_early = advance(early_sum, made)
    sum_late = advance(late_sum)
    sums = jnp.sum(held(vec_terms, (made,), "hold_terms"), axis=0)
    sum_vec = jnp.concatenate([sums[0:2], sums[8:10], sums[2:5], sums[10:12], sums[16:18]], axis=0)
    sum_out = sum_early[:, :EMBED]
    sum_kvr = jnp.concatenate([sum_late, sum_early[:, EMBED:]], axis=1)

    base_rate = 2.5 / math.sqrt(EMBED)
    new_kvr = adam_step(w_kvr, m_kvr, v_kvr, sum_kvr, base_rate, 0.01)
    new_out = adam_step(w_out, m_out, v_out, sum_out, 4.0 * base_rate, 0.01)
    new_fkr = adam_step(f_kr, m_fkr, v_fkr, sum_fkr, base_rate, 0.01)
    new_fvalue = adam_step(f_value, m_fvalue, v_fvalue, sum_fvalue, 2.5 / math.sqrt(FF), 0.01)
    vec_master = lax.dynamic_slice_in_dim(vectors, flat_index * columns, columns, 1)
    vec_rates = jnp.array([0.6, 0.3, 0.6, 0.3, 0.3, 0.3, 0.3, 0.3, 0.3, 3.0, 0.5], F32)[:, None]
    new_vectors = adam_step(vec_master, vec_m, vec_v, sum_vec, vec_rates, 0.0)
    shape = tokens.shape
    return (
        (mixed.reshape(shape), token_grad.reshape(shape))
        + new_kvr + new_out + new_fkr + new_fvalue + new_vectors
    )


def solution(mesh):
    rows = P(("tok", "rep"), None)
    columns = P(None, ("tok", "rep"))
    token_spec = P(None, "rep", "tok", None)
    channel_spec = P(None, "rep", None, "tok")
    placed = (
        (token_spec, token_spec, channel_spec, channel_spec, P(None, "rep", None, None), P(None, "rep", None))
        + (rows,) * 4 + (P(),) + (rows,) * 8 + (columns,) * 2
    )
    return jax.shard_map(
        on_device,
        mesh=mesh,
        in_specs=placed,
        out_specs=(token_spec, token_spec) + (rows,) * 12 + (columns,) * 3,
        check_vma=False,
    )
```

```python
import functools
import math

import jax
import jax.numpy as jnp
from jax import lax
from jax.experimental import pallas as pl
from jax.experimental.pallas import tpu as pltpu
from jax.sharding import PartitionSpec as P

EMBED = 1024
FF = 4096
SEG_LEN = 2048
STEP = 10
CHUNKS = 8
GROUP = 16
STEPS = 16
ROWS = STEPS * GROUP
COLS = 256
EPS = 1e-05
TINY = 1.2e-38
COSTS = dict(
    value=60, edge=14, grad_value=30, grad_hidden=40, grad_value_add_first=8, grad_hidden_add_first=100, wkv_back=24,
    grad_value_merge=50, grad_hidden_merge=50, input_back_high=24,
)
F32 = jnp.float32
BF16 = jnp.bfloat16
MIB = 1024 * 1024
VMEM = dict(
    mix_one=30, wkv=28, hidden=36, value=60, edge=60, grad_value=60, middle_back=60, wkv_back=60, input_back_high=44,
    input_back_low=60, grad_hidden_merge=60, grad_value_add_first=60, grad_hidden_add_first=60, grad_value_merge=60, grad_hidden=60,
)


def dot_nn(a, b):
    return jnp.dot(a, b, preferred_element_type=F32)


def dot_nt(a, b):
    return lax.dot_general(a, b, (((1,), (1,)), ((), ())), preferred_element_type=F32)


def dot_tn(a, b):
    return lax.dot_general(a, b, (((0,), (0,)), ((), ())), preferred_element_type=F32)


def sigmoid(v):
    return 0.5 * jnp.tanh(0.5 * v) + 0.5


def normalize(v):
    center = v - jnp.mean(v, axis=-1, keepdims=True)
    rstd = lax.rsqrt(jnp.mean(center * center, axis=-1, keepdims=True) + EPS)
    return center * rstd, rstd


def norm_back(e, n, rstd):
    return (e - jnp.mean(e, axis=-1, keepdims=True) - n * jnp.mean(e * n, axis=-1, keepdims=True)) * rstd


def swap_matrix():
    row = lax.broadcasted_iota(jnp.int32, (ROWS, ROWS), 0)
    col = lax.broadcasted_iota(jnp.int32, (ROWS, ROWS), 1)
    return jnp.where(col == (row % GROUP) * STEPS + row // GROUP, 1.0, 0.0).astype(BF16)


def swap_in(block):
    return dot_nn(swap_matrix(), block.reshape(ROWS, EMBED))


def swap_out(rows):
    moved = dot_nn(swap_matrix(), rows).astype(BF16)
    return moved.reshape(GROUP // CHUNKS, CHUNKS, STEPS, EMBED)


def part(at, count=1):
    return slice(at * EMBED, (at + count) * EMBED)


def col_chunks():
    return [slice(c * COLS, (c + 1) * COLS) for c in range(EMBED // COLS)]


def step_rows(j):
    return slice(j * GROUP, (j + 1) * GROUP)


def full(shape):
    return pl.BlockSpec(shape, lambda i: (0,) * len(shape), pipeline_mode=pl.Buffered(buffer_count=1))


def ordered(kernel, skip, count):
    return lambda *refs: kernel(*refs[:skip], *refs[skip + count :])


def cost(name):
    return pl.CostEstimate(flops=int(COSTS.get(name, 2) * 1e9), bytes_accessed=0, transcendentals=0)


def call(kernel, grid, in_specs, out_specs, out_shape, scratch, name, after=(), bits=None, weights=(), aliases=None):
    if bits is not None:
        kernel = grouped(kernel, [len(pieces) for pieces in weights])
        in_specs = [SMEM_SPEC] + [ANY_SPEC] * sum(len(pieces) for pieces in weights) + in_specs
    made = pl.pallas_call(
        ordered(kernel, 0, len(after)),
        grid=(grid,),
        in_specs=[ANY_SPEC] * len(after) + in_specs,
        out_specs=out_specs,
        out_shape=out_shape,
        scratch_shapes=scratch,
        compiler_params=pltpu.CompilerParams(
            dimension_semantics=("arbitrary",), vmem_limit_bytes=VMEM.get(name, 16) * MIB
        ),
        cost_estimate=cost(name),
        input_output_aliases=aliases or {},
        name=name,
    )
    head = (bits,) + tuple(piece for pieces in weights for piece in pieces) if bits is not None else ()
    return lambda *args: made(*after, *head, *args)


def grouped(kernel, counts):
    def run(bits_ref, *refs):
        groups = []
        for count in counts:
            groups.append(refs[:count])
            refs = refs[count:]
        return kernel(bits_ref, *groups, *refs)

    return run


SMEM_SPEC = pl.BlockSpec(memory_space=pltpu.SMEM)
ANY_SPEC = pl.BlockSpec(memory_space=pl.ANY)


def column_loads(pieces, target, sems, first, low, high, base=0, bits_ref=None):
    cols, place = slice(low, high), slice(low - base, high - base)
    if len(pieces) == 1:
        return [pltpu.make_async_copy(pieces[0].at[:, cols], target.at[:, place], sems.at[first])]
    copies = []
    height = target.shape[0] // 8
    for piece, core in zip(pieces, (bits_ref[0], 1 - bits_ref[0])):
        for q in range(4):
            rows = pl.ds(pl.multiple_of((2 * q + core) * height, height), height)
            copies.append(
                pltpu.make_async_copy(
                    piece.at[q * height : (q + 1) * height, cols], target.at[rows, place],
                    sems.at[first + len(copies)],
                )
            )
    return copies


def start_loads(*loads):
    @pl.when(pl.program_id(0) == 0)
    def _():
        for copies in loads:
            for copy in copies:
                copy.start()


def wait_all(copies):
    for copy in copies:
        copy.wait()


def wait_load(copies):
    pl.when(pl.program_id(0) == 0)(lambda: wait_all(copies))


def first_and_rest(body):
    pl.when(pl.program_id(0) == 0)(lambda: body(True))
    pl.when(pl.program_id(0) > 0)(lambda: body(False))


def mix_one_kernel(
    bits_ref, pieces, tok_ref, edge_ref, vec_ref,
    xp_ref, mix_ref, k_ref, v_ref, r_ref, end_ref, total_ref,
    carry, state_a, state_b, w_ref, sems,
):
    i = pl.program_id(0)
    loads = [
        column_loads(pieces, w_ref, sems, 16 * at, at * EMBED, (at + 1) * EMBED) for at in range(3)
    ]
    start_loads(*loads)

    @pl.when(i == 0)
    def _():
        carry[...] = edge_ref[...]
        state_a[...] = jnp.zeros_like(state_a)
        state_b[...] = jnp.zeros_like(state_b)

    xp_ref[...] = swap_in(tok_ref[...]).astype(BF16)
    hp = carry[...]
    for j in range(STEPS):
        rows = step_rows(j)
        n, _ = normalize(xp_ref[rows, :].astype(F32))
        h = n * vec_ref[0:1, :] + vec_ref[1:2, :]
        diff = h - hp
        for at in range(3):
            mix_ref[rows, part(at)] = (hp + diff * vec_ref[4 + at : 5 + at, :]).astype(BF16)
        hp = h
    carry[...] = hp

    def project(first):
        for at, out_ref in enumerate((k_ref, v_ref, r_ref)):
            if first:
                wait_all(loads[at])
            out_ref[...] = dot_nn(mix_ref[:, part(at)], w_ref[:, part(at)]).astype(out_ref.dtype)

    first_and_rest(project)
    for cols in col_chunks():
        retain = jnp.exp(-jnp.exp(vec_ref[9:10, cols]))
        a = state_a[:, cols]
        b = state_b[:, cols]
        for j in range(STEPS):
            weight = jnp.exp(k_ref[step_rows(j), cols].astype(F32))
            a = retain * a + weight * v_ref[step_rows(j), cols].astype(F32)
            b = retain * b + weight
        state_a[:, cols] = a
        state_b[:, cols] = b

    @pl.when(i == pl.num_programs(0) - 1)
    def _():
        end_ref[:GROUP, :] = state_a[...]
        end_ref[GROUP:, :] = state_b[...]
        rate = -jnp.exp(vec_ref[9:10, :])
        decay = jnp.exp(rate * float(STEPS * pl.num_programs(0)))
        for q in range(2 * GROUP // CHUNKS):
            total = end_ref[q * CHUNKS : q * CHUNKS + 1, :]
            for s in range(1, CHUNKS):
                total = decay * total + end_ref[q * CHUNKS + s : q * CHUNKS + s + 1, :]
            total_ref[q : q + 1, :] = total


def wkv_kernel(
    bits_ref, pieces, k_ref, v_ref, r_ref, xp_ref, vec_ref, start_ref, end_ref,
    wkv_ref, y_ref, x1_ref, mix_ref, st_ref, first_ref, last_ref,
    carry, state_a, state_b, w_ref, sems,
):
    i = pl.program_id(0)
    loads = column_loads(pieces, w_ref, sems, 0, 3 * EMBED, 4 * EMBED, 3 * EMBED)
    start_loads(loads)

    @pl.when(i == 0)
    def _():
        rate = -jnp.exp(vec_ref[9:10, :])
        decay = jnp.exp(rate * float(STEPS * pl.num_programs(0)))
        for q in range(2 * GROUP // CHUNKS):
            state = start_ref[q : q + 1, :]
            target = state_a if q < GROUP // CHUNKS else state_b
            base = (q % (GROUP // CHUNKS)) * CHUNKS
            for s in range(CHUNKS):
                target[base + s : base + s + 1, :] = state
                state = decay * state + end_ref[q * CHUNKS + s : q * CHUNKS + s + 1, :]
        carry[...] = jnp.zeros_like(carry)

    st_ref[0, :GROUP, :] = state_a[...]
    st_ref[0, GROUP:, :] = state_b[...]
    for cols in col_chunks():
        retain = jnp.exp(-jnp.exp(vec_ref[9:10, cols]))
        bonus = vec_ref[10:11, cols]
        a = state_a[:, cols]
        b = state_b[:, cols]
        for j in range(STEPS):
            rows = step_rows(j)
            key = k_ref[rows, cols].astype(F32)
            value = v_ref[rows, cols].astype(F32)
            own = jnp.exp(bonus + key)
            weight = jnp.exp(key)
            wkv = ((a + own * value) * pl.reciprocal(b + own)).astype(BF16)
            wkv_ref[rows, cols] = wkv
            y_ref[rows, cols] = (sigmoid(r_ref[rows, cols].astype(F32)) * wkv.astype(F32)).astype(BF16)
            a = retain * a + weight * value
            b = retain * b + weight
        state_a[:, cols] = a
        state_b[:, cols] = b
    wait_load(loads)
    x1_ref[...] = xp_ref[...].astype(F32) + dot_nn(y_ref[...], w_ref[...])
    hp = carry[...]
    for j in range(STEPS):
        rows = step_rows(j)
        n, _ = normalize(x1_ref[rows, :])
        h = n * vec_ref[2:3, :] + vec_ref[3:4, :]
        diff = h - hp
        for at in range(2):
            mix_ref[rows, part(at)] = (hp + diff * vec_ref[7 + at : 8 + at, :]).astype(BF16)
        if j == 0:

            @pl.when(i == 0)
            def _(h=h):
                first_ref[...] = h

        hp = h
    carry[...] = hp
    last_ref[...] = hp


def hidden_kernel(bits_ref, pieces, mix_ref, kq_ref, gate_ref, w_ref, sems):
    loads = [
        column_loads(pieces, w_ref, sems, 16 * at, at * EMBED, (at + 1) * EMBED) for at in range(5)
    ]
    start_loads(*loads)

    def project(first):
        for c in range(FF // EMBED):
            if first:
                wait_all(loads[c])
            active = jnp.maximum(dot_nn(mix_ref[:, part(0)], w_ref[:, part(c)]), 0.0)
            kq_ref[:, part(c)] = (active * active).astype(BF16)
        if first:
            wait_all(loads[4])
        gate_ref[...] = dot_nn(mix_ref[:, part(1)], w_ref[:, FF:]).astype(BF16)

    first_and_rest(project)


def rep_loads(bits_ref, pieces, target, sems, first, low):
    copies = []
    for at, piece in enumerate(pieces):
        high = bits_ref[4] if at % 2 == 0 else 1 - bits_ref[4]
        bit = bits_ref[3] if at < 2 else 1 - bits_ref[3]
        height = target.shape[0] // 32
        for block in range(8):
            rows = pl.ds(pl.multiple_of((4 * block + 2 * high + bit) * height, height), height)
            copies.append(
                pltpu.make_async_copy(
                    piece.at[block * height : (block + 1) * height, :], target.at[rows, low:],
                    sems.at[first + len(copies)],
                )
            )
    return copies


def value_kernel(
    bits_ref, pieces, others, kq_ref, gate_ref, x1_ref, cot_ref,
    mixed_ref, dvf_ref, grad_ref, cp_ref, w_ref, vf_ref, out_ref, sems,
):
    half = EMBED // 2
    if others:
        loads = [
            column_loads(pieces, w_ref, sems, 0, 0, half),
            rep_loads(bits_ref, others, w_ref, sems, 1, half),
        ]
    else:
        loads = [column_loads(pieces, w_ref, sems, at, at * half, (at + 1) * half) for at in range(2)]
    start_loads(*loads)
    cp_ref[...] = swap_in(cot_ref[...]).astype(BF16)

    def project(first):
        if not first:
            vf_ref[...] = dot_nn(kq_ref[...], w_ref[...])
            return
        for at in range(2):
            wait_all(loads[at])
            cols = slice(at * half, (at + 1) * half)
            vf_ref[:, cols] = dot_nn(kq_ref[...], w_ref[:, cols])

    first_and_rest(project)
    for j in range(STEPS):
        rows = step_rows(j)
        gate = sigmoid(gate_ref[rows, :].astype(F32))
        vf = vf_ref[rows, :]
        out_ref[rows, :] = (x1_ref[rows, :] + gate * vf).astype(BF16)
        scaled = cp_ref[rows, :].astype(F32) * gate
        dvf_ref[rows, :] = scaled.astype(BF16)
        grad_ref[rows, FF:] = (scaled * vf * (1.0 - gate)).astype(BF16)
    for c in range(FF // EMBED):
        back = dot_nt(dvf_ref[...], w_ref[part(c), :])
        square = kq_ref[:, part(c)].astype(F32)
        root = square * lax.rsqrt(jnp.maximum(square, TINY))
        grad_ref[:, part(c)] = (back * (2.0 * root)).astype(BF16)
    mixed_ref[...] = swap_out(out_ref[...])


def send_rows(flag_ref, shift, send_ref):
    for m in range(send_ref.shape[0]):
        row = shift[m * CHUNKS : m * CHUNKS + 1]
        send_ref[m : m + 1, :] = jnp.where(flag_ref[m] > 0, 0.0, row)


def take_rows(carry, shift_ref, got_ref):
    for m in range(got_ref.shape[0]):
        base = m * CHUNKS
        carry[base : base + CHUNKS - 1, :] = shift_ref[base + 1 : base + CHUNKS, :]
        carry[base + CHUNKS - 1 : base + CHUNKS, :] = got_ref[m : m + 1, :]


def edge_kernel(bits_ref, pieces, flag_ref, grad_ref, vec_ref, shift_ref, send_ref, w_ref, sems):
    loads = column_loads(pieces, w_ref, sems, 0, 0, FF + EMBED)
    start_loads(loads)
    wait_all(loads)
    shift = dot_nt(grad_ref[:, :FF], w_ref[:, :FF]) * (1.0 - vec_ref[7:8, :])
    shift += dot_nt(grad_ref[:, FF:], w_ref[:, FF:]) * (1.0 - vec_ref[8:9, :])
    shift_ref[...] = shift
    send_rows(flag_ref, shift, send_ref)


def add_sums(sums, values):
    for at, value in enumerate(values):
        sums[at] += value


def middle_back_kernel(weights, ins, outs, scratch, copies, grad):
    pieces, out_pieces = weights
    (
        grad_ref, x1_ref, before_ref, edge_ref, later_ref, got_ref, cp_ref, vec_ref, k_ref, v_ref, r_ref, wkv_ref,
        st_ref,
    ) = ins
    dx1_ref, out_ref, dwkv_ref, vsum_ref, first_ref, total_ref = outs
    carry, den, state_p, state_q, w_ref, wo_ref, dxk_ref, dxr_ref, sums, sems = scratch
    i = pl.program_id(0)
    count = pl.num_programs(0)
    loads = [
        column_loads((pieces,), w_ref, sems, 0, 0, FF + EMBED),
        column_loads((out_pieces,), wo_ref, sems, 16, 3 * EMBED, 4 * EMBED, 3 * EMBED),
    ]
    start_loads(*loads)

    @pl.when(i == 0)
    def _():
        take_rows(carry, later_ref, got_ref)
        sums[...] = jnp.zeros_like(sums)
        state_p[...] = jnp.zeros_like(state_p)
        state_q[...] = jnp.zeros_like(state_q)

    for cols in col_chunks():
        retain = jnp.exp(-jnp.exp(vec_ref[9:10, cols]))
        bonus = vec_ref[10:11, cols]
        a = st_ref[0, :GROUP, cols]
        b = st_ref[0, GROUP:, cols]
        for j in range(STEPS):
            rows = step_rows(j)
            key = k_ref[rows, cols].astype(F32)
            value = v_ref[rows, cols].astype(F32)
            own = jnp.exp(bonus + key)
            weight = jnp.exp(key)
            scale = pl.reciprocal(b + own)
            den[0, rows, cols] = scale
            den[1, rows, cols] = (a + own * value) * scale
            a = retain * a + weight * value
            b = retain * b + weight
    wait_load(loads[0] + loads[1] + copies)
    dxk_ref[...] = dot_nt(grad_ref[:, :FF], w_ref[:, :FF])
    dxr_ref[...] = dot_nt(grad_ref[:, FF:], w_ref[:, FF:])
    grad()
    gain = vec_ref[2:3, :]
    offset = vec_ref[3:4, :]
    share_k = vec_ref[7:8, :]
    share_r = vec_ref[8:9, :]
    n, rstd = normalize(x1_ref[step_rows(STEPS - 1), :])
    later = carry[...]
    for j in reversed(range(STEPS)):
        rows = step_rows(j)
        if j > 0:
            n_next, rstd_next = normalize(x1_ref[step_rows(j - 1), :])
            h_before = n_next * gain + offset
        else:
            n_before, _ = normalize(before_ref[...])
            h_before = jnp.where(i == count - 1, edge_ref[...], n_before * gain + offset)
        diff = n * gain + offset - h_before
        dxk = dxk_ref[rows, :]
        dxr = dxr_ref[rows, :]
        kept_k = dxk * share_k
        kept_r = dxr * share_r
        dh = kept_k + kept_r + later
        later = (dxk - kept_k) + (dxr - kept_r)
        add_sums(sums, (dh * n, dh, dxk * diff, dxr * diff))
        dx1 = cp_ref[rows, :].astype(F32) + norm_back(dh * gain, n, rstd)
        dx1_ref[rows, :] = dx1
        out_ref[rows, part(0)] = dx1.astype(BF16)
        if j > 0:
            n, rstd = n_next, rstd_next
    carry[...] = later
    dxk_ref[...] = dot_nt(out_ref[:, part(0)], wo_ref[...])
    for cols in col_chunks():
        retain = jnp.exp(-jnp.exp(vec_ref[9:10, cols]))
        right = slice(EMBED + cols.start, EMBED + cols.stop)
        p = state_p[:, cols]
        q = state_q[:, cols]
        for j in reversed(range(STEPS)):
            rows = step_rows(j)
            gate = sigmoid(r_ref[rows, cols].astype(F32))
            scaled = dxk_ref[rows, cols] * gate
            dwkv = scaled.astype(BF16)
            dwkv_ref[rows, cols] = dwkv
            out_ref[rows, right] = (scaled * wkv_ref[rows, cols].astype(F32) * (1.0 - gate)).astype(BF16)
            grad = dwkv.astype(F32) * den[0, rows, cols]
            p = grad + retain * p
            q = retain * q - grad * den[1, rows, cols]
        state_p[:, cols] = p
        state_q[:, cols] = q

    @pl.when(i == count - 1)
    def _():
        vsum_ref[...] = jnp.zeros_like(vsum_ref)
        for at in range(4):
            vsum_ref[at : at + 1, :] = jnp.sum(sums[at], axis=0, keepdims=True)
        first_ref[:GROUP, :] = state_p[...]
        first_ref[GROUP:, :] = state_q[...]
        rate = -jnp.exp(vec_ref[9:10, :])
        decay = jnp.exp(rate * float(STEPS * count))
        for q in range(2 * GROUP // CHUNKS):
            base = q * CHUNKS
            total = first_ref[base + CHUNKS - 1 : base + CHUNKS, :]
            for s in reversed(range(CHUNKS - 1)):
                total = decay * total + first_ref[base + s : base + s + 1, :]
            for d in range(total_ref.shape[0]):
                total_ref[d, q : q + 1, :] = total


def wkv_back_kernel(weights, ins, outs, scratch, copies, grad):
    (pieces,) = weights
    flag_ref, k_ref, v_ref, dwkv_ref, dr_ref, st_ref, vec_ref, every_ref, first_ref = ins
    out_ref, vsum_ref, edge_ref, send_ref = outs
    past_a, past_b, state_p, state_q, sums, w_ref, sems = scratch
    make_grad = grad
    i = pl.program_id(0)
    count = pl.num_programs(0)
    loads = column_loads((pieces,), w_ref, sems, 0, 0, 3 * EMBED)
    start_loads(loads)

    @pl.when(i == 0)
    def _():
        sums[...] = jnp.zeros_like(sums)
        rate = -jnp.exp(vec_ref[9:10, :])
        decay = jnp.exp(rate * float(STEPS * count))
        devices, four, _ = every_ref.shape
        micro = four // 2
        whole = jnp.exp(rate * float(STEPS * count * CHUNKS))
        for q in range(2 * GROUP // CHUNKS):
            state = jnp.zeros((1, EMBED), F32)
            passed = state
            for d in reversed(range(devices)):
                state = jnp.where(flag_ref[micro] == d, passed, state)
                begins = flag_ref[micro + 1 + d * micro + q % micro]
                passed = jnp.where(begins > 0, 0.0, whole * passed + every_ref[d, q : q + 1, :])
            target = state_p if q < GROUP // CHUNKS else state_q
            base = (q % (GROUP // CHUNKS)) * CHUNKS
            for s in reversed(range(CHUNKS)):
                target[base + s : base + s + 1, :] = state
                state = decay * state + first_ref[q * CHUNKS + s : q * CHUNKS + s + 1, :]

    for cols in col_chunks():
        right = slice(EMBED + cols.start, EMBED + cols.stop)
        retain = jnp.exp(-jnp.exp(vec_ref[9:10, cols]))
        bonus = vec_ref[10:11, cols]
        a = st_ref[0, :GROUP, cols]
        b = st_ref[0, GROUP:, cols]
        for j in range(STEPS):
            rows = step_rows(j)
            weight = jnp.exp(k_ref[rows, cols].astype(F32))
            past_a[rows, cols] = a
            past_b[rows, cols] = b
            a = retain * a + weight * v_ref[rows, cols].astype(F32)
            b = retain * b + weight
        p = state_p[:, cols]
        q = state_q[:, cols]
        sum_decay = sums[0, :, cols]
        sum_bonus = sums[1, :, cols]
        for j in reversed(range(STEPS)):
            rows = step_rows(j)
            key = k_ref[rows, cols].astype(F32)
            value = v_ref[rows, cols].astype(F32)
            own = jnp.exp(bonus + key)
            weight = jnp.exp(key)
            a = past_a[rows, cols]
            b = past_b[rows, cols]
            scale = pl.reciprocal(b + own)
            wkv = (a + own * value) * scale
            grad = dwkv_ref[rows, cols].astype(F32) * scale
            own_grad = grad * own
            bonus_term = own_grad * (value - wkv)
            out_ref[rows, cols] = (bonus_term + weight * (value * p + q)).astype(BF16)
            out_ref[rows, right] = (own_grad + weight * p).astype(BF16)
            sum_decay += a * p + b * q
            sum_bonus += bonus_term
            p = grad + retain * p
            q = retain * q - grad * wkv
        state_p[:, cols] = p
        state_q[:, cols] = q
        sums[0, :, cols] = sum_decay
        sums[1, :, cols] = sum_bonus
    wait_load(copies)
    make_grad()

    @pl.when(i == count - 1)
    def _():
        rate = -jnp.exp(vec_ref[9:10, :])
        vsum_ref[...] = jnp.zeros_like(vsum_ref)
        vsum_ref[0:1, :] = jnp.sum(sums[0], axis=0, keepdims=True) * jnp.exp(rate) * rate
        vsum_ref[1:2, :] = jnp.sum(sums[1], axis=0, keepdims=True)
        wait_all(loads)
        rows = slice(0, GROUP)
        edge = dot_nt(out_ref[rows, part(0)], w_ref[:, part(0)]) * (1.0 - vec_ref[4:5, :])
        edge += dot_nt(out_ref[rows, part(1)], w_ref[:, part(1)]) * (1.0 - vec_ref[5:6, :])
        edge += dot_nt(dr_ref[rows, :], w_ref[:, part(2)]) * (1.0 - vec_ref[6:7, :])
        edge_ref[...] = edge
        send_rows(flag_ref, edge, send_ref)


def input_back_kernel(lowest, weights, ins, outs, scratch, copies=(), grad=None):
    (pieces,) = weights
    grad_ref, dr_ref, xp_ref, before_ref, edge_ref, later_ref, got_ref, dx1_ref, vec_ref = ins[:9]
    out_ref, vsum_ref, later_out = outs
    carry, w_ref, back, rows_ref, sums, sems = scratch
    i = pl.program_id(0)
    count = pl.num_programs(0)
    loads = column_loads((pieces,), w_ref, sems, 0, 0, 3 * EMBED)
    start_loads(loads)

    @pl.when(i == 0)
    def _():
        if lowest:
            carry[...] = later_ref[...]
        else:
            take_rows(carry, later_ref, got_ref)
        sums[...] = jnp.zeros_like(sums)

    wait_load(loads)
    for at, grads in enumerate((grad_ref[:, part(0)], grad_ref[:, part(1)], dr_ref[...])):
        back[at] = dot_nt(grads, w_ref[:, part(at)])
    wait_load(list(copies))
    if grad is not None:
        grad()
    gain = vec_ref[0:1, :]
    offset = vec_ref[1:2, :]
    n, rstd = normalize(xp_ref[step_rows(STEPS - 1), :].astype(F32))
    later = carry[...]
    for j in reversed(range(STEPS)):
        rows = step_rows(j)
        if j > 0:
            n_next, rstd_next = normalize(xp_ref[step_rows(j - 1), :].astype(F32))
            h_before = n_next * gain + offset
        else:
            n_before, _ = normalize(before_ref[...].astype(F32))
            h_before = n_before * gain + offset
            if lowest:
                h_before = jnp.where(i == count - 1, edge_ref[...], h_before)
        diff = n * gain + offset - h_before
        dh = later
        later = None
        for at in range(3):
            grad = back[at, rows, :]
            kept = grad * vec_ref[4 + at : 5 + at, :]
            sums[2 + at] += grad * diff
            dh = dh + kept
            passed = grad - kept
            later = passed if later is None else later + passed
        sums[0] += dh * n
        sums[1] += dh
        rows_ref[rows, :] = (dx1_ref[rows, :] + norm_back(dh * gain, n, rstd)).astype(BF16)
        if j > 0:
            n, rstd = n_next, rstd_next
    carry[...] = later
    later_out[...] = later
    out_ref[...] = swap_out(rows_ref[...])

    @pl.when(i == count - 1)
    def _():
        vsum_ref[...] = jnp.zeros_like(vsum_ref)
        for at in range(5):
            vsum_ref[at : at + 1, :] = jnp.sum(sums[at], axis=0, keepdims=True)
        if lowest:
            vsum_ref[...] += ins[10][...]


def adam_step(master, moment, second, gradient, rate, shrink):
    moment_new = 0.9 * moment + 0.1 * gradient
    second_new = 0.95 * second + 0.05 * gradient * gradient
    scaled = moment_new / (1.0 - 0.9**STEP) / (jnp.sqrt(second_new / (1.0 - 0.95**STEP)) + 1e-08)
    return (master - rate * (scaled + shrink * master), moment_new, second_new)


def neighbour(block, axis, distance):
    devices = range(lax.axis_size(axis))
    return lax.ppermute(block, axis, [(i, i + distance) for i in devices if i + distance in devices])


def everyone(block, axis):
    count = lax.axis_size(axis)
    return lax.all_to_all(
        jnp.broadcast_to(block[None], (count,) + block.shape), axis, 0, 0, tiled=True
    )


def scatter_rows(grad):
    part = lax.psum_scatter(grad.astype(BF16), "tok", scatter_dimension=0, tiled=True)
    return lax.psum_scatter(part, "rep", scatter_dimension=0, tiled=True).astype(F32)


def weight_grad(a, b):
    return dot_tn(a, b).astype(BF16)


def flip(block, axis, bit):
    return lax.ppermute(block, axis, [(i, i ^ bit) for i in range(lax.axis_size(axis))])


def place_all_kernel(bits_ref, own, far, near, both, out):
    height = own.shape[0]
    for source, high, low in (
        (own, bits_ref[4], bits_ref[3]), (far, 1 - bits_ref[4], bits_ref[3]),
        (near, bits_ref[4], 1 - bits_ref[3]), (both, 1 - bits_ref[4], 1 - bits_ref[3]),
    ):
        out[pl.ds(pl.multiple_of((2 * high + low) * height, height), height), :] = source[...]


def place(kernel, bits, inputs, shapes, name, after=()):
    vmem = pl.BlockSpec(memory_space=pltpu.VMEM)
    return pl.pallas_call(
        ordered(kernel, 0, len(after)),
        in_specs=[ANY_SPEC] * len(after) + [SMEM_SPEC] + [vmem] * len(inputs),
        out_specs=[vmem] * len(shapes),
        out_shape=[jax.ShapeDtypeStruct(shape, BF16) for shape in shapes],
        compiler_params=pltpu.CompilerParams(vmem_limit_bytes=VMEM.get(name, 16) * MIB),
        cost_estimate=cost(name),
        name=name,
    )(*after, bits, *inputs)


def cast_kernel(source, target):
    target[...] = source[...].astype(BF16)


def cast(shard, after, name):
    block = pl.BlockSpec(shard.shape, lambda i: (0, 0))
    return call(
        cast_kernel, 1, [block], block, jax.ShapeDtypeStruct(shard.shape, BF16), [], name, after
    )(shard)


def gather_plain(shard):
    return [lax.all_gather(lax.all_gather(shard, "rep", axis=0, tiled=True), "tok", axis=0, tiled=True)]


def rep_rows(shard):
    far = flip(shard, "rep", 2)
    return shard, far, flip(shard, "rep", 1), flip(far, "rep", 1)


def gather_rep(shard, bits, name, after=()):
    height, width = shard.shape
    return place(place_all_kernel, bits, rep_rows(shard), [(4 * height, width)], name + "_rep", after)[0]


def held(array, after, name):
    return pl.pallas_call(
        lambda *refs: None,
        in_specs=[ANY_SPEC] * (1 + len(after)),
        out_specs=ANY_SPEC,
        out_shape=jax.ShapeDtypeStruct(array.shape, array.dtype),
        input_output_aliases={0: 0},
        cost_estimate=cost(name),
        name=name,
    )(array, *after)


SLOTS = ((0, 0), (0, 1), (1, 0), (1, 1))


def store_slot(outs, slot, value, left):
    dy, dx = SLOTS[slot]
    if left:
        outs[dx][dy] = value
    else:
        outs[2 + dy][dx] = value


def beside(main, counts, pairs, takes, bits_ref, *refs):
    lists, lhs_count = [], 2 * len(pairs)
    for count in (counts[0], counts[1], lhs_count, 2 * len(takes), counts[2], 4, counts[3], 3):
        lists.append(refs[:count])
        refs = refs[count:]
    weights, ins, lhs_refs, rhs_refs, outs, grads, scratch, (lhs, made, sems) = lists
    i = pl.program_id(0)
    steps = pl.num_programs(0)
    height = EMBED // 8
    copies = []
    for at, base in enumerate(pairs):
        for which in range(2):
            for slot, (dy, dx) in enumerate(SLOTS):
                block = base + 4 * (bits_ref[2] ^ dy) + 2 * (bits_ref[1] ^ dx) + bits_ref[0]
                cols = pl.ds(pl.multiple_of(block * height, height), height)
                copies.append(
                    pltpu.make_async_copy(
                        lhs_refs[2 * at + which].at[:, cols],
                        lhs.at[2 * at + which, :, slot * height : (slot + 1) * height],
                        sems.at[len(copies)],
                    )
                )
    start_loads(copies)

    def grad():
        column = 0
        for at, (width, of_step) in enumerate(takes):
            pair = of_step[0] if len(set(of_step)) == 1 else i * len(pairs) // steps
            total = dot_tn(lhs[2 * pair], rhs_refs[2 * at][...]) + dot_tn(lhs[2 * pair + 1], rhs_refs[2 * at + 1][...])
            made[:, column : column + width] = total.astype(BF16)
            column += width

    main(weights, ins, outs, scratch, copies, grad)
    for left in (True, False):

        @pl.when((i < steps // 2) == left)
        def _(left=left):
            for slot in range(4):
                store_slot(grads, slot, made[slot * height : (slot + 1) * height, :], left)


def alone(main, counts, bits_ref, *refs):
    lists = []
    for count in counts:
        lists.append(refs[:count])
        refs = refs[count:]
    main(*lists, [], lambda: None)


def call_main(
    kernel, grid, ins, in_specs, out_specs, out_shape, scratch, name, after, bits, weights, lhs=(), takes=(),
    rhs=(), aliases=None,
):
    counts = (len(weights), len(in_specs), len(out_specs), len(scratch))
    if lhs:
        rows = rhs[0].shape[0]
        height = EMBED // 8
        lhs_args = [array for own, other, _ in lhs for array in (own, other)]
        rhs_specs, rhs_args = [], []
        for width, base, _ in takes:
            rhs_specs += [pl.BlockSpec((rows, width), lambda i, base=base: (0, base + i))] * 2
            rhs_args += rhs
        total = sum(width for width, _, _ in takes)
        left = pl.BlockSpec((2, height, total), lambda i: (0, 0, jnp.minimum(i, grid // 2 - 1)))
        right = pl.BlockSpec((2, height, total), lambda i: (0, 0, jnp.maximum(i - grid // 2, 0)))
        body = functools.partial(
            beside, kernel, counts, [base for _, _, base in lhs], [(width, pair) for width, _, pair in takes]
        )
        in_specs = in_specs + [ANY_SPEC] * len(lhs_args) + rhs_specs
        out_specs = out_specs + [left, left, right, right]
        out_shape = out_shape + [jax.ShapeDtypeStruct((2, height, total * grid // 2), BF16)] * 4
        scratch = scratch + [
            pltpu.VMEM((2 * len(lhs), rows, 4 * height), BF16), pltpu.VMEM((4 * height, total), BF16),
            pltpu.SemaphoreType.DMA((8 * len(lhs),)),
        ]
        ins = (*ins, *lhs_args, *rhs_args)
    else:
        body = functools.partial(alone, kernel, counts)
    heads = len(weights)

    def run(bits_ref, *refs):
        body(bits_ref, *[group[0] for group in refs[:heads]], *refs[heads:])

    results = call(
        run, grid, in_specs, out_specs, out_shape, scratch, name, after, bits, weights, aliases
    )(*ins)
    return results[: counts[2]], results[counts[2] :]


def grad_only(weights, ins, outs, scratch, copies, grad):
    wait_load(copies)
    grad()


def tall_kernel(bits_ref, lhs_own, lhs_other, rhs_own, rhs_other, *outs):
    i = pl.program_id(0)
    total = dot_tn(lhs_own[...], rhs_own[...]) + dot_tn(lhs_other[...], rhs_other[...])
    total = total.astype(BF16)
    half = total.shape[1] // 2
    for at, (left, right) in enumerate(((0, 2), (0, 3), (1, 2), (1, 3))):

        @pl.when(i == at)
        def _(left=left, right=right):
            outs[left][0] = total[:, :half]
            outs[right][0] = total[:, half:]


def core_grad(bits, lhs, rhs, name, after=()):
    rows, height, width = rhs[0].shape[0], lhs[0].shape[1] // 8, rhs[0].shape[1] // 2

    def column(i, b):
        return (0, 4 * (b[2] ^ (i % 2)) + 2 * (b[1] ^ (i // 2)) + b[0])

    spec = pl.BlockSpec((rows, height), column)
    whole = pl.BlockSpec((rows, 2 * width), lambda i, b: (0, 0))
    return pl.pallas_call(
        ordered(tall_kernel, 1, len(after)),
        grid_spec=pltpu.PrefetchScalarGridSpec(
            num_scalar_prefetch=1,
            grid=(4,),
            in_specs=[ANY_SPEC] * len(after) + [spec, spec, whole, whole],
            out_specs=[
                pl.BlockSpec((1, height, width), lambda i, b: (jnp.minimum(i, 1), 0, 0)),
                pl.BlockSpec((1, height, width), lambda i, b: (jnp.maximum(i - 2, 0), 0, 0)),
                pl.BlockSpec((1, height, width), lambda i, b: (i // 2, 0, 0)),
                pl.BlockSpec((1, height, width), lambda i, b: (i // 2, 0, 0)),
            ],
        ),
        out_shape=[jax.ShapeDtypeStruct((2, height, width), BF16)] * 4,
        compiler_params=pltpu.CompilerParams(
            dimension_semantics=("arbitrary",), vmem_limit_bytes=VMEM.get(name, 16) * MIB
        ),
        cost_estimate=cost(name),
        name=name,
    )(bits, *after, *lhs, *rhs)


def add_kernel(count, bits_ref, *refs):
    for at in range(count):
        total = refs[2 * at][...].astype(F32) + refs[2 * at + 1][...].astype(F32)
        refs[2 * count + at][...] = total.astype(BF16)


def add_split(bits, grid, sums, name, after=()):
    in_specs, out_specs, shapes, args = [], [], [], []
    for a, b, block, source, shape, target in sums:
        in_specs += [pl.BlockSpec(block, source)] * 2
        args += [a, b]
        out_specs.append(pl.BlockSpec(block, target))
        shapes.append(jax.ShapeDtypeStruct(shape, BF16))
    return pl.pallas_call(
        ordered(functools.partial(add_kernel, len(sums)), 1, len(after)),
        grid_spec=pltpu.PrefetchScalarGridSpec(
            num_scalar_prefetch=1, grid=grid, in_specs=[ANY_SPEC] * len(after) + in_specs, out_specs=out_specs
        ),
        out_shape=shapes,
        compiler_params=pltpu.CompilerParams(vmem_limit_bytes=VMEM.get(name, 16) * MIB),
        cost_estimate=cost(name),
        name=name,
    )(bits, *after, *args)


def merge_kernel(moves, bits_ref, p_keep, p_got, q_keep, q_got, *outs):
    p = (p_keep[...].astype(F32) + p_got[...].astype(F32)).astype(BF16)
    q = (q_keep[...].astype(F32) + q_got[...].astype(F32)).astype(BF16)
    half = p.shape[-1]
    if len(outs) == 1:
        for side, start, width, column in moves or ((0, 0, half, 0), (1, 0, q.shape[-1], half)):
            outs[0][:, column : column + width] = (p, q)[side][0, :, start : start + width]
        return
    height = p.shape[1] // 2
    moves = moves or ((0, 0, half, 0), (1, 0, q.shape[-1], half))
    for out, low in ((outs[0], 1 - bits_ref[3]), (outs[1], bits_ref[3])):
        for at in range(2):

            @pl.when(low == at)
            def _(out=out, at=at):
                rows = slice(at * height, (at + 1) * height)
                for side, start, width, column in moves:
                    out[0, :, column : column + width] = (p, q)[side][0, rows, start : start + width]


def merge(bits, p_keep, p_got, q_keep, q_got, shapes, name, after, moves=()):
    _, block, p_width = p_keep.shape
    q_width = q_keep.shape[2]
    in_specs = [
        pl.BlockSpec((1, block // 2, width), lambda h, b: (0, h, 0))
        for width in (p_width, p_width, q_width, q_width)
    ]
    if len(shapes) == 1:
        out_specs = [pl.BlockSpec((block // 2, p_width + q_width), lambda h, b: (h, 0))]
    else:
        out_specs = [pl.BlockSpec((1,) + shapes[0][1:], lambda h, b: (h, 0, 0))] * 2
    return pl.pallas_call(
        ordered(functools.partial(merge_kernel, moves), 1, len(after)),
        grid_spec=pltpu.PrefetchScalarGridSpec(
            num_scalar_prefetch=1, grid=(2,), in_specs=[ANY_SPEC] * len(after) + in_specs, out_specs=out_specs
        ),
        out_shape=[jax.ShapeDtypeStruct(shape, BF16) for shape in shapes],
        compiler_params=pltpu.CompilerParams(vmem_limit_bytes=VMEM.get(name, 16) * MIB),
        cost_estimate=cost(name),
        name=name,
    )(bits, *after, p_keep, p_got, q_keep, q_got)


def reduce_grad(bits, made, offload, name, moves=()):
    p_keep, p_send, q_keep, q_send = made
    p_got, q_got = flip(p_send, "tok", 2), flip(q_send, "tok", 4)
    after = yield p_keep
    _, block, p_width = p_keep.shape
    q_width = q_keep.shape[2]
    half = block // 2
    sums = []
    for which in (1, 0):
        for keep, got, width in ((p_keep, p_got, p_width), (q_keep, q_got, q_width)):
            sums.append((
                keep, got, (1, half, width), lambda r, b, which=which: (which, r, 0),
                (1, block, width), lambda r, b: (0, r, 0),
            ))
    p_send, q_send, p_keep, q_keep = add_split(bits, (2,), sums, name + "_add_first", after)
    p_got, q_got = flip(p_send, "tok", 4), flip(q_send, "tok", 2)
    after = yield p_keep
    width = p_width + q_width
    if offload:
        (total,) = merge(bits, p_keep, p_got, q_keep, q_got, [(block, width)], name + "_merge", after, moves)
        yield total
        part = lax.psum_scatter(total, "rep", scatter_dimension=0, tiled=True)
        after = yield part
        yield held(part, after, name + "_hold").astype(F32)
        return
    shape = (2, block // 4, width)
    send, keep = merge(bits, p_keep, p_got, q_keep, q_got, [shape] * 2, name + "_merge", after, moves)
    got = flip(send, "rep", 1)
    after = yield keep
    sums = [
        (keep, got, (1,) + shape[1:], lambda i, b, f=f: (b[4] ^ f, 0, 0), (1,) + shape[1:], lambda i, b: (0, 0, 0))
        for f in (1, 0)
    ]
    send, keep = add_split(bits, (1,), sums, name + "_add_low", after)
    got = flip(send, "rep", 2)
    yield keep
    after = yield got
    if after:
        got = held(got, after, name + "_hold")
    yield (keep.astype(F32) + got.astype(F32))[0]


def reduce_plain(lhs, rhs):
    sums, column = [], 0
    for array, _, base, tiles in lhs:
        if array.shape[1] > EMBED and array.shape[1] != FF:
            array = array[:, base * EMBED // 8 : base * EMBED // 8 + EMBED]
        sums.append(scatter_rows(weight_grad(array, rhs[0][:, part(column, tiles)])))
        column += tiles
    total = jnp.concatenate(sums, axis=1)
    for _ in range(5):
        yield total[:8]
    yield total


def advance(work, *after):
    return work.send(tuple(after))


def on_device(
    tokens, cotangent, init_num, init_den, prev_att, seg_doc, w_kvr, w_out, f_kr, f_value, vectors,
    m_kvr, v_kvr, m_out, v_out, m_fkr, v_fkr, m_fvalue, v_fvalue, vec_m, vec_v,
):
    tok_count = lax.axis_size("tok")
    rep_count = lax.axis_size("rep")
    here = lax.axis_index("tok")
    flat_index = here * rep_count + lax.axis_index("rep")
    micro, _, local_len, _ = tokens.shape
    seg_count = seg_doc.shape[2]
    chunk = local_len // CHUNKS
    blocks = chunk // STEPS
    rows = micro * local_len

    rep_index = lax.axis_index("rep")
    bits = jnp.stack([here & 1, (here >> 1) & 1, (here >> 2) & 1, rep_index & 1, (rep_index >> 1) & 1])
    bits = bits.astype(jnp.int32)
    paired = tok_count == 8 and rep_count == 4
    att_shard = jnp.concatenate([w_kvr, w_out], axis=1).astype(BF16)
    before_mix = before_wkv = before_hidden = ()
    if paired:
        half_cols = EMBED // 2
        value_left, value_raw = f_value[:, :half_cols].astype(BF16), f_value[:, half_cols:].astype(BF16)
        att_part = gather_rep(att_shard, bits, "place_att")
        att_w = [lax.all_gather(att_part, "tok", axis=0, tiled=True)]
        hidden_part = gather_rep(cast(f_kr, (att_part,), "cast_hidden"), bits, "place_hidden")
        fkr = [lax.all_gather(hidden_part, "tok", axis=0, tiled=True)]
        value_rows = lax.all_gather(value_raw, "tok", axis=0, tiled=True)
        value_part = gather_rep(value_left, bits, "place_value", (hidden_part,))
        fvalue = [lax.all_gather(value_part, "tok", axis=0, tiled=True)]
        value_rows = held(value_rows, (value_part,), "hold_value")
        value_far = flip(value_rows, "rep", 2)
        value_near = flip(value_rows, "rep", 1)
        value_others = [value_rows, value_far, value_near, flip(value_far, "rep", 1)]
        before_mix = (value_rows,)
        before_wkv = (value_far, value_near)
    else:
        value_others = []
        att_w, fkr, fvalue = gather_plain(att_shard), gather_plain(f_kr.astype(BF16)), gather_plain(f_value.astype(BF16))

    def other_core(array):
        return flip(array, "tok", 1) if paired else None

    documents = seg_doc[:, 0, :]
    marker = jnp.concatenate(
        [jnp.ones((micro, 1), jnp.bool_), documents[:, 1:] != documents[:, :-1]], axis=1
    )
    starts = jnp.arange(tok_count) * local_len
    fresh = jnp.logical_and(marker[:, starts // SEG_LEN], (starts % SEG_LEN == 0)[None, :])
    fresh_here = lax.dynamic_index_in_dim(fresh, here, 1, keepdims=True)
    seg_here = here * local_len // SEG_LEN
    prev_here = lax.dynamic_index_in_dim(prev_att[:, 0], seg_here, 1, keepdims=False).astype(F32)
    init_all = everyone(jnp.concatenate([init_num[:, 0], init_den[:, 0]], axis=0), "tok")
    init_all = jnp.moveaxis(init_all, 0, 2).reshape(2 * micro, seg_count, EMBED)
    rate = -jnp.exp(vectors[9:10])
    fade = jnp.exp(rate * float(local_len))
    fresh_four = jnp.concatenate([fresh, fresh], axis=0)
    flags = jnp.concatenate(
        [fresh_here[:, 0].astype(jnp.int32), jnp.reshape(here, (1,)).astype(jnp.int32),
         jnp.moveaxis(fresh, 1, 0).reshape(-1).astype(jnp.int32)]
    )

    x4 = tokens.reshape(micro, CHUNKS, chunk, EMBED)
    c4 = cotangent.reshape(micro, CHUNKS, chunk, EMBED)

    def edge_back(last, incoming):
        moved = jnp.concatenate([incoming[:, None], last.reshape(micro, CHUNKS, EMBED)[:, :-1]], axis=1)
        return moved.reshape(GROUP, EMBED)

    raw_in = neighbour(tokens[:, 0, -1, :], "tok", 1)
    raw_edge = edge_back(x4[:, :, -1, :], raw_in).astype(F32)
    edge_n, _ = normalize(raw_edge)
    edge_h = edge_n * vectors[0:1] + vectors[1:2]
    first_row = (jnp.arange(GROUP) % CHUNKS == 0)[:, None]
    fresh_rows = jnp.repeat(fresh_here[:, 0], CHUNKS)[:, None]
    replace = jnp.logical_and(first_row, fresh_rows)
    edge_one = jnp.where(replace, jnp.repeat(prev_here, CHUNKS, axis=0), edge_h)

    def up(width):
        return pl.BlockSpec((ROWS, width), lambda i: (i, 0))

    def down(width):
        return pl.BlockSpec((ROWS, width), lambda i: (blocks - 1 - i, 0))

    before_spec = pl.BlockSpec(
        (GROUP, EMBED), lambda i: (jnp.maximum((blocks - 1 - i) * STEPS - 1, 0), 0)
    )
    natural_up = pl.BlockSpec((micro, CHUNKS, STEPS, EMBED), lambda i: (0, 0, i, 0))
    natural_down = pl.BlockSpec((micro, CHUNKS, STEPS, EMBED), lambda i: (0, 0, blocks - 1 - i, 0))
    st_up = pl.BlockSpec((1, 2 * GROUP, EMBED), lambda i: (i, 0, 0))
    st_down = pl.BlockSpec((1, 2 * GROUP, EMBED), lambda i: (blocks - 1 - i, 0, 0))
    vec_spec = full(vectors.shape)
    edge_spec = full((GROUP, EMBED))
    state_spec = full((2 * GROUP, EMBED))
    total_spec = full((2 * micro, EMBED))
    sum_spec = full((8, EMBED))

    def like(width, dtype):
        return jax.ShapeDtypeStruct((rows, width), dtype)

    def small(count, dtype=F32):
        return jax.ShapeDtypeStruct((count, EMBED), dtype)

    def weight(height, width):
        return pltpu.VMEM((height, width), BF16)

    sems = pltpu.SemaphoreType.DMA((80,))
    state = pltpu.VMEM((GROUP, EMBED), F32)
    square = 2 * rows * EMBED * EMBED

    xp, mix, k, v, r, ends, totals = call(
        mix_one_kernel, blocks,
        [natural_up, edge_spec, vec_spec],
        [up(EMBED), up(3 * EMBED)] + [up(EMBED)] * 3 + [state_spec, total_spec],
        [like(EMBED, BF16), like(3 * EMBED, BF16), like(EMBED, BF16), like(EMBED, BF16), like(EMBED, BF16),
         small(2 * GROUP), small(2 * micro)],
        [state] * 3 + [weight(EMBED, 3 * EMBED), sems], "mix_one", before_mix, bits, (att_w,),
    )(x4, edge_one, vectors)

    every = everyone(totals, "tok")
    carried = jnp.zeros((2 * micro, EMBED), F32)
    begin = jnp.zeros((2 * micro, EMBED), F32)
    for d in range(tok_count):
        seg = d * local_len // SEG_LEN
        carried = jnp.where(fresh_four[:, d : d + 1], init_all[:, seg], carried)
        begin = jnp.where(here == d, carried, begin)
        carried = fade * carried + every[d]

    wkv, y, x1, mix_two, saved, first_two, last_two = call(
        wkv_kernel, blocks,
        [up(EMBED)] * 4 + [vec_spec, total_spec, state_spec],
        [up(EMBED)] * 3 + [up(2 * EMBED), st_up, edge_spec, edge_spec],
        [like(EMBED, BF16), like(EMBED, BF16), like(EMBED, F32), like(2 * EMBED, BF16),
         jax.ShapeDtypeStruct((blocks, 2 * GROUP, EMBED), F32), small(GROUP), small(GROUP)],
        [state] * 3 + [weight(EMBED, EMBED), sems], "wkv", before_wkv, bits, (att_w,),
    )(k, v, r, xp, vectors, begin, ends)

    if paired:
        mix = held(mix, (last_two,), "hold_mix")
    row_in = neighbour(last_two.reshape(micro, CHUNKS, EMBED)[:, -1], "tok", 1)
    edge_two = jnp.where(replace, 0.0, edge_back(last_two, row_in))
    diff_two = first_two - edge_two
    fixed = jnp.concatenate([edge_two + diff_two * vectors[7:8], edge_two + diff_two * vectors[8:9]], axis=1)
    mix_two = lax.dynamic_update_slice(mix_two, fixed.astype(BF16), (0, 0))

    kq, gate = call(
        hidden_kernel, blocks,
        [up(2 * EMBED)],
        [up(FF), up(EMBED)],
        [like(FF, BF16), like(EMBED, BF16)],
        [weight(EMBED, FF + EMBED), sems], "hidden", before_hidden, bits, (fkr,),
    )(mix_two)
    kq_other, mix_two_other, y_other, mix_other = [other_core(array) for array in (kq, mix_two, y, mix)]

    known = (mix_two_other, y_other, mix_other) if paired else ()
    mixed, dvf, dkf, cp = call(
        value_kernel, blocks,
        [up(FF), up(EMBED), up(EMBED), natural_up],
        [natural_up, up(EMBED), up(FF + EMBED), up(EMBED)],
        [jax.ShapeDtypeStruct(x4.shape, BF16), like(EMBED, BF16), like(FF + EMBED, BF16),
         like(EMBED, BF16)],
        [weight(FF, EMBED), pltpu.VMEM((ROWS, EMBED), F32), weight(ROWS, EMBED), sems],
        "value", known, bits, (fvalue, value_others),
    )(kq, gate, x1, c4)
    row_spec = full((micro, EMBED))
    shift_two, send_two = call(
        edge_kernel, 1,
        [SMEM_SPEC, pl.BlockSpec((GROUP, FF + EMBED), lambda i: (0, 0)), vec_spec], [edge_spec, row_spec],
        [small(GROUP), small(micro)],
        [weight(EMBED, FF + EMBED), sems], "edge", (), bits, (fkr,),
    )(flags, dkf, vectors)

    got_two = neighbour(send_two, "tok", -1)

    def reduced(made, plain, offload, name, moves=()):
        work = reduce_grad(bits, made, offload, name, moves) if paired else reduce_plain(*plain)
        next(work)
        return work

    def fused(kernel, grid, ins, in_specs, out_specs, out_shape, scratch, name, after, weights, lhs, takes, rhs,
              aliases=None):
        if not paired:
            lhs = takes = rhs = ()
        return call_main(
            kernel, grid, ins, in_specs, out_specs, out_shape, scratch, name, after, bits, weights, lhs, takes,
            rhs, aliases,
        )

    wide, narrow = FF // blocks, EMBED // blocks
    dvf_other = other_core(dvf)
    if paired:
        dkf = held(dkf, (dvf_other, shift_two), "hold_dkf")
    dkf_other = other_core(dkf)
    made = core_grad(bits, (kq, kq_other), (dvf, dvf_other), "grad_value", (shift_two, got_two)) if paired else (shift_two,)
    value_sum = reduced(made, ([(kq, None, 0, 1)], (dvf, None)), True, "grad_value")

    every_spec = full((tok_count, 2 * micro, EMBED))
    _, grads = fused(
        grad_only, blocks, (vectors,), [vec_spec], [], [], [], "grad_hidden", (made[0],), (),
        [(mix_two, mix_two_other, 0), (mix_two, mix_two_other, 8)],
        [(wide, 0, (0,) * blocks), (narrow, FF // narrow, (1,) * blocks)], (dkf, dkf_other),
    ) if paired else (None, made)
    hidden_sum = reduced(
        grads, ([(mix_two, None, 0, 4), (mix_two, None, 8, 1)], (dkf, None)), False, "grad_hidden",
        [(at // (blocks // 2), at % (blocks // 2) * (wide + narrow), wide, at * wide) for at in range(blocks)]
        + [(at // (blocks // 2), at % (blocks // 2) * (wide + narrow) + wide, narrow, FF + at * narrow)
           for at in range(blocks)],
    )
    made = grads
    (dx1, datt, dwkv, vsum_two, firsts, back_totals), grads = fused(
        middle_back_kernel, blocks,
        (dkf, x1, x1, edge_two, shift_two, got_two, cp, vectors, k, v, r, wkv, saved),
        [down(FF + EMBED), down(EMBED), before_spec, edge_spec,
         edge_spec, row_spec, down(EMBED), vec_spec] + [down(EMBED)] * 4 + [st_down],
        [down(EMBED), down(2 * EMBED), down(EMBED)] + [sum_spec, state_spec, every_spec],
        [like(EMBED, F32), like(2 * EMBED, BF16), like(EMBED, BF16), small(8),
         small(2 * GROUP), jax.ShapeDtypeStruct((tok_count, 2 * micro, EMBED), F32)],
        [state, pltpu.VMEM((2, ROWS, EMBED), F32), state, state, weight(EMBED, FF + EMBED),
         weight(EMBED, EMBED), pltpu.VMEM((ROWS, EMBED), F32), pltpu.VMEM((ROWS, EMBED), F32),
         pltpu.VMEM((4, GROUP, EMBED), F32), sems],
        "middle_back", (made[0],), (fkr, att_w), (), (), (),
    )
    every_back = lax.all_to_all(back_totals, "tok", 0, 0, tiled=True)
    made = advance(value_sum, firsts)
    made = advance(hidden_sum, made)
    datt_other = other_core(datt)
    right_down = pl.BlockSpec((ROWS, EMBED), lambda i: (blocks - 1 - i, 1))
    (dkv, vsum_wkv, shift_one, send_one), grads = fused(
        wkv_back_kernel, blocks,
        (flags, k, v, dwkv, datt, saved, vectors, every_back, firsts),
        [SMEM_SPEC] + [down(EMBED)] * 3 + [right_down, st_down, vec_spec, every_spec, state_spec],
        [down(2 * EMBED), sum_spec, edge_spec, row_spec],
        [like(2 * EMBED, BF16), small(8), small(GROUP), small(micro)],
        [pltpu.VMEM((ROWS, EMBED), F32)] * 2 + [state] * 2
        + [pltpu.VMEM((2, GROUP, EMBED), F32), weight(EMBED, 3 * EMBED), sems],
        "wkv_back", (made,), (att_w,),
        [(y, y_other, 0), (mix, mix_other, 16)], [(2 * EMBED // blocks, 0, (0, 0, 1, 1))], (datt, datt_other),
    )
    early_sum = reduced(grads, ([(y, None, 0, 1), (mix, None, 16, 1)], (datt, None)), False, "grad_early")
    dkv_other = other_core(dkv)

    got_one = neighbour(send_one, "tok", -1)
    made = advance(value_sum, dkv)
    value_part = advance(value_sum)
    made = advance(hidden_sum, made)

    half = blocks // 2

    def input_back(high, before, later_rows, started):
        def at(width, column=0):
            return pl.BlockSpec((ROWS, width), lambda i: (high - i, column))

        before_block = pl.BlockSpec((GROUP, EMBED), lambda i: (jnp.maximum((high - i) * STEPS - 1, 0), 0))
        natural = pl.BlockSpec((micro, CHUNKS, STEPS, EMBED), lambda i: (0, 0, high - i, 0))
        return fused(
            functools.partial(input_back_kernel, bool(started)), half,
            (dkv, datt, xp, xp, edge_one, later_rows, got_one, dx1, vectors, *started),
            [at(2 * EMBED), at(EMBED, 1), at(EMBED), before_block, edge_spec, edge_spec, row_spec, at(EMBED), vec_spec]
            + [ANY_SPEC, sum_spec][: len(started)],
            [natural, sum_spec, edge_spec],
            [jax.ShapeDtypeStruct(x4.shape, BF16), small(8), small(GROUP)],
            [state, weight(EMBED, 3 * EMBED), pltpu.VMEM((3, ROWS, EMBED), F32), weight(ROWS, EMBED),
             pltpu.VMEM((5, GROUP, EMBED), F32), sems],
            "input_back_low" if started else "input_back_high", before, (att_w,),
            () if started else [(mix, mix_other, 0), (mix, mix_other, 8)], [(EMBED, 0, (0, 1))], (dkv, dkv_other),
            {len(before) + 1 + len(att_w) + 9: 0} if started else None,
        )

    (token_high, vsum_high, later_half), grads = input_back(blocks - 1, (made,), shift_one, ())
    late_sum = reduced(grads, ([(mix, None, 0, 1), (mix, None, 8, 1)], (dkv, None)), False, "grad_late")
    made = advance(early_sum, vsum_high)
    made = advance(hidden_sum, made)
    hidden_got = advance(hidden_sum)
    (token_grad, vsum_one, _), _ = input_back(half - 1, (made, value_part), later_half, (token_high, vsum_high))

    made = advance(late_sum, vsum_one)
    made = advance(early_sum, made)
    made = advance(late_sum, made, hidden_got)
    columns = vec_m.shape[1]
    grad_vec = held(jnp.concatenate([vsum_one, vsum_two, vsum_wkv], axis=0), (made,), "hold_vec")
    pieces = jnp.moveaxis(grad_vec.reshape(grad_vec.shape[0], tok_count * rep_count, columns), 1, 0)
    vec_terms = lax.all_to_all(pieces, ("tok", "rep"), 0, 0, tiled=True)
    if not paired:
        advance(value_sum)
    sum_fvalue = advance(value_sum, made)
    made = advance(early_sum, made)
    sum_fkr = advance(hidden_sum, made)
    advance(early_sum)
    made = advance(late_sum, made)
    advance(late_sum)
    sum_early = advance(early_sum, made)
    sum_late = advance(late_sum)
    sums = jnp.sum(held(vec_terms, (made,), "hold_terms"), axis=0)
    sum_vec = jnp.concatenate([sums[0:2], sums[8:10], sums[2:5], sums[10:12], sums[16:18]], axis=0)
    sum_out = sum_early[:, :EMBED]
    sum_kvr = jnp.concatenate([sum_late, sum_early[:, EMBED:]], axis=1)

    base_rate = 2.5 / math.sqrt(EMBED)
    new_kvr = adam_step(w_kvr, m_kvr, v_kvr, sum_kvr, base_rate, 0.01)
    new_out = adam_step(w_out, m_out, v_out, sum_out, 4.0 * base_rate, 0.01)
    new_fkr = adam_step(f_kr, m_fkr, v_fkr, sum_fkr, base_rate, 0.01)
    new_fvalue = adam_step(f_value, m_fvalue, v_fvalue, sum_fvalue, 2.5 / math.sqrt(FF), 0.01)
    vec_master = lax.dynamic_slice_in_dim(vectors, flat_index * columns, columns, 1)
    vec_rates = jnp.array([0.6, 0.3, 0.6, 0.3, 0.3, 0.3, 0.3, 0.3, 0.3, 3.0, 0.5], F32)[:, None]
    new_vectors = adam_step(vec_master, vec_m, vec_v, sum_vec, vec_rates, 0.0)
    shape = tokens.shape
    return (
        (mixed.reshape(shape), token_grad.reshape(shape))
        + new_kvr + new_out + new_fkr + new_fvalue + new_vectors
    )


def solution(mesh):
    rows = P(("tok", "rep"), None)
    columns = P(None, ("tok", "rep"))
    token_spec = P(None, "rep", "tok", None)
    channel_spec = P(None, "rep", None, "tok")
    placed = (
        (token_spec, token_spec, channel_spec, channel_spec, P(None, "rep", None, None), P(None, "rep", None))
        + (rows,) * 4 + (P(),) + (rows,) * 8 + (columns,) * 2
    )
    return jax.shard_map(
        on_device,
        mesh=mesh,
        in_specs=placed,
        out_specs=(token_spec, token_spec) + (rows,) * 12 + (columns,) * 3,
        check_vma=False,
    )
```
